256 devices in a mesh: space: 32 (over y, x, core), rx: 8 (over z).
Axes of the slice: x: 4, y: 4, z: 8, core: 2. Of those that a mesh axis runs over, the one named last changes fastest.
Arguments:
- lambda_next: float32 [64, 3, 64, 32, 128], P('rx', None, 'space'), may hold values from -40 to 40
- class_ids: int32 [64, 32, 128], P('space'), may hold values from 0 to 15
- class_rate: float32 [16], replicated, may hold values from 0.2 to 4
- coil_x: int32 [64], P('rx'), may hold values from 0 to 62
- coil_y: int32 [64], P('rx'), may hold values from 0 to 30
- coil_z: int32 [64], P('rx'), may hold values from 0 to 127
- coil_amp: float32 [64], P('rx'), may hold values from -12 to 12
Outputs:
- adjoint: float32 [64, 3, 64, 32, 128], P('rx', None, 'space')
The draws below stay inside these ranges and needn't reach their ends.
All inputs are finite; a program needn't handle non-finite values.
Results may differ from the reference program's by a relative error of at most 0.0003.
Values sent between devices are 32-bit elements; how exact they have to be, the bound alone decides.
No kernel may reach another device: no remote copies, remote signals or barrier semaphores. Data moves between devices by JAX's collectives and lax.ppermute only.
A program may use at most 128 MiB of HBM per device.

```python
import math
import jax
import jax.numpy as jnp
from jax import lax

NREC = 64
CLASSES = 16
ITERS = 3
NY = 32
NZ = 128
NX = 64


def draw_lambda_next(key, part):
    key = jax.random.fold_in(key, 11)
    key_base, key_column, key_plane = jax.random.split(key, 3)
    shape = (NREC, 3, NX, NY, NZ)
    column_scale = jnp.exp(jax.random.uniform(key_column, (NREC, 1, 1, 1, 1), jnp.float32, 0.0, math.log(10.0)))
    plane_scale = jnp.exp(jax.random.uniform(key_plane, (1, 1, NX, 1, 1), jnp.float32, 0.0, math.log(10.0)))
    trend = 1.0 + 2.0 * jnp.arange(NX, dtype=jnp.float32).reshape(1, 1, NX, 1, 1) / NX
    base = jnp.clip(jax.random.normal(key_base, shape, jnp.float32), -4.0, 4.0)
    return base * column_scale * plane_scale * trend / 30.0


def plant(values, key, smallest, top_value):
    longest = values.shape.index(max(values.shape))
    spots = []
    for shift in (0, 1):
        where = [jax.random.randint(jax.random.fold_in(key, axis), (), 0, length) for axis, length in enumerate(values.shape)]
        where[longest] = (where[longest] + shift) % values.shape[longest]
        spots.append(tuple(where))
    return values.at[spots[0]].set(smallest).at[spots[1]].set(top_value)


def level_of(own_key, extent, pieces, low, largest):
    level = 1.0
    for axis_at, blocks in pieces:
        draws = jax.random.uniform(jax.random.fold_in(jax.random.fold_in(own_key, 6), axis_at), (blocks,), jnp.float32, low / len(pieces), largest / len(pieces))
        level = level * jnp.repeat(jnp.exp(draws), extent[axis_at] // blocks).reshape((-1,) + (1,) * (len(extent) - 1 - axis_at))
    return level


def bell_draw(rng, dims, scale, reach, cuts=(), kind=jnp.bfloat16):
    entries = scale * jax.random.normal(rng, dims, jnp.float32)
    if cuts:
        entries = entries * level_of(rng, dims, cuts, -0.22, 0.18)
    return jnp.clip(entries, -reach, reach).astype(kind)


def setup_inputs(seed: int = 0) -> dict:
    arg_keys = jax.random.split(jax.random.key(seed), 8)
    lambda_next = draw_lambda_next(jax.random.fold_in(arg_keys[7], 71), 0)
    class_ids = plant(jax.random.randint(arg_keys[1], (NX, NY, NZ), 0, CLASSES), jax.random.fold_in(arg_keys[1], 1), 0, CLASSES - 1).astype(jnp.int32)
    class_rate = jnp.clip(jnp.exp(jax.random.uniform(arg_keys[2], (CLASSES,), jnp.float32, math.log(0.2), math.log(4.0))), 0.2, 4.0)
    coil_x = plant(jax.random.randint(arg_keys[3], (NREC,), 0, NX - 1), jax.random.fold_in(arg_keys[3], 1), 0, (NX - 1) - 1).astype(jnp.int32)
    coil_y = plant(jax.random.randint(arg_keys[4], (NREC,), 0, NY - 1), jax.random.fold_in(arg_keys[4], 1), 0, (NY - 1) - 1).astype(jnp.int32)
    coil_z = plant(jax.random.randint(arg_keys[5], (NREC,), 0, NZ), jax.random.fold_in(arg_keys[5], 1), 0, NZ - 1).astype(jnp.int32)
    coil_amp = bell_draw(arg_keys[6], (NREC,), 3.0, 12.0, ((0, 8),), jnp.float32)
    return {"lambda_next": lambda_next, "class_ids": class_ids, "class_rate": class_rate, "coil_x": coil_x, "coil_y": coil_y, "coil_z": coil_z, "coil_amp": coil_amp}


def forward(values, along):
    result = values
    for spatial in range(3):
        position = result.ndim - 3 + spatial
        length = result.shape[position]
        if spatial == along:
            result = lax.slice_in_dim(result, 1, length, axis=position) - lax.slice_in_dim(result, 0, length - 1, axis=position)
        else:
            result = lax.slice_in_dim(result, 0, length - 1, axis=position)
    return result

def backward(values, along):
    result = values
    for spatial in range(3):
        position = result.ndim - 3 + spatial
        length = result.shape[position]
        if spatial == along:
            result = lax.slice_in_dim(result, 0, length - 1, axis=position) - lax.slice_in_dim(result, 1, length, axis=position)
        else:
            result = lax.slice_in_dim(result, 1, length, axis=position)
    return result

def curl_curl(padded):
    edge_x = padded[..., 0, :, :, :]
    edge_y = padded[..., 1, :, :, :]
    edge_z = padded[..., 2, :, :, :]
    curl_x = forward(edge_z, 1) - forward(edge_y, 2)
    curl_y = forward(edge_x, 2) - forward(edge_z, 0)
    curl_z = forward(edge_y, 0) - forward(edge_x, 1)
    result_x = backward(curl_y, 2) - backward(curl_z, 1)
    result_y = backward(curl_z, 0) - backward(curl_x, 2)
    result_z = backward(curl_x, 1) - backward(curl_y, 0)
    return jnp.stack([result_x, result_y, result_z], axis=-4)

def inner_products(left, right):
    left_flat = left.reshape(left.shape[0], -1)
    right_flat = right.reshape(right.shape[0], -1)
    return lax.dot_general(left_flat.astype(jnp.float32), right_flat.astype(jnp.float32), (((1,), (1,)), ((), ())), precision=lax.Precision.HIGHEST, preferred_element_type=jnp.float32)

def combine(block, weights):
    flat = block.reshape(block.shape[0], -1)
    mixed = lax.dot_general(weights.astype(jnp.float32), flat.astype(jnp.float32), (((0,), (0,)), ((), ())), precision=lax.Precision.HIGHEST, preferred_element_type=jnp.float32)
    return mixed.reshape(block.shape)

def solve_spd(matrix, right):
    symmetric = 0.5 * (matrix + matrix.T)
    factor = jnp.linalg.cholesky(symmetric)
    return jax.scipy.linalg.cho_solve((factor, True), right)

def lookup(class_ids, class_rate):
    levels = jnp.arange(class_rate.shape[0], dtype=jnp.int32)
    hits = (class_ids[..., None] == levels).astype(jnp.float32)
    return jnp.sum(hits * class_rate, axis=-1)

def reference(lambda_next, class_ids, class_rate, coil_x, coil_y, coil_z, coil_amp):
    mass_rate = lookup(class_ids, class_rate)
    receivers = jnp.arange(NREC, dtype=jnp.int32)
    first = jnp.zeros((NREC,), jnp.int32)
    second = first + 1
    source = jnp.zeros_like(lambda_next)
    source = source.at[receivers, first, coil_x, coil_y, coil_z].add(coil_amp)
    source = source.at[receivers, second, coil_x + 1, coil_y, coil_z].add(coil_amp)
    source = source.at[receivers, first, coil_x, coil_y + 1, coil_z].add(-coil_amp)
    source = source.at[receivers, second, coil_x, coil_y, coil_z].add(-coil_amp)
    right = mass_rate * lambda_next + source

    def operate(fields):
        padded = jnp.pad(fields, ((0, 0), (1, 1), (1, 1), (1, 1)))
        return mass_rate * fields + curl_curl(padded)
    solution = jnp.zeros_like(right)
    residual = right
    direction = right
    squares = inner_products(residual, residual)
    for iteration in range(ITERS):
        image = lax.map(operate, direction)
        curvature = inner_products(direction, image)
        weights = solve_spd(curvature, squares)
        solution = solution + combine(direction, weights)
        residual = residual - combine(image, weights)
        if iteration + 1 < ITERS:
            squares_next = inner_products(residual, residual)
            ratios = solve_spd(squares, squares_next)
            direction = residual + combine(direction, ratios)
            squares = squares_next
    return solution
```

```python
import jax
import jax.numpy as jnp
from jax import lax
from jax.sharding import PartitionSpec as P

ITERS = 3
SHIFT = 6.0


def extended(x, sides, width):
    for axis, dim in sides:
        size, length = (lax.axis_size(axis), x.shape[dim])
        up = [(i, (i + 1) % size) for i in range(size - 1)]
        down = [(j, i) for i, j in up]
        last = lax.slice_in_dim(x, length - width, length, axis=dim)
        leading = lax.slice_in_dim(x, 0, width, axis=dim)
        before = lax.ppermute(last, axis, up)
        after = lax.ppermute(leading, axis, down)
        x = jnp.concatenate([before, x, after], axis=dim)
    return x


def forward(values, along):
    result = values
    for spatial in range(3):
        position = result.ndim - 3 + spatial
        length = result.shape[position]
        if spatial == along:
            result = lax.slice_in_dim(result, 1, length, axis=position) - lax.slice_in_dim(
                result, 0, length - 1, axis=position
            )
        else:
            result = lax.slice_in_dim(result, 0, length - 1, axis=position)
    return result


def backward(values, along):
    result = values
    for spatial in range(3):
        position = result.ndim - 3 + spatial
        length = result.shape[position]
        if spatial == along:
            result = lax.slice_in_dim(result, 0, length - 1, axis=position) - lax.slice_in_dim(
                result, 1, length, axis=position
            )
        else:
            result = lax.slice_in_dim(result, 1, length, axis=position)
    return result


def curl_curl(padded):
    edge_x = padded[..., 0, :, :, :]
    edge_y = padded[..., 1, :, :, :]
    edge_z = padded[..., 2, :, :, :]
    curl_x = forward(edge_z, 1) - forward(edge_y, 2)
    curl_y = forward(edge_x, 2) - forward(edge_z, 0)
    curl_z = forward(edge_y, 0) - forward(edge_x, 1)
    result_x = backward(curl_y, 2) - backward(curl_z, 1)
    result_y = backward(curl_z, 0) - backward(curl_x, 2)
    result_z = backward(curl_x, 1) - backward(curl_y, 0)
    return jnp.stack([result_x, result_y, result_z], axis=-4)


def inner_products(left, right):
    left_flat = left.reshape(left.shape[0], -1)
    right_flat = right.reshape(right.shape[0], -1)
    return lax.dot_general(
        left_flat,
        right_flat,
        (((1,), (1,)), ((), ())),
        precision=lax.Precision.HIGHEST,
        preferred_element_type=jnp.float32,
    )


def combine(block, weights):
    flat = block.reshape(block.shape[0], -1)
    mixed = lax.dot_general(
        weights,
        flat,
        (((0,), (0,)), ((), ())),
        precision=lax.Precision.HIGHEST,
        preferred_element_type=jnp.float32,
    )
    return mixed


def reduce_bricks(parts):
    space, rx = (lax.axis_size("space"), lax.axis_size("rx"))
    rows = parts.shape[0]
    pieces = parts.reshape(space, rows // space, parts.shape[1])
    pieces = lax.all_to_all(pieces, "space", split_axis=0, concat_axis=0, tiled=True)
    own = jnp.sum(pieces, axis=0)
    pieces = jnp.broadcast_to(own[None], (rx, *own.shape))
    pieces = lax.all_to_all(pieces, "rx", split_axis=0, concat_axis=0, tiled=True)
    own = jnp.sum(pieces, axis=0)
    pieces = jnp.broadcast_to(own[None], (space, *own.shape))
    pieces = lax.all_to_all(pieces, "space", split_axis=0, concat_axis=0, tiled=True)
    return pieces.reshape(rows, parts.shape[1])


def lookup(class_ids, class_rate):
    levels = jnp.arange(class_rate.shape[0], dtype=jnp.int32)
    hits = (class_ids[..., None] == levels).astype(jnp.float32)
    return jnp.sum(hits * class_rate, axis=-1)


def matches(positions, coords):
    return (positions[None, :] == coords[:, None]).astype(jnp.float32)


def apply_bricks(fields, mass_rate):
    padded = extended(fields, (("space", 2), ("rx", 3)), 1)
    padded = jnp.pad(padded, ((0, 0), (0, 0), (0, 0), (0, 0), (1, 1)))
    return mass_rate * fields + curl_curl(padded)


def body(lambda_next, class_ids, class_rate, coil_x, coil_y, coil_z, coil_amp):
    width_x = lambda_next.shape[2]
    width_y = lambda_next.shape[3]
    width_z = lambda_next.shape[4]
    mass_rate = lookup(class_ids, class_rate)
    cells_x = lax.axis_index("space") * width_x + jnp.arange(width_x, dtype=jnp.int32)
    cells_y = jnp.arange(width_y, dtype=jnp.int32)
    cells_z = jnp.arange(width_z, dtype=jnp.int32)
    near_x = matches(cells_x, coil_x)
    far_x = matches(cells_x, coil_x + 1)
    near_y = matches(cells_y, coil_y)
    far_y = matches(cells_y, coil_y + 1)
    plane_z = matches(cells_z, coil_z)
    loop_x = near_x[:, :, None] * (near_y - far_y)[:, None, :]
    loop_y = (far_x - near_x)[:, :, None] * near_y[:, None, :]
    scaled_z = coil_amp[:, None] * plane_z
    source_x = loop_x[:, :, :, None] * scaled_z[:, None, None, :]
    source_y = loop_y[:, :, :, None] * scaled_z[:, None, None, :]
    source = jnp.stack([source_x, source_y, jnp.zeros_like(source_x)], axis=1)
    right = mass_rate * lambda_next + source
    pieces = lax.axis_size("rx")
    residual = lax.all_to_all(right, "rx", split_axis=3, concat_axis=0, tiled=True)
    slab_y = width_y // pieces
    mass_cells = lax.dynamic_slice_in_dim(mass_rate, lax.axis_index("rx") * slab_y, slab_y, 1)
    shifted = mass_cells - SHIFT
    basis = [residual]
    for _ in range(ITERS):
        basis.append(apply_bricks(basis[-1], shifted))
    moments = jnp.concatenate([inner_products(basis[(k + 1) // 2], basis[k // 2]) for k in range(2 * ITERS)], axis=0)
    moments = reduce_bricks(moments)
    n = residual.shape[0]
    moments = [moments[k * n : (k + 1) * n] for k in range(2 * ITERS)]
    moments = [0.5 * (m + m.T) for m in moments]
    gram = jnp.concatenate(
        [
            jnp.concatenate([moments[i + j + 1] + SHIFT * moments[i + j] for j in range(ITERS)], axis=1)
            for i in range(ITERS)
        ],
        axis=0,
    )
    factor = jnp.linalg.cholesky(gram)
    weights = jax.scipy.linalg.cho_solve((factor, True), jnp.concatenate(moments[:ITERS], axis=0))
    solution = combine(jnp.concatenate(basis[:ITERS], axis=0), weights)
    solution = solution.reshape(residual.shape)
    return lax.all_to_all(solution, "rx", split_axis=0, concat_axis=3, tiled=True)


def solution(mesh):
    in_specs = (
        P("rx", None, "space", None, None),
        P("space", None, None),
        P(),
        P("rx"),
        P("rx"),
        P("rx"),
        P("rx"),
    )
    out_specs = P("rx", None, "space", None, None)
    return jax.shard_map(body, mesh=mesh, in_specs=in_specs, out_specs=out_specs, check_vma=False)
```

```python
import functools

import jax
import jax.numpy as jnp
from jax import lax
from jax.experimental import pallas as pl
from jax.experimental.pallas import tpu as pltpu
from jax.sharding import PartitionSpec as P

SHIFT = 6.0
LANES = 128
HALF = 64
PLANE = 32
GHOST = 11
F32 = jnp.float32
BF16 = jnp.bfloat16
NT = (((1,), (1,)), ((), ()))
NN = (((1,), (0,)), ((), ()))


def lane_ids():
    lane = lax.broadcasted_iota(jnp.int32, (8, LANES), 1)
    return lane & 31, (lane >> 5) & 1, lane >> 6


def turn(a, shift):
    return pltpu.roll(a, shift, axis=a.ndim - 1)


def y_next(a):
    return jnp.where(lane_ids()[0] == 31, 0.0, turn(a, LANES - 1))


def y_prev(a):
    return jnp.where(lane_ids()[0] == 0, 0.0, turn(a, 1))


def z_both(a):
    half = turn(a, HALF)
    mixed = jnp.where(lane_ids()[2] == 0, half[:-1], half[1:])
    return jnp.concatenate([mixed, half[-1:]], axis=0), jnp.concatenate([half[:1], mixed], axis=0)


def x_next(a, beyond):
    return jnp.where(lane_ids()[1] == 0, turn(a, LANES - PLANE), beyond)


def x_prev(a, beyond):
    return jnp.where(lane_ids()[1] == 1, turn(a, PLANE), beyond)


def pack_up(a, b):
    return jnp.where(lane_ids()[1] == 1, a, turn(b, LANES - PLANE))


def pack_down(a, b):
    return jnp.where(lane_ids()[1] == 0, a, turn(b, PLANE))


def unpack(m, second, up):
    if second:
        return m
    return turn(m, LANES - PLANE) if up else turn(m, PLANE)


def slopes(v):
    return v[1] + y_next(v[0]) - v[0], v[2] + z_both(v[0])[0] - v[0]


def apply_tiles(v, shifted, beyond, before):
    g1, g2 = slopes(v)
    e1 = v[1] - x_next(v[1], beyond[0])
    e2 = v[2] - x_next(v[2], beyond[1])
    q2 = z_both(v[2])[1] - v[2]
    q1 = y_prev(v[1]) - v[1]
    v1_next, v1_prev = z_both(v[1])
    r0 = 2.0 * v[0] + v[1] + v[2] - g1 - g2 + y_prev(e1 - v[0]) + z_both(e2 - v[0])[1] - e1 - e2
    r1 = g1 - x_prev(g1, before[0]) + e1 + 2.0 * v[1] - v1_next - v1_prev - y_next(q2) + q2
    r2 = g2 - x_prev(g2, before[1]) + e2 + 2.0 * v[2] - y_next(v[2]) - y_prev(v[2]) - z_both(q1)[0] + q1
    return [shifted * v[0] + r0, shifted * v[1] + r1, shifted * v[2] + r2]


def halves(a):
    high = a.astype(BF16)
    return high, (a - high.astype(F32)).astype(BF16)


def enter_kernel(rate, coil_x, coil_y, coil_z, amp, field, ids, out, mass_out, flipped, padded, mass_pad):
    lane = lax.broadcasted_iota(jnp.int32, (64, LANES), 1)
    row = lax.broadcasted_iota(jnp.int32, (64, LANES), 0)
    classes = ids[...].reshape(64, LANES)
    mass = jnp.zeros((64, LANES), F32)
    for k in range(rate.shape[0]):
        mass = jnp.where(classes == k, rate[k], mass)
    left = lane < HALF
    flipped[...] = jnp.transpose(jnp.concatenate([mass, mass], axis=0))
    rows = jnp.where(left, flipped[pl.ds(0, 64, stride=2), :], flipped[pl.ds(1, 64, stride=2), :])
    mass_pad[0:8, :] = jnp.zeros((8, LANES), F32)
    mass_pad[8 * 65 :, :] = jnp.zeros((16, LANES), F32)
    for r in range(8):
        mass_pad[pl.ds(8 + r, 64, stride=8), :] = rows
    first = pl.multiple_of(lax.axis_index("rx") * 64, 64)
    mass_out[...] = mass_pad[pl.ds(first, 8 * GHOST), :].reshape(GHOST, 8, LANES) - SHIFT
    base = lax.axis_index("space") * 2

    def right(r, c):
        values = mass * field[r, c].reshape(64, LANES)
        if c == 2:
            return values
        near = coil_x[r] - base
        far = near + 1
        spot = jnp.where((near >= 0) & (near < 2), near * 32 + coil_y[r], -100)
        if c == 0:
            plus, minus = spot, spot + 1
        else:
            plus, minus = jnp.where((far >= 0) & (far < 2), far * 32 + coil_y[r], -100), spot
        strength = jnp.where(row == plus, amp[r], jnp.where(row == minus, -amp[r], 0.0))
        return values + jnp.where(lane == coil_z[r], strength, 0.0)

    for c in range(3):
        padded[0:8, :] = jnp.zeros((8, LANES), F32)
        padded[8 * 65 :, :] = jnp.zeros((16, LANES), F32)
        for r in range(4):
            flipped[...] = jnp.transpose(jnp.concatenate([right(r, c), right(r + 4, c)], axis=0))
            even = flipped[pl.ds(0, 64, stride=2), :]
            odd = flipped[pl.ds(1, 64, stride=2), :]
            padded[pl.ds(8 + r, 64, stride=8), :] = jnp.where(left, even, turn(odd, HALF))
            padded[pl.ds(12 + r, 64, stride=8), :] = jnp.where(left, turn(even, HALF), odd)
        for d in range(8):
            out[d, c] = padded[64 * d : 64 * d + 8 * GHOST, :].reshape(GHOST, 8, LANES)


def leave_kernel(tiles, out, gathered, flipped):
    left = lax.broadcasted_iota(jnp.int32, (64, LANES), 1) < HALF
    for c in range(3):
        for s in range(8):
            gathered[64 * s : 64 * s + 64, :] = tiles[s, c].reshape(64, LANES)
        for r in range(4):
            one = gathered[pl.ds(r, 64, stride=8), :]
            two = gathered[pl.ds(r + 4, 64, stride=8), :]
            flipped[pl.ds(0, 64, stride=2), :] = jnp.where(left, one, turn(two, HALF))
            flipped[pl.ds(1, 64, stride=2), :] = jnp.where(left, turn(one, HALF), two)
            back = jnp.transpose(flipped[...])
            out[r, c] = back[:64].reshape(2, PLANE, LANES)
            out[r + 4, c] = back[64:].reshape(2, PLANE, LANES)


def send_up(up, s, v, w, first, last):
    for c, (a, b) in enumerate(zip(slopes(v), slopes(w), strict=True)):
        up[s, c] = pack_up(a[first:last], b[first:last])


def send_down(down, s, v, w, first, last):
    for c in range(2):
        down[s, c] = pack_down(v[c + 1][first:last], w[c + 1][first:last])


def first_kernel(v0, up, down):
    def step(s, carry):
        v, w = ([v0[s + 4 * k, c] for c in range(3)] for k in range(2))
        send_up(up, s, v, w, 0, GHOST - 1)
        send_down(down, s, v, w, 0, GHOST - 1)
        return carry

    lax.fori_loop(0, 4, step, 0)


def inside(values, first_tile, last_tile):
    index = lax.axis_index("rx")
    rows = values.shape[0]
    low = jnp.where(index == 0, 0.0, 1.0)
    high = jnp.where(index == lax.axis_size("rx") - 1, 0.0, 1.0)
    pieces = [values]
    if first_tile:
        pieces = [values[:1] * low, values[1:]]
    if last_tile:
        pieces = [*pieces[:-1], pieces[-1][:-1], pieces[-1][-1:] * high]
    return jnp.concatenate(pieces, axis=0) if rows else values


def second_kernel(v0, mass, below, above, v1, up, down):
    def step(s, carry):
        fields = []
        for k in range(2):
            v = [v0[s + 4 * k, c] for c in range(3)]
            zero = jnp.zeros((1, 8, LANES), F32)
            beyond = [jnp.concatenate([unpack(above[s, c], k, False), zero], axis=0) for c in range(2)]
            before = [jnp.concatenate([unpack(below[s, c], k, True), zero], axis=0) for c in range(2)]
            result = apply_tiles(v, mass[...], beyond, before)
            result = [inside(r[: GHOST - 1], True, True) for r in result]
            for c in range(3):
                v1[s + 4 * k, c] = result[c]
            fields.append(result)
        send_up(up, s, *fields, 1, GHOST - 1)
        send_down(down, s, *fields, 0, GHOST - 1)
        return carry

    lax.fori_loop(0, 4, step, 0)


def third_kernel(v1, mass, below, above, v2, down):
    def step(s, carry):
        fields = []
        for k in range(2):
            v = [v1[s + 4 * k, c] for c in range(3)]
            zero = jnp.zeros((1, 8, LANES), F32)
            beyond = [unpack(above[s, c], k, False) for c in range(2)]
            before = [jnp.concatenate([zero, unpack(below[s, c], k, True)], axis=0) for c in range(2)]
            result = apply_tiles(v, mass[: GHOST - 1], beyond, before)
            result = [inside(r[1:], False, True) for r in result]
            for c in range(3):
                v2[s + 4 * k, c] = result[c]
            fields.append(result)
        send_down(down, s, *fields, 0, 8)
        return carry

    lax.fori_loop(0, 4, step, 0)


def columns(ref, c, first):
    return jnp.concatenate([ref[:, c, first + k].reshape(64, LANES) for k in range(2)], axis=1)


def moments_kernel(v0, v1, v2, out):
    total = jnp.zeros((192, 384), F32)
    for c in range(3):
        for k in range(0, 8, 2):
            stack = jnp.concatenate([columns(v0, c, k + 1), columns(v1, c, k + 1), columns(v2, c, k)], axis=0)
            high, low = halves(stack)
            total = total + lax.dot_general(
                high, jnp.concatenate([high, low], axis=0), NT, preferred_element_type=F32
            )
    main, cross = total[:, :192], total[:, 192:]

    def block(i, j):
        at = lambda m, p, q: m[64 * p : 64 * p + 64, 64 * q : 64 * q + 64]
        return at(main, i, j) + at(cross, i, j) + at(cross, j, i)

    out[0:64, :] = jnp.concatenate([block(0, 0), block(0, 1)], axis=1)
    out[64:128, :] = jnp.concatenate([block(1, 1), block(1, 2)], axis=1)
    out[128:192, :] = jnp.concatenate([block(2, 2), jnp.zeros((64, 64), F32)], axis=1)


def energy_kernel(v2, mass, above, moments, out, curl, scaled):
    y, x, parity = lane_ids()
    first_x = jnp.where((x == 0) & (lax.axis_index("space") == 0), 1.0, 0.0)
    first_y = jnp.where(y == 0, 1.0, 0.0)
    tile = lax.broadcasted_iota(jnp.int32, (8, 8, LANES), 0)
    first_z = jnp.where((tile == 0) & (parity == 0) & (lax.axis_index("rx") == 0), 1.0, 0.0)
    own = mass[1:9]
    faces = [first_y + first_z, first_x + first_z, first_x + first_y]

    def step(s, carry):
        for k in range(2):
            v = [v2[s + 4 * k, c] for c in range(3)]
            z1 = z_both(v[1])[0][:8]
            z0 = z_both(v[0])[0][:8]
            v = [a[:8] for a in v]
            x1 = x_next(v[1], unpack(above[s, 0], k, False))
            x2 = x_next(v[2], unpack(above[s, 1], k, False))
            curl[s + 4 * k, 0] = y_next(v[2]) - v[2] - z1 + v[1]
            curl[s + 4 * k, 1] = z0 - v[0] - x2 + v[2]
            curl[s + 4 * k, 2] = x1 - v[1] - y_next(v[0]) + v[0]
            for c in range(3):
                scaled[s + 4 * k, c] = v[c] * (own + faces[c])
        return carry

    lax.fori_loop(0, 4, step, 0)
    bends = jnp.zeros((64, 128), F32)
    mixed = jnp.zeros((128, 128), F32)
    for c in range(3):
        for k in range(0, 8, 2):
            high, low = halves(columns(curl, c, k))
            bends = bends + lax.dot_general(high, jnp.concatenate([high, low], axis=0), NT, preferred_element_type=F32)
            wide = jnp.concatenate(halves(columns(scaled, c, k)), axis=0)
            field = jnp.concatenate(halves(columns(v2, c, k)), axis=0)
            mixed = mixed + lax.dot_general(wide, field, NT, preferred_element_type=F32)
    last = bends[:, :64] + 2.0 * bends[:, 64:] + mixed[:64, :64] + mixed[:64, 64:] + mixed[64:, :64]
    out[0:128, :] = moments[0:128, :]
    out[128:192, :] = jnp.concatenate([moments[128:192, :64], last], axis=1)


def spread(a, lane):
    return jnp.broadcast_to(a[:, lane : lane + 1], (8, LANES))


def solve_tiles(tiles):
    sub = lax.broadcasted_iota(jnp.int32, (8, LANES), 0)
    origin = [list(pair) for pair in tiles]
    for p in range(24):
        side, lane0 = p // 16, 8 * (p % 16)
        sides = range(side, 2)
        rows = list(tiles[p])
        for k in range(8):
            lane = lane0 + k
            column = spread(rows[side], lane)
            pivot = jnp.broadcast_to(column[k : k + 1], (8, LANES))
            floor = jnp.broadcast_to(spread(origin[p][side], lane)[k : k + 1], (8, LANES)) * 2e-7
            inverse = jnp.where(pivot > floor, 1.0 / jnp.where(pivot > floor, pivot, 1.0), 0.0)
            for t in sides:
                scaled = jnp.broadcast_to(rows[t][k : k + 1], (8, LANES)) * inverse
                rows[t] = jnp.where(sub == k, scaled, rows[t] - column * scaled)
        tiles[p] = rows
        lines = [[jnp.broadcast_to(rows[t][k : k + 1], (8, LANES)) for k in range(8)] if t in sides else None for t in range(2)]
        for i in range(24):
            if i == p:
                continue
            factors = [spread(tiles[i][side], lane0 + k) for k in range(8)]
            new = list(tiles[i])
            for t in sides:
                one = factors[0] * lines[t][0]
                for k in range(1, 8):
                    one = one + factors[k] * lines[t][k]
                new[t] = new[t] - one
            tiles[i] = new
    return jnp.concatenate([pair[1] for pair in tiles], axis=0)


def finish_kernel(moments, v0, v1, v2, out):
    n = []
    for b in range(3):
        block = moments[64 * b : 64 * b + 64, :]
        other = jnp.transpose(jnp.concatenate([block, block], axis=0))
        n.append(0.5 * (block[:, :64] + other[:64, :64]))
        n.append(0.5 * (block[:, 64:] + other[64:, :64]))
    h = [n[m + 1] + SHIFT * n[m] for m in range(5)]
    tiles = []
    for i in range(3):
        lefts = jnp.concatenate([h[i], h[i + 1]], axis=1)
        rights = jnp.concatenate([h[i + 2], n[i]], axis=1)
        tiles += [[lefts[8 * j : 8 * j + 8], rights[8 * j : 8 * j + 8]] for j in range(8)]
    weights = jnp.transpose(solve_tiles(tiles))[64:]
    high, low = halves(weights)
    both = jnp.concatenate([high, low], axis=0)
    for c in range(3):
        for k in range(0, 8, 2):
            stack = jnp.concatenate([columns(v0, c, k + 1), columns(v1, c, k + 1), columns(v2, c, k)], axis=0)
            fine, rest = halves(stack)
            one = lax.dot_general(both, fine, NN, preferred_element_type=F32)
            two = lax.dot_general(high, rest, NN, preferred_element_type=F32)
            mixed = one[:64] + one[64:] + two
            for j in range(2):
                out[:, c, k + j] = mixed[:, LANES * j : LANES * j + LANES].reshape(8, 8, LANES)


def call(kernel, outs, scratch=(), smem=0, n_in=1, flops=0):
    single = not isinstance(outs, list)
    shapes = [outs] if single else outs
    vmem = pl.BlockSpec(memory_space=pltpu.VMEM)
    done = pl.pallas_call(
        kernel,
        out_shape=[jax.ShapeDtypeStruct(s, F32) for s in shapes],
        in_specs=[pl.BlockSpec(memory_space=pltpu.SMEM)] * smem + [vmem] * n_in,
        out_specs=[vmem] * len(shapes),
        scratch_shapes=[pltpu.VMEM(s, F32) for s in scratch],
        compiler_params=pltpu.CompilerParams(vmem_limit_bytes=48 * 1024 * 1024),
        cost_estimate=pl.CostEstimate(flops=flops, bytes_accessed=4 * 1024 * 1024, transcendentals=0),
    )
    return (lambda *a: done(*a)[0]) if single else done


def exchange(x, axis):
    return lax.all_to_all(x, axis, split_axis=0, concat_axis=0, tiled=True)


def reduce_bricks(parts):
    space, rx = (lax.axis_size("space"), lax.axis_size("rx"))
    rows = parts.shape[0]
    pieces = exchange(parts.reshape(space, rows // space, LANES), "space")
    own = jnp.sum(pieces, axis=0)
    pieces = exchange(jnp.broadcast_to(own[None], (rx, *own.shape)), "rx")
    own = jnp.sum(pieces, axis=0)
    pieces = exchange(jnp.broadcast_to(own[None], (space, *own.shape)), "space")
    return pieces.reshape(rows, LANES)


def body(lambda_next, class_ids, class_rate, coil_x, coil_y, coil_z, coil_amp):
    size = lax.axis_size("space")
    rise = [(i, i + 1) for i in range(size - 1)]
    fall = [(j, i) for i, j in rise]
    outgoing, mass = call(
        enter_kernel,
        [(8, 3, GHOST, 8, LANES), (GHOST, 8, LANES)],
        [(LANES, LANES), (67 * 8, LANES), (67 * 8, LANES)],
        smem=5,
        n_in=2,
    )(class_rate, coil_x, coil_y, coil_z, coil_amp, lambda_next, class_ids)
    v0 = exchange(outgoing, "rx")
    up, down = call(first_kernel, [(4, 2, 10, 8, LANES), (4, 2, 10, 8, LANES)])(v0)
    below = lax.ppermute(up, "space", rise)
    above = lax.ppermute(down, "space", fall)
    v1, up, down = call(second_kernel, [(8, 3, 10, 8, LANES), (4, 2, 9, 8, LANES), (4, 2, 10, 8, LANES)], n_in=4)(
        v0, mass, below, above
    )
    below = lax.ppermute(up, "space", rise)
    above = lax.ppermute(down, "space", fall)
    v2, down = call(third_kernel, [(8, 3, 9, 8, LANES), (4, 2, 8, 8, LANES)], n_in=4)(v1, mass, below, above)
    above = lax.ppermute(down, "space", fall)
    moments = call(moments_kernel, (192, LANES), n_in=3, flops=10**8)(v0, v1, v2)
    moments = call(energy_kernel, (192, LANES), [(8, 3, 8, 8, LANES)] * 2, n_in=4)(v2, mass, above, moments)
    moments = reduce_bricks(moments)
    mixed = call(finish_kernel, (8, 3, 8, 8, LANES), n_in=4)(moments, v0, v1, v2)
    mixed = exchange(mixed, "rx")
    return call(leave_kernel, (8, 3, 2, PLANE, LANES), [(512, LANES), (LANES, LANES)])(mixed)


def solution(mesh):
    in_specs = (
        P("rx", None, "space", None, None),
        P("space", None, None),
        P(),
        P("rx"),
        P("rx"),
        P("rx"),
        P("rx"),
    )
    out_specs = P("rx", None, "space", None, None)
    return jax.shard_map(body, mesh=mesh, in_specs=in_specs, out_specs=out_specs, check_vma=False)
```

```python
import jax
import jax.numpy as jnp
from jax import lax
from jax.experimental import pallas as pl
from jax.experimental.pallas import tpu as pltpu
from jax.sharding import PartitionSpec as P

SHIFT = 6.0
LANES = 128
HALF = 64
PLANE = 32
GHOST = 11
F32 = jnp.float32
BF16 = jnp.bfloat16
NT = (((1,), (1,)), ((), ()))
NN = (((1,), (0,)), ((), ()))


def lane_ids():
    lane = lax.broadcasted_iota(jnp.int32, (8, LANES), 1)
    return lane & 31, (lane >> 5) & 1, lane >> 6


def turn(a, shift):
    return pltpu.roll(a, shift, axis=a.ndim - 1)


def y_next(a):
    return jnp.where(lane_ids()[0] == 31, 0.0, turn(a, LANES - 1))


def y_prev(a):
    return jnp.where(lane_ids()[0] == 0, 0.0, turn(a, 1))


def z_both(a):
    half = turn(a, HALF)
    mixed = jnp.where(lane_ids()[2] == 0, half[:-1], half[1:])
    return jnp.concatenate([mixed, half[-1:]], axis=0), jnp.concatenate([half[:1], mixed], axis=0)


def x_next(a, beyond):
    return jnp.where(lane_ids()[1] == 0, turn(a, LANES - PLANE), beyond)


def x_prev(a, beyond):
    return jnp.where(lane_ids()[1] == 1, turn(a, PLANE), beyond)


def pack_up(a, b):
    return jnp.where(lane_ids()[1] == 1, a, turn(b, LANES - PLANE))


def pack_down(a, b):
    return jnp.where(lane_ids()[1] == 0, a, turn(b, PLANE))


def unpack(m, second, up):
    if second:
        return m
    return turn(m, LANES - PLANE) if up else turn(m, PLANE)


def slopes(v):
    return v[1] + y_next(v[0]) - v[0], v[2] + z_both(v[0])[0] - v[0]


def apply_tiles(v, shifted, beyond, before):
    g1, g2 = slopes(v)
    e1 = v[1] - x_next(v[1], beyond[0])
    e2 = v[2] - x_next(v[2], beyond[1])
    q2 = z_both(v[2])[1] - v[2]
    q1 = y_prev(v[1]) - v[1]
    v1_next, v1_prev = z_both(v[1])
    r0 = 2.0 * v[0] + v[1] + v[2] - g1 - g2 + y_prev(e1 - v[0]) + z_both(e2 - v[0])[1] - e1 - e2
    r1 = g1 - x_prev(g1, before[0]) + e1 + 2.0 * v[1] - v1_next - v1_prev - y_next(q2) + q2
    r2 = g2 - x_prev(g2, before[1]) + e2 + 2.0 * v[2] - y_next(v[2]) - y_prev(v[2]) - z_both(q1)[0] + q1
    return [shifted * v[0] + r0, shifted * v[1] + r1, shifted * v[2] + r2]


def halves(a):
    high = a.astype(BF16)
    return high, (a - high.astype(F32)).astype(BF16)


def thirds(a):
    high = a.astype(BF16)
    rest = a - high.astype(F32)
    middle = rest.astype(BF16)
    return high, middle, (rest - middle.astype(F32)).astype(BF16)


def multiply(a, b):
    ah, am, al = thirds(a)
    bh, bm, bl = thirds(b)
    left = jnp.concatenate([ah, ah, am, am, ah, al], axis=1)
    right = jnp.concatenate([bh, bm, bh, bm, bl, bh], axis=0)
    return lax.dot_general(left, right, NN, preferred_element_type=F32)


def enter_kernel(*refs):
    sources, (out, mass_out), rest = refs[:7], refs[7:9], refs[9:]
    targets, (flipped, padded, mass_pad, sems) = rest[:7], rest[7:]
    copies = [pltpu.make_async_copy(a, b, sems.at[i]) for i, (a, b) in enumerate(zip(sources, targets, strict=True))]
    for copy in copies:
        copy.start()
    for copy in copies:
        copy.wait()
    field, ids, rate, coil_x, coil_y, coil_z, amp = targets
    lane = lax.broadcasted_iota(jnp.int32, (64, LANES), 1)
    row = lax.broadcasted_iota(jnp.int32, (64, LANES), 0)
    classes = ids[...].reshape(64, LANES)
    mass = jnp.zeros((64, LANES), F32)
    for k in range(rate.shape[0]):
        mass = jnp.where(classes == k, rate[k], mass)
    left = lane < HALF
    flipped[...] = jnp.transpose(jnp.concatenate([mass, mass], axis=0))
    rows = jnp.where(left, flipped[pl.ds(0, 64, stride=2), :], flipped[pl.ds(1, 64, stride=2), :])
    mass_pad[0:8, :] = jnp.zeros((8, LANES), F32)
    mass_pad[8 * 65 :, :] = jnp.zeros((16, LANES), F32)
    for r in range(8):
        mass_pad[pl.ds(8 + r, 64, stride=8), :] = rows
    first = pl.multiple_of(lax.axis_index("rx") * 64, 64)
    mass_out[...] = mass_pad[pl.ds(first, 8 * GHOST), :].reshape(GHOST, 8, LANES) - SHIFT
    base = lax.axis_index("space") * 2

    def right(r, c):
        values = mass * field[r, c].reshape(64, LANES)
        if c == 2:
            return values
        near = coil_x[r] - base
        far = near + 1
        spot = jnp.where((near >= 0) & (near < 2), near * 32 + coil_y[r], -100)
        if c == 0:
            plus, minus = spot, spot + 1
        else:
            plus, minus = jnp.where((far >= 0) & (far < 2), far * 32 + coil_y[r], -100), spot
        strength = jnp.where(row == plus, amp[r], jnp.where(row == minus, -amp[r], 0.0))
        return values + jnp.where(lane == coil_z[r], strength, 0.0)

    for c in range(3):
        padded[0:8, :] = jnp.zeros((8, LANES), F32)
        padded[8 * 65 :, :] = jnp.zeros((16, LANES), F32)
        for r in range(4):
            flipped[...] = jnp.transpose(jnp.concatenate([right(r, c), right(r + 4, c)], axis=0))
            even = flipped[pl.ds(0, 64, stride=2), :]
            odd = flipped[pl.ds(1, 64, stride=2), :]
            padded[pl.ds(8 + r, 64, stride=8), :] = jnp.where(left, even, turn(odd, HALF))
            padded[pl.ds(12 + r, 64, stride=8), :] = jnp.where(left, turn(even, HALF), odd)
        for d in range(8):
            out[d, c] = padded[64 * d : 64 * d + 8 * GHOST, :].reshape(GHOST, 8, LANES)


def leave_kernel(tiles, out, gathered, flipped):
    left = lax.broadcasted_iota(jnp.int32, (64, LANES), 1) < HALF
    for c in range(3):
        for s in range(8):
            gathered[64 * s : 64 * s + 64, :] = tiles[s, c].reshape(64, LANES)
        for r in range(4):
            one = gathered[pl.ds(r, 64, stride=8), :]
            two = gathered[pl.ds(r + 4, 64, stride=8), :]
            flipped[pl.ds(0, 64, stride=2), :] = jnp.where(left, one, turn(two, HALF))
            flipped[pl.ds(1, 64, stride=2), :] = jnp.where(left, turn(one, HALF), two)
            back = jnp.transpose(flipped[...])
            out[r, c] = back[:64].reshape(2, PLANE, LANES)
            out[r + 4, c] = back[64:].reshape(2, PLANE, LANES)


def is_even():
    return lax.axis_index("space") % 2 == 0


def send(inner, outer, s, v, w, last):
    even = is_even()
    rises = [pack_up(a[:last], b[:last]) for a, b in zip(slopes(v), slopes(w), strict=True)]
    for c in range(2):
        falls = pack_down(v[c + 1][:last], w[c + 1][:last])
        inner[s, c] = jnp.where(even, rises[c], falls)
        outer[s, c] = jnp.where(even, falls, rises[c])


def receive(inner, outer, s, c):
    even = is_even()
    return jnp.where(even, outer[s, c], inner[s, c]), jnp.where(even, inner[s, c], outer[s, c])


def first_kernel(v0, inner, outer):
    def step(s, carry):
        v, w = ([v0[s + 4 * k, c] for c in range(3)] for k in range(2))
        send(inner, outer, s, v, w, GHOST - 1)
        return carry

    lax.fori_loop(0, 4, step, 0)


def inside(values, first_tile, last_tile):
    index = lax.axis_index("rx")
    rows = values.shape[0]
    low = jnp.where(index == 0, 0.0, 1.0)
    high = jnp.where(index == lax.axis_size("rx") - 1, 0.0, 1.0)
    pieces = [values]
    if first_tile:
        pieces = [values[:1] * low, values[1:]]
    if last_tile:
        pieces = [*pieces[:-1], pieces[-1][:-1], pieces[-1][-1:] * high]
    return jnp.concatenate(pieces, axis=0) if rows else values


def second_kernel(v0, mass, inner, outer, v1, next_inner, next_outer):
    def step(s, carry):
        fields = []
        below, above = zip(*(receive(inner, outer, s, c) for c in range(2)), strict=True)
        for k in range(2):
            v = [v0[s + 4 * k, c] for c in range(3)]
            zero = jnp.zeros((1, 8, LANES), F32)
            beyond = [jnp.concatenate([unpack(above[c], k, False), zero], axis=0) for c in range(2)]
            before = [jnp.concatenate([unpack(below[c], k, True), zero], axis=0) for c in range(2)]
            result = apply_tiles(v, mass[...], beyond, before)
            result = [inside(r[: GHOST - 1], True, True) for r in result]
            for c in range(3):
                v1[s + 4 * k, c] = result[c]
            fields.append(result)
        send(next_inner, next_outer, s, *fields, GHOST - 1)
        return carry

    lax.fori_loop(0, 4, step, 0)


def third_kernel(v1, mass, inner, outer, v2, down):
    def step(s, carry):
        fields = []
        below, above = zip(*(receive(inner, outer, s, c) for c in range(2)), strict=True)
        for k in range(2):
            v = [v1[s + 4 * k, c] for c in range(3)]
            beyond = [unpack(above[c], k, False) for c in range(2)]
            before = [unpack(below[c], k, True) for c in range(2)]
            result = apply_tiles(v, mass[: GHOST - 1], beyond, before)
            result = [inside(r[1:], False, True) for r in result]
            for c in range(3):
                v2[s + 4 * k, c] = result[c]
            fields.append(result)
        for c in range(2):
            down[s, c] = pack_down(fields[0][c + 1][:8], fields[1][c + 1][:8])
        return carry

    lax.fori_loop(0, 4, step, 0)


def columns(ref, c, first):
    return jnp.concatenate([ref[:, c, first + k].reshape(64, LANES) for k in range(2)], axis=1)


def moments_kernel(v0, v1, v2, out):
    total = jnp.zeros((192, 576), F32)
    middles = jnp.zeros((192, 192), F32)
    for c in range(3):
        for k in range(0, 8, 2):
            stack = jnp.concatenate([columns(v0, c, k + 1), columns(v1, c, k + 1), columns(v2, c, k)], axis=0)
            parts = thirds(stack)
            total = total + lax.dot_general(
                parts[0], jnp.concatenate(parts, axis=0), NT, preferred_element_type=F32
            )
            middles = middles + lax.dot_general(parts[1], parts[1], NT, preferred_element_type=F32)
    main, cross = total[:, :192] + middles, total[:, 192:384] + total[:, 384:]

    def block(i, j):
        at = lambda m, p, q: m[64 * p : 64 * p + 64, 64 * q : 64 * q + 64]
        return at(main, i, j) + at(cross, i, j) + at(cross, j, i)

    out[0:64, :] = jnp.concatenate([block(0, 0), block(0, 1)], axis=1)
    out[64:128, :] = jnp.concatenate([block(1, 1), block(1, 2)], axis=1)
    out[128:192, :] = jnp.concatenate([block(2, 2), jnp.zeros((64, 64), F32)], axis=1)


def energy_kernel(v2, mass, above, moments, out, curl, scaled):
    y, x, parity = lane_ids()
    first_x = jnp.where((x == 0) & (lax.axis_index("space") == 0), 1.0, 0.0)
    first_y = jnp.where(y == 0, 1.0, 0.0)
    tile = lax.broadcasted_iota(jnp.int32, (8, 8, LANES), 0)
    first_z = jnp.where((tile == 0) & (parity == 0) & (lax.axis_index("rx") == 0), 1.0, 0.0)
    own = mass[1:9]
    faces = [first_y + first_z, first_x + first_z, first_x + first_y]

    def step(s, carry):
        for k in range(2):
            v = [v2[s + 4 * k, c] for c in range(3)]
            z1 = z_both(v[1])[0][:8]
            z0 = z_both(v[0])[0][:8]
            v = [a[:8] for a in v]
            x1 = x_next(v[1], unpack(above[s, 0], k, False))
            x2 = x_next(v[2], unpack(above[s, 1], k, False))
            curl[s + 4 * k, 0] = y_next(v[2]) - v[2] - z1 + v[1]
            curl[s + 4 * k, 1] = z0 - v[0] - x2 + v[2]
            curl[s + 4 * k, 2] = x1 - v[1] - y_next(v[0]) + v[0]
            for c in range(3):
                scaled[s + 4 * k, c] = v[c] * (own + faces[c])
        return carry

    lax.fori_loop(0, 4, step, 0)
    bends = jnp.zeros((128, 192), F32)
    mixed = jnp.zeros((192, 192), F32)
    for c in range(3):
        for k in range(0, 8, 2):
            parts = jnp.concatenate(thirds(columns(curl, c, k)), axis=0)
            bends = bends + lax.dot_general(parts[:128], parts, NT, preferred_element_type=F32)
            wide = jnp.concatenate(thirds(columns(scaled, c, k)), axis=0)
            field = jnp.concatenate(thirds(columns(v2, c, k)), axis=0)
            mixed = mixed + lax.dot_general(wide, field, NT, preferred_element_type=F32)
    last = bends[:64, :64] + 2.0 * (bends[:64, 64:128] + bends[:64, 128:]) + bends[64:, 64:128]
    for i, j in ((0, 0), (0, 1), (1, 0), (1, 1), (0, 2), (2, 0)):
        last = last + mixed[64 * i : 64 * i + 64, 64 * j : 64 * j + 64]
    out[0:128, :] = moments[0:128, :]
    out[128:192, :] = jnp.concatenate([moments[128:192, :64], last], axis=1)


def spread(a, lane):
    return jnp.broadcast_to(a[:, lane : lane + 1], (8, LANES))


def line(a, k):
    return jnp.broadcast_to(a[k : k + 1], (8, LANES))


def invert(matrix):
    unit = lax.broadcasted_iota(jnp.int32, (64, 64), 0) == lax.broadcasted_iota(jnp.int32, (64, 64), 1)
    both = jnp.concatenate([matrix, jnp.where(unit, 1.0, 0.0)], axis=1)
    tiles = [both[8 * i : 8 * i + 8] for i in range(8)]
    origin = list(tiles)
    sub = lax.broadcasted_iota(jnp.int32, (8, LANES), 0)
    lane = lax.broadcasted_iota(jnp.int32, (8, LANES), 1)
    zero = jnp.zeros((8, LANES), F32)
    for p in range(8):
        rows, first = tiles[p], 8 * p
        cols = [spread(rows, first + k) for k in range(8)]
        for k in range(8):
            floor = line(spread(origin[p], first + k), k) * 2e-7
            pivot = line(cols[k], k)
            sound = pivot > floor
            inverse = jnp.where(sound, 1.0 / jnp.where(sound, pivot, 1.0), 0.0)
            own, hit = cols[k], sub == k
            for j in range(k + 1, 8):
                scaled = line(cols[j], k) * inverse
                cols[j] = jnp.where(hit, scaled, cols[j] - own * scaled)
            scaled = line(rows, k) * inverse
            rows = jnp.where(hit, scaled, rows - own * scaled)
        tiles[p] = rows
        inside_panel = (lane >= first) & (lane < first + 8)
        apart = [zero if i in (p, p + 1) else jnp.where(inside_panel, tiles[i], 0.0) for i in range(8)]
        placed = [rows if i == p else zero for i in range(8)]
        change = multiply(jnp.concatenate(apart, axis=0)[:, :64], jnp.concatenate(placed, axis=0))
        for i in range(8):
            if i == p + 1:
                f = [spread(tiles[i], first + k) * line(rows, k) for k in range(8)]
                tiles[i] = tiles[i] - (((f[0] + f[1]) + (f[2] + f[3])) + ((f[4] + f[5]) + (f[6] + f[7])))
            elif i != p:
                tiles[i] = tiles[i] - change[8 * i : 8 * i + 8]
    return jnp.concatenate(tiles, axis=0)[:, 64:]


def solve_blocks(n, h):
    first = multiply(invert(h[0]), jnp.concatenate([h[1], h[2], n[0]], axis=1))
    change = multiply(jnp.concatenate([h[1], h[2]], axis=0), first)
    second = jnp.concatenate([h[2], h[3], n[1]], axis=1) - change[:64]
    third = jnp.concatenate([h[3], h[4], n[2]], axis=1) - change[64:]
    below = third[:, :64]
    second = multiply(invert(second[:, :64]), second[:, 64:])
    third = third[:, 64:] - multiply(below, second)
    y2 = multiply(invert(third[:, :64]), third[:, 64:])
    y1 = second[:, 64:] - multiply(second[:, :64], y2)
    y0 = first[:, 128:] - multiply(first[:, :64], y1) - multiply(first[:, 64:128], y2)
    return jnp.concatenate([y0, y1, y2], axis=0)


def finish_kernel(moments, v0, v1, v2, out):
    n = []
    for b in range(3):
        block = moments[64 * b : 64 * b + 64, :]
        other = jnp.transpose(jnp.concatenate([block, block], axis=0))
        n.append(0.5 * (block[:, :64] + other[:64, :64]))
        n.append(0.5 * (block[:, 64:] + other[64:, :64]))
    h = [n[m + 1] + SHIFT * n[m] for m in range(5)]
    solved = solve_blocks(n, h)
    weights = jnp.transpose(jnp.concatenate([solved, solved], axis=1))[64:]
    high, low = halves(weights)
    both = jnp.concatenate([high, low], axis=0)
    for c in range(3):
        for k in range(0, 8, 2):
            stack = jnp.concatenate([columns(v0, c, k + 1), columns(v1, c, k + 1), columns(v2, c, k)], axis=0)
            fine, rest = halves(stack)
            one = lax.dot_general(both, fine, NN, preferred_element_type=F32)
            two = lax.dot_general(high, rest, NN, preferred_element_type=F32)
            mixed = one[:64] + one[64:] + two
            for j in range(2):
                out[:, c, k + j] = mixed[:, LANES * j : LANES * j + LANES].reshape(8, 8, LANES)


def call(kernel, outs, scratch=(), n_in=1, flops=0, where=pltpu.VMEM):
    single = not isinstance(outs, list)
    shapes = [outs] if single else outs
    vmem = pl.BlockSpec(memory_space=pltpu.VMEM)
    scratch = [pltpu.VMEM(a, F32) if isinstance(a, tuple) else a for a in scratch]
    done = pl.pallas_call(
        kernel,
        out_shape=[jax.ShapeDtypeStruct(s, F32) for s in shapes],
        in_specs=[pl.BlockSpec(memory_space=where)] * n_in,
        out_specs=[vmem] * len(shapes),
        scratch_shapes=scratch,
        compiler_params=pltpu.CompilerParams(vmem_limit_bytes=48 * 1024 * 1024),
        cost_estimate=pl.CostEstimate(flops=flops, bytes_accessed=4 * 1024 * 1024, transcendentals=0),
    )
    return (lambda *a: done(*a)[0]) if single else done


def exchange(x, axis):
    return lax.all_to_all(x, axis, split_axis=0, concat_axis=0, tiled=True)


def reduce_bricks(parts):
    space, rx = (lax.axis_size("space"), lax.axis_size("rx"))
    rows = parts.shape[0]
    pieces = exchange(parts.reshape(space, rows // space, LANES), "space")
    own = jnp.sum(pieces, axis=0)
    pieces = exchange(jnp.broadcast_to(own[None], (rx, *own.shape)), "rx")
    own = jnp.sum(pieces, axis=0)
    pieces = exchange(jnp.broadcast_to(own[None], (space, *own.shape)), "space")
    return pieces.reshape(rows, LANES)


def body(lambda_next, class_ids, class_rate, coil_x, coil_y, coil_z, coil_amp):
    size = lax.axis_size("space")
    chips = [(i, i ^ 1) for i in range(size)]
    fall = [(i + 1, i) for i in range(size - 1)]
    beside = [pair for i in range(1, size - 1, 2) for pair in ((i, i + 1), (i + 1, i))]
    arrays = (lambda_next, class_ids, class_rate, coil_x, coil_y, coil_z, coil_amp)
    spaces = [pltpu.VMEM] * 2 + [pltpu.SMEM] * 5
    outgoing, mass = call(
        enter_kernel,
        [(8, 3, GHOST, 8, LANES), (GHOST, 8, LANES)],
        [space(a.shape, a.dtype) for space, a in zip(spaces, arrays, strict=True)]
        + [(LANES, LANES), (67 * 8, LANES), (67 * 8, LANES), pltpu.SemaphoreType.DMA((7,))],
        n_in=7,
        where=pl.ANY,
    )(*arrays)
    v0 = exchange(outgoing, "rx")
    message = (4, 2, 10, 8, LANES)
    inner, outer = call(first_kernel, [message] * 2)(v0)
    outer = lax.ppermute(outer, "space", beside)
    inner = lax.ppermute(inner, "space", chips)
    v1, inner, outer = call(second_kernel, [(8, 3, 10, 8, LANES), message, message], n_in=4)(v0, mass, inner, outer)
    outer = lax.ppermute(outer, "space", beside)
    inner = lax.ppermute(inner, "space", chips)
    v2, down = call(third_kernel, [(8, 3, 9, 8, LANES), (4, 2, 8, 8, LANES)], n_in=4)(v1, mass, inner, outer)
    above = lax.ppermute(down, "space", fall)
    moments = call(moments_kernel, (192, LANES), n_in=3, flops=10**8)(v0, v1, v2)
    moments = call(energy_kernel, (192, LANES), [(8, 3, 8, 8, LANES)] * 2, n_in=4)(v2, mass, above, moments)
    moments = reduce_bricks(moments)
    mixed = call(finish_kernel, (8, 3, 8, 8, LANES), n_in=4)(moments, v0, v1, v2)
    mixed = exchange(mixed, "rx")
    return call(leave_kernel, (8, 3, 2, PLANE, LANES), [(512, LANES), (LANES, LANES)])(mixed)


def solution(mesh):
    in_specs = (
        P("rx", None, "space", None, None),
        P("space", None, None),
        P(),
        P("rx"),
        P("rx"),
        P("rx"),
        P("rx"),
    )
    out_specs = P("rx", None, "space", None, None)
    return jax.shard_map(body, mesh=mesh, in_specs=in_specs, out_specs=out_specs, check_vma=False)
```

```python
import functools

import jax
import jax.numpy as jnp
from jax import lax
from jax.experimental import pallas as pl
from jax.experimental.pallas import tpu as pltpu
from jax.sharding import PartitionSpec as P

SHIFT = 6.0
LANES = 128
HALF = 64
PLANE = 32
GHOST = 11
F32 = jnp.float32
BF16 = jnp.bfloat16
NT = (((1,), (1,)), ((), ()))
NN = (((1,), (0,)), ((), ()))


def lane_ids():
    lane = lax.broadcasted_iota(jnp.int32, (8, LANES), 1)
    return lane & 31, (lane >> 5) & 1, lane >> 6


def turn(a, shift):
    return pltpu.roll(a, shift, axis=a.ndim - 1)


def y_next(a):
    return jnp.where(lane_ids()[0] == 31, 0.0, turn(a, LANES - 1))


def y_prev(a):
    return jnp.where(lane_ids()[0] == 0, 0.0, turn(a, 1))


def z_both(a):
    half = turn(a, HALF)
    mixed = jnp.where(lane_ids()[2] == 0, half[:-1], half[1:])
    return jnp.concatenate([mixed, half[-1:]], axis=0), jnp.concatenate([half[:1], mixed], axis=0)


def x_next(a, beyond):
    return jnp.where(lane_ids()[1] == 0, turn(a, LANES - PLANE), beyond)


def x_prev(a, beyond):
    return jnp.where(lane_ids()[1] == 1, turn(a, PLANE), beyond)


def pack_up(a, b):
    return jnp.where(lane_ids()[1] == 1, a, turn(b, LANES - PLANE))


def pack_down(a, b):
    return jnp.where(lane_ids()[1] == 0, a, turn(b, PLANE))


def unpack(m, second, up):
    if not second:
        m = turn(m, LANES - PLANE) if up else turn(m, PLANE)
    return jnp.where(lane_ids()[1] == (0 if up else 1), m, 0.0)


def slopes(v):
    return v[1] + y_next(v[0]) - v[0], v[2] + z_both(v[0])[0] - v[0]


def apply_tiles(v, shifted):
    g1, g2 = slopes(v)
    e1 = v[1] - x_next(v[1], 0.0)
    e2 = v[2] - x_next(v[2], 0.0)
    q2 = z_both(v[2])[1] - v[2]
    q1 = y_prev(v[1]) - v[1]
    v1_next, v1_prev = z_both(v[1])
    r0 = 2.0 * v[0] + v[1] + v[2] - g1 - g2 + y_prev(e1 - v[0]) + z_both(e2 - v[0])[1] - e1 - e2
    r1 = g1 - x_prev(g1, 0.0) + e1 + 2.0 * v[1] - v1_next - v1_prev - y_next(q2) + q2
    r2 = g2 - x_prev(g2, 0.0) + e2 + 2.0 * v[2] - y_next(v[2]) - y_prev(v[2]) - z_both(q1)[0] + q1
    return [shifted * v[0] + r0, shifted * v[1] + r1, shifted * v[2] + r2]


def halves(a):
    high = a.astype(BF16)
    return high, (a - high.astype(F32)).astype(BF16)


def thirds(a):
    high = a.astype(BF16)
    rest = a - high.astype(F32)
    middle = rest.astype(BF16)
    return high, middle, (rest - middle.astype(F32)).astype(BF16)


def multiply(a, b):
    ah, am, al = thirds(a)
    bh, bm, bl = thirds(b)
    left = jnp.concatenate([ah, ah, am, am, ah, al], axis=1)
    right = jnp.concatenate([bh, bm, bh, bm, bl, bh], axis=0)
    return lax.dot_general(left, right, NN, preferred_element_type=F32)


def enter_kernel(*refs):
    sources, (out, mass_out), rest = refs[:7], refs[7:9], refs[9:]
    targets, (flipped, padded, mass_pad, sems) = rest[:7], rest[7:]
    copies = [pltpu.make_async_copy(a, b, sems.at[i]) for i, (a, b) in enumerate(zip(sources, targets, strict=True))]
    for copy in copies:
        copy.start()
    for copy in copies:
        copy.wait()
    field, ids, rate, coil_x, coil_y, coil_z, amp = targets
    lane = lax.broadcasted_iota(jnp.int32, (64, LANES), 1)
    row = lax.broadcasted_iota(jnp.int32, (64, LANES), 0)
    classes = ids[...].reshape(64, LANES)
    mass = jnp.zeros((64, LANES), F32)
    for k in range(rate.shape[0]):
        mass = jnp.where(classes == k, rate[k], mass)
    left = lane < HALF
    flipped[...] = jnp.transpose(jnp.concatenate([mass, mass], axis=0))
    rows = jnp.where(left, flipped[pl.ds(0, 64, stride=2), :], flipped[pl.ds(1, 64, stride=2), :])
    mass_pad[0:8, :] = jnp.zeros((8, LANES), F32)
    mass_pad[8 * 65 :, :] = jnp.zeros((16, LANES), F32)
    for r in range(8):
        mass_pad[pl.ds(8 + r, 64, stride=8), :] = rows
    first = pl.multiple_of(lax.axis_index("rx") * 64, 64)
    mass_out[...] = mass_pad[pl.ds(first, 8 * GHOST), :].reshape(GHOST, 8, LANES) - SHIFT
    base = lax.axis_index("space") * 2

    def right(r, c):
        values = mass * field[r, c].reshape(64, LANES)
        if c == 2:
            return values
        near = coil_x[r] - base
        far = near + 1
        spot = jnp.where((near >= 0) & (near < 2), near * 32 + coil_y[r], -100)
        if c == 0:
            plus, minus = spot, spot + 1
        else:
            plus, minus = jnp.where((far >= 0) & (far < 2), far * 32 + coil_y[r], -100), spot
        strength = jnp.where(row == plus, amp[r], jnp.where(row == minus, -amp[r], 0.0))
        return values + jnp.where(lane == coil_z[r], strength, 0.0)

    for c in range(3):
        padded[0:8, :] = jnp.zeros((8, LANES), F32)
        padded[8 * 65 :, :] = jnp.zeros((16, LANES), F32)
        for r in range(4):
            flipped[...] = jnp.transpose(jnp.concatenate([right(r, c), right(r + 4, c)], axis=0))
            even = flipped[pl.ds(0, 64, stride=2), :]
            odd = flipped[pl.ds(1, 64, stride=2), :]
            padded[pl.ds(8 + r, 64, stride=8), :] = jnp.where(left, even, turn(odd, HALF))
            padded[pl.ds(12 + r, 64, stride=8), :] = jnp.where(left, turn(even, HALF), odd)
        for d in range(8):
            out[d, c] = padded[64 * d : 64 * d + 8 * GHOST, :].reshape(GHOST, 8, LANES)


def leave_kernel(tiles, out, gathered, flipped):
    left = lax.broadcasted_iota(jnp.int32, (64, LANES), 1) < HALF
    for c in range(3):
        for s in range(8):
            gathered[64 * s : 64 * s + 64, :] = tiles[s, c].reshape(64, LANES)
        for r in range(4):
            one = gathered[pl.ds(r, 64, stride=8), :]
            two = gathered[pl.ds(r + 4, 64, stride=8), :]
            flipped[pl.ds(0, 64, stride=2), :] = jnp.where(left, one, turn(two, HALF))
            flipped[pl.ds(1, 64, stride=2), :] = jnp.where(left, turn(one, HALF), two)
            back = jnp.transpose(flipped[...])
            out[r, c] = back[:64].reshape(2, PLANE, LANES)
            out[r + 4, c] = back[64:].reshape(2, PLANE, LANES)


def is_even():
    return lax.axis_index("space") % 2 == 0


def send(message, to_above, s, v, w):
    last = GHOST - 1

    @pl.when(to_above)
    def _():
        for c, (a, b) in enumerate(zip(slopes(v), slopes(w), strict=True)):
            message[s, c] = pack_up(a[:last], b[:last])

    @pl.when(jnp.logical_not(to_above))
    def _():
        for c in range(2):
            message[s, c] = pack_down(v[c + 1][:last], w[c + 1][:last])


def message_kernel(outer, v, message):
    def step(s, carry):
        fields = [[v[s + 4 * k, c] for c in range(3)] for k in range(2)]
        send(message, is_even() != outer, s, *fields)
        return carry

    lax.fori_loop(0, 4, step, 0)


def receive(inner, outer, s, c):
    even = is_even()
    return jnp.where(even, outer[s, c], inner[s, c]), jnp.where(even, inner[s, c], outer[s, c])


def inside(values, first_tile, last_tile):
    index = lax.axis_index("rx")
    rows = values.shape[0]
    low = jnp.where(index == 0, 0.0, 1.0)
    high = jnp.where(index == lax.axis_size("rx") - 1, 0.0, 1.0)
    pieces = [values]
    if first_tile:
        pieces = [values[:1] * low, values[1:]]
    if last_tile:
        pieces = [*pieces[:-1], pieces[-1][:-1], pieces[-1][-1:] * high]
    return jnp.concatenate(pieces, axis=0) if rows else values


def base_kernel(first, v, mass, base, inner):
    def step(s, carry):
        fields = [[v[s + 4 * k, c] for c in range(3)] for k in range(2)]
        for k in range(2):
            result = apply_tiles(fields[k], mass[: v.shape[2]])
            for c in range(3):
                base[s + 4 * k, c] = result[c][first : first + base.shape[2]]
        send(inner, is_even(), s, *fields)
        return carry

    lax.fori_loop(0, 4, step, 0)


def completed(base, inner, outer, s, k, first):
    below, above = zip(*(receive(inner, outer, s, c) for c in range(2)), strict=True)
    beyond = [unpack(a, k, False) for a in above]
    before = [unpack(a, k, True) for a in below]
    changes = [
        beyond[0] + beyond[1] - y_prev(beyond[0]) - z_both(beyond[1])[1],
        -beyond[0] - before[0],
        -beyond[1] - before[1],
    ]
    return [inside(base[s + 4 * k, c] + changes[c][first:], first == 0, True) for c in range(3)]


def second_kernel(outer, base, inner, v1, next_outer):
    def step(s, carry):
        fields = [completed(base, inner, outer, s, k, 0) for k in range(2)]
        for k in range(2):
            for c in range(3):
                v1[s + 4 * k, c] = fields[k][c]
        send(next_outer, jnp.logical_not(is_even()), s, *fields)
        return carry

    lax.fori_loop(0, 4, step, 0)


def third_kernel(outer, base, inner, v2, down):
    def step(s, carry):
        fields = [completed(base, inner, outer, s, k, 1) for k in range(2)]
        for k in range(2):
            for c in range(3):
                v2[s + 4 * k, c] = fields[k][c]
        for c in range(2):
            down[s, c] = pack_down(fields[0][c + 1][:8], fields[1][c + 1][:8])
        return carry

    lax.fori_loop(0, 4, step, 0)


def columns(ref, c, first):
    return jnp.concatenate([ref[:, c, first + k].reshape(64, LANES) for k in range(2)], axis=1)


def bend(parts):
    return lax.dot_general(parts[:128], parts, NT, preferred_element_type=F32)


def fold(bends):
    return bends[:64, :64] + 2.0 * (bends[:64, 64:128] + bends[:64, 128:]) + bends[64:, 64:128]


def moments_kernel(v0, v1, v2, mass, out, curl, curl0, scaled):
    y, x, parity = lane_ids()
    first_x = jnp.where((x == 0) & (lax.axis_index("space") == 0), 1.0, 0.0)
    first_y = jnp.where(y == 0, 1.0, 0.0)
    tile = lax.broadcasted_iota(jnp.int32, (8, 8, LANES), 0)
    first_z = jnp.where((tile == 0) & (parity == 0) & (lax.axis_index("rx") == 0), 1.0, 0.0)
    own = mass[1:9]
    faces = [first_y + first_z, first_x + first_z, first_x + first_y]

    def step(s, carry):
        v = [v2[s, c] for c in range(3)]
        z1 = z_both(v[1])[0][:8]
        z0 = z_both(v[0])[0][:8]
        v = [a[:8] for a in v]
        curl0[s, 0] = y_next(v[2]) - v[2] - z1 + v[1]
        curl[s, 0] = z0 - v[0] - x_next(v[2], 0.0) + v[2]
        curl[s, 1] = x_next(v[1], 0.0) - v[1] - y_next(v[0]) + v[0]
        for c in range(3):
            scaled[s, c] = v[c] * (own + faces[c])
        return carry

    lax.fori_loop(0, 8, step, 0)
    bends = jnp.zeros((128, 192), F32)
    mixed = jnp.zeros((192, 192), F32)
    total = jnp.zeros((192, 576), F32)
    middles = jnp.zeros((192, 192), F32)
    for c in range(3):
        for k in range(0, 8, 2):
            stack = jnp.concatenate([columns(v0, c, k + 1), columns(v1, c, k + 1), columns(v2, c, k)], axis=0)
            parts = thirds(stack)
            total = total + lax.dot_general(
                parts[0], jnp.concatenate(parts, axis=0), NT, preferred_element_type=F32
            )
            middles = middles + lax.dot_general(parts[1], parts[1], NT, preferred_element_type=F32)
            wide = jnp.concatenate(thirds(columns(scaled, c, k)), axis=0)
            field = jnp.concatenate([a[128:] for a in parts], axis=0)
            mixed = mixed + lax.dot_general(wide, field, NT, preferred_element_type=F32)
            if c == 0:
                bends = bends + bend(jnp.concatenate(thirds(columns(curl0, c, k)), axis=0))
    main, cross = total[:, :192] + middles, total[:, 192:384] + total[:, 384:]
    last = fold(bends)
    for i, j in ((0, 0), (0, 1), (1, 0), (1, 1), (0, 2), (2, 0)):
        last = last + mixed[64 * i : 64 * i + 64, 64 * j : 64 * j + 64]

    def block(i, j):
        at = lambda m, p, q: m[64 * p : 64 * p + 64, 64 * q : 64 * q + 64]
        return at(main, i, j) + at(cross, i, j) + at(cross, j, i)

    out[0:64, :] = jnp.concatenate([block(0, 0), block(0, 1)], axis=1)
    out[64:128, :] = jnp.concatenate([block(1, 1), block(1, 2)], axis=1)
    out[128:192, :] = jnp.concatenate([block(2, 2), last], axis=1)


def energy_kernel(curl, above, moments, out):
    bends = jnp.zeros((128, 192), F32)
    for c in range(2):
        for k in range(0, 8, 2):
            rows = []
            for j in range(2):
                beyond = jnp.concatenate([unpack(above[:, 1 - c, k + j], half, False) for half in range(2)], axis=0)
                bent = curl[:, c, k + j] - beyond if c == 0 else curl[:, c, k + j] + beyond
                rows.append(bent.reshape(64, LANES))
            bends = bends + bend(jnp.concatenate(thirds(jnp.concatenate(rows, axis=1)), axis=0))
    out[0:128, :] = moments[0:128, :]
    out[128:192, :] = moments[128:192, :] + jnp.concatenate([jnp.zeros((64, 64), F32), fold(bends)], axis=1)


def spread(a, lane):
    return jnp.broadcast_to(a[:, lane : lane + 1], (8, LANES))


def line(a, k):
    return jnp.broadcast_to(a[k : k + 1], (8, LANES))


def invert(matrix):
    unit = lax.broadcasted_iota(jnp.int32, (64, 64), 0) == lax.broadcasted_iota(jnp.int32, (64, 64), 1)
    both = jnp.concatenate([matrix, jnp.where(unit, 1.0, 0.0)], axis=1)
    tiles = [both[8 * i : 8 * i + 8] for i in range(8)]
    origin = list(tiles)
    sub = lax.broadcasted_iota(jnp.int32, (8, LANES), 0)
    lane = lax.broadcasted_iota(jnp.int32, (8, LANES), 1)
    zero = jnp.zeros((8, LANES), F32)
    for p in range(8):
        rows, first = tiles[p], 8 * p
        cols = [spread(rows, first + k) for k in range(8)]
        for k in range(8):
            floor = line(spread(origin[p], first + k), k) * 2e-7
            pivot = line(cols[k], k)
            inverse = jnp.where(pivot > floor, 1.0 / pivot, 0.0)
            own, hit = cols[k], sub == k
            for j in range(k + 1, 8):
                scaled = line(cols[j], k) * inverse
                cols[j] = jnp.where(hit, scaled, cols[j] - own * scaled)
            scaled = line(rows, k) * inverse
            rows = jnp.where(hit, scaled, rows - own * scaled)
        tiles[p] = rows
        inside_panel = (lane >= first) & (lane < first + 8)
        apart = [zero if i in (p, p + 1) else jnp.where(inside_panel, tiles[i], 0.0) for i in range(8)]
        placed = [rows if i == p else zero for i in range(8)]
        change = multiply(jnp.concatenate(apart, axis=0)[:, :64], jnp.concatenate(placed, axis=0))
        for i in range(8):
            if i == p + 1:
                f = [spread(tiles[i], first + k) * line(rows, k) for k in range(8)]
                tiles[i] = tiles[i] - (((f[0] + f[1]) + (f[2] + f[3])) + ((f[4] + f[5]) + (f[6] + f[7])))
            elif i != p:
                tiles[i] = tiles[i] - change[8 * i : 8 * i + 8]
    return jnp.concatenate(tiles, axis=0)[:, 64:]


def solve_blocks(n, h):
    first = multiply(invert(h[0]), jnp.concatenate([h[1], h[2], n[0]], axis=1))
    change = multiply(jnp.concatenate([h[1], h[2]], axis=0), first)
    second = jnp.concatenate([h[2], h[3], n[1]], axis=1) - change[:64]
    third = jnp.concatenate([h[3], h[4], n[2]], axis=1) - change[64:]
    below = third[:, :64]
    second = multiply(invert(second[:, :64]), second[:, 64:])
    third = third[:, 64:] - multiply(below, second)
    y2 = multiply(invert(third[:, :64]), third[:, 64:])
    y1 = second[:, 64:] - multiply(second[:, :64], y2)
    y0 = first[:, 128:] - multiply(first[:, :64], y1) - multiply(first[:, 64:128], y2)
    return jnp.concatenate([y0, y1, y2], axis=0)


def finish_kernel(moments, v0, v1, v2, out):
    n = []
    for b in range(3):
        block = moments[64 * b : 64 * b + 64, :]
        other = jnp.transpose(jnp.concatenate([block, block], axis=0))
        n.append(0.5 * (block[:, :64] + other[:64, :64]))
        n.append(0.5 * (block[:, 64:] + other[64:, :64]))
    h = [n[m + 1] + SHIFT * n[m] for m in range(5)]
    solved = solve_blocks(n, h)
    weights = jnp.transpose(jnp.concatenate([solved, solved], axis=1))[64:]
    high, low = halves(weights)
    both = jnp.concatenate([high, low], axis=0)
    for c in range(3):
        for k in range(0, 8, 2):
            stack = jnp.concatenate([columns(v0, c, k + 1), columns(v1, c, k + 1), columns(v2, c, k)], axis=0)
            fine, rest = halves(stack)
            one = lax.dot_general(both, fine, NN, preferred_element_type=F32)
            two = lax.dot_general(high, rest, NN, preferred_element_type=F32)
            mixed = one[:64] + one[64:] + two
            for j in range(2):
                out[:, c, k + j] = mixed[:, LANES * j : LANES * j + LANES].reshape(8, 8, LANES)


def call(kernel, outs, scratch=(), n_in=1, flops=0, where=pltpu.VMEM, limit=48):
    single = not isinstance(outs, list)
    shapes = [outs] if single else outs
    vmem = pl.BlockSpec(memory_space=pltpu.VMEM)
    scratch = [pltpu.VMEM(a, F32) if isinstance(a, tuple) else a for a in scratch]
    done = pl.pallas_call(
        kernel,
        out_shape=[jax.ShapeDtypeStruct(s, F32) for s in shapes],
        in_specs=[pl.BlockSpec(memory_space=where)] * n_in,
        out_specs=[vmem] * len(shapes),
        scratch_shapes=scratch,
        compiler_params=pltpu.CompilerParams(vmem_limit_bytes=limit * 1024 * 1024),
        cost_estimate=pl.CostEstimate(flops=flops, bytes_accessed=4 * 1024 * 1024, transcendentals=0),
    )
    return (lambda *a: done(*a)[0]) if single else done


def exchange(x, axis):
    return lax.all_to_all(x, axis, split_axis=0, concat_axis=0, tiled=True)


def reduce_bricks(parts):
    space, rx = (lax.axis_size("space"), lax.axis_size("rx"))
    rows = parts.shape[0]
    pieces = exchange(parts.reshape(space, rows // space, LANES), "space")
    own = jnp.sum(pieces, axis=0)
    pieces = exchange(jnp.broadcast_to(own[None], (rx, *own.shape)), "rx")
    own = jnp.sum(pieces, axis=0)
    pieces = exchange(jnp.broadcast_to(own[None], (space, *own.shape)), "space")
    return pieces.reshape(rows, LANES)


def body(lambda_next, class_ids, class_rate, coil_x, coil_y, coil_z, coil_amp):
    size = lax.axis_size("space")
    chips = [(i, i ^ 1) for i in range(size)]
    fall = [(i + 1, i) for i in range(size - 1)]
    beside = [pair for i in range(1, size - 1, 2) for pair in ((i, i + 1), (i + 1, i))]
    arrays = (lambda_next, class_ids, class_rate, coil_x, coil_y, coil_z, coil_amp)
    spaces = [pltpu.VMEM] * 2 + [pltpu.SMEM] * 5
    outgoing, mass = call(
        enter_kernel,
        [(8, 3, GHOST, 8, LANES), (GHOST, 8, LANES)],
        [space(a.shape, a.dtype) for space, a in zip(spaces, arrays, strict=True)]
        + [(LANES, LANES), (67 * 8, LANES), (67 * 8, LANES), pltpu.SemaphoreType.DMA((7,))],
        n_in=7,
        where=pl.ANY,
        limit=60,
    )(*arrays)
    v0 = exchange(outgoing, "rx")
    message = (4, 2, 10, 8, LANES)
    outer = lax.ppermute(call(functools.partial(message_kernel, True), message)(v0), "space", beside)
    base, inner = call(functools.partial(base_kernel, 0), [(8, 3, 10, 8, LANES), message], n_in=2, flops=10**8)(v0, mass)
    inner = lax.ppermute(inner, "space", chips)
    v1, outer = call(second_kernel, [(8, 3, 10, 8, LANES), message], n_in=3)(outer, base, inner)
    outer = lax.ppermute(outer, "space", beside)
    base, inner = call(functools.partial(base_kernel, 1), [(8, 3, 9, 8, LANES), message], n_in=2, flops=10**8)(v1, mass)
    inner = lax.ppermute(inner, "space", chips)
    v2, down = call(third_kernel, [(8, 3, 9, 8, LANES), (4, 2, 8, 8, LANES)], n_in=3)(outer, base, inner)
    above = lax.ppermute(down, "space", fall)
    moments, curl = call(
        moments_kernel, [(192, LANES), (8, 2, 8, 8, LANES)], [(8, 1, 8, 8, LANES), (8, 3, 8, 8, LANES)], n_in=4, flops=10**8
    )(v0, v1, v2, mass)
    moments = call(energy_kernel, (192, LANES), n_in=3)(curl, above, moments)
    moments = reduce_bricks(moments)
    mixed = call(finish_kernel, (8, 3, 8, 8, LANES), n_in=4)(moments, v0, v1, v2)
    mixed = exchange(mixed, "rx")
    return call(leave_kernel, (8, 3, 2, PLANE, LANES), [(512, LANES), (LANES, LANES)])(mixed)


def solution(mesh):
    in_specs = (
        P("rx", None, "space", None, None),
        P("space", None, None),
        P(),
        P("rx"),
        P("rx"),
        P("rx"),
        P("rx"),
    )
    out_specs = P("rx", None, "space", None, None)
    return jax.shard_map(body, mesh=mesh, in_specs=in_specs, out_specs=out_specs, check_vma=False)
```

```python
import functools

import jax
import jax.numpy as jnp
from jax import lax
from jax.experimental import pallas as pl
from jax.experimental.pallas import tpu as pltpu
from jax.sharding import PartitionSpec as P

SHIFT = 6.0
LANES = 128
HALF = 64
PLANE = 32
GHOST = 11
SENT = 31
F32 = jnp.float32
BF16 = jnp.bfloat16
NT = (((1,), (1,)), ((), ()))
NN = (((1,), (0,)), ((), ()))


def lane_ids():
    lane = lax.broadcasted_iota(jnp.int32, (8, LANES), 1)
    return lane & 31, (lane >> 5) & 1, lane >> 6


def turn(a, shift):
    return pltpu.roll(a, shift, axis=a.ndim - 1)


def y_next(a):
    return jnp.where(lane_ids()[0] == 31, 0.0, turn(a, LANES - 1))


def y_prev(a):
    return jnp.where(lane_ids()[0] == 0, 0.0, turn(a, 1))


def z_both(a):
    half = turn(a, HALF)
    mixed = jnp.where(lane_ids()[2] == 0, half[:-1], half[1:])
    return jnp.concatenate([mixed, half[-1:]], axis=0), jnp.concatenate([half[:1], mixed], axis=0)


def x_next(a, beyond):
    return jnp.where(lane_ids()[1] == 0, turn(a, LANES - PLANE), beyond)


def x_prev(a, beyond):
    return jnp.where(lane_ids()[1] == 1, turn(a, PLANE), beyond)


def pack_up(a, b):
    return jnp.where(lane_ids()[1] == 1, a, turn(b, LANES - PLANE))


def pack_down(a, b):
    return jnp.where(lane_ids()[1] == 0, a, turn(b, PLANE))


def unpack(m, second, up):
    if not second:
        m = turn(m, LANES - PLANE) if up else turn(m, PLANE)
    return jnp.where(lane_ids()[1] == (0 if up else 1), m, 0.0)


def slopes(v):
    return v[1] + y_next(v[0]) - v[0], v[2] + z_both(v[0])[0] - v[0]


def apply_tiles(v, shifted):
    g1, g2 = slopes(v)
    e1 = v[1] - x_next(v[1], 0.0)
    e2 = v[2] - x_next(v[2], 0.0)
    q2 = z_both(v[2])[1] - v[2]
    q1 = y_prev(v[1]) - v[1]
    v1_next, v1_prev = z_both(v[1])
    r0 = 2.0 * v[0] + v[1] + v[2] - g1 - g2 + y_prev(e1 - v[0]) + z_both(e2 - v[0])[1] - e1 - e2
    r1 = g1 - x_prev(g1, 0.0) + e1 + 2.0 * v[1] - v1_next - v1_prev - y_next(q2) + q2
    r2 = g2 - x_prev(g2, 0.0) + e2 + 2.0 * v[2] - y_next(v[2]) - y_prev(v[2]) - z_both(q1)[0] + q1
    return [shifted * v[0] + r0, shifted * v[1] + r1, shifted * v[2] + r2]


def halves(a):
    high = a.astype(BF16)
    return high, (a - high.astype(F32)).astype(BF16)


def thirds(a):
    high = a.astype(BF16)
    rest = a - high.astype(F32)
    middle = rest.astype(BF16)
    return high, middle, (rest - middle.astype(F32)).astype(BF16)


def multiply(a, b):
    ah, am, al = thirds(a)
    bh, bm, bl = thirds(b)
    left = jnp.concatenate([ah, ah, am, am, ah, al], axis=1)
    right = jnp.concatenate([bh, bm, bh, bm, bl, bh], axis=0)
    return lax.dot_general(left, right, NN, preferred_element_type=F32)


def enter_kernel(*refs):
    (source, *sources), (out, mass_out), rest = refs[:7], refs[7:9], refs[9:]
    (field, *targets), (flipped, padded, ghost, mass_pad, loads, stores) = rest[:7], rest[7:]
    copies = [pltpu.make_async_copy(a, b, loads.at[i]) for i, (a, b) in enumerate(zip(sources, targets, strict=True))]
    parts = [pltpu.make_async_copy(source.at[:, c], field.at[c], loads.at[6 + c]) for c in range(3)]
    for copy in copies + parts:
        copy.start()
    for copy in copies:
        copy.wait()
    ids, rate, coil_x, coil_y, coil_z, amp = targets
    lane = lax.broadcasted_iota(jnp.int32, (64, LANES), 1)
    row = lax.broadcasted_iota(jnp.int32, (64, LANES), 0)
    classes = ids[...].reshape(64, LANES)
    mass = jnp.zeros((64, LANES), F32)
    for k in range(rate.shape[0]):
        mass = jnp.where(classes == k, rate[k], mass)
    left = lane < HALF
    flipped[...] = jnp.transpose(jnp.concatenate([mass, mass], axis=0))
    rows = jnp.where(left, flipped[pl.ds(0, 64, stride=2), :], flipped[pl.ds(1, 64, stride=2), :])
    mass_pad[0:8, :] = jnp.zeros((8, LANES), F32)
    mass_pad[8 * 65 :, :] = jnp.zeros((16, LANES), F32)
    for r in range(8):
        mass_pad[pl.ds(8 + r, 64, stride=8), :] = rows
    first = pl.multiple_of(lax.axis_index("rx") * 64, 64)
    mass_out[...] = mass_pad[pl.ds(first, 8 * GHOST), :].reshape(GHOST, 8, LANES) - SHIFT
    base = lax.axis_index("space") * 2

    def right(r, c):
        values = mass * field[c, r].reshape(64, LANES)
        if c == 2:
            return values
        near = coil_x[r] - base
        far = near + 1
        spot = jnp.where((near >= 0) & (near < 2), near * 32 + coil_y[r], -100)
        if c == 0:
            plus, minus = spot, spot + 1
        else:
            plus, minus = jnp.where((far >= 0) & (far < 2), far * 32 + coil_y[r], -100), spot
        strength = jnp.where(row == plus, amp[r], jnp.where(row == minus, -amp[r], 0.0))
        return values + jnp.where(lane == coil_z[r], strength, 0.0)

    sends = []
    for c in range(3):
        parts[c].wait()
        padded[c, 0:8, :] = jnp.zeros((8, LANES), F32)
        padded[c, 8 * 65 :, :] = jnp.zeros((16, LANES), F32)
        for r in range(4):
            flipped[...] = jnp.transpose(jnp.concatenate([right(r, c), right(r + 4, c)], axis=0))
            even = flipped[pl.ds(0, 64, stride=2), :]
            odd = flipped[pl.ds(1, 64, stride=2), :]
            padded[c, pl.ds(8 + r, 64, stride=8), :] = jnp.where(left, even, turn(odd, HALF))
            padded[c, pl.ds(12 + r, 64, stride=8), :] = jnp.where(left, turn(even, HALF), odd)
        sends += [(padded.at[c, 64 * d : 64 * d + 80], out.at[d, 80 * c : 80 * c + 80]) for d in range(8)]
        if c == 1:
            for d in range(8):
                tiles = [padded[k, 64 * d + 80 : 64 * d + 88, :] for k in range(2)]
                ghost[8 * d : 8 * d + 8, :] = jnp.where(left[:8], tiles[0], turn(tiles[1], HALF))
            sends += [(ghost.at[8 * d : 8 * d + 8], out.at[d, 240:248]) for d in range(8)]
        for i, pair in enumerate(sends):
            if i >= (0, 8, 24)[c]:
                sends[i] = pltpu.make_async_copy(*pair, stores.at[i])
                sends[i].start()
    for copy in sends:
        copy.wait()


def first_fields(v0, s):
    last = v0[s, pl.ds(SENT - 1, 1)]
    ends = [last, turn(last, HALF), jnp.zeros((1, 8, LANES), F32)]
    return [jnp.concatenate([v0[s, 10 * c : 10 * c + 10], ends[c]], axis=0) for c in range(3)]


def fields_of(v, s):
    return first_fields(v, s) if v.shape[1] == SENT else [v[s, c] for c in range(3)]


def leave_kernel(tiles, out, gathered, flipped, result, sems):
    left = lax.broadcasted_iota(jnp.int32, (64, LANES), 1) < HALF
    sends = []
    for c in range(3):
        for s in range(8):
            gathered[64 * s : 64 * s + 64, :] = tiles[s, c].reshape(64, LANES)
        for r in range(4):
            one = gathered[pl.ds(r, 64, stride=8), :]
            two = gathered[pl.ds(r + 4, 64, stride=8), :]
            flipped[pl.ds(0, 64, stride=2), :] = jnp.where(left, one, turn(two, HALF))
            flipped[pl.ds(1, 64, stride=2), :] = jnp.where(left, turn(one, HALF), two)
            back = jnp.transpose(flipped[...])
            result[c, r] = back[:64].reshape(2, PLANE, LANES)
            result[c, r + 4] = back[64:].reshape(2, PLANE, LANES)
        sends.append(pltpu.make_async_copy(result.at[c], out.at[:, c], sems.at[c]))
        sends[c].start()
    for copy in sends:
        copy.wait()


def is_even():
    return lax.axis_index("space") % 2 == 0


def send(message, to_above, s, v, w):
    last = GHOST - 1

    @pl.when(to_above)
    def _():
        for c, (a, b) in enumerate(zip(slopes(v), slopes(w), strict=True)):
            message[s, c] = pack_up(a[:last], b[:last])

    @pl.when(jnp.logical_not(to_above))
    def _():
        for c in range(2):
            message[s, c] = pack_down(v[c + 1][:last], w[c + 1][:last])


def message_kernel(outer, v, message):
    def step(s, carry):
        fields = [fields_of(v, s + 4 * k) for k in range(2)]
        send(message, is_even() != outer, s, *fields)
        return carry

    lax.fori_loop(0, 4, step, 0)


def receive(inner, outer, s, c):
    even = is_even()
    return jnp.where(even, outer[s, c], inner[s, c]), jnp.where(even, inner[s, c], outer[s, c])


def inside(values, first_tile, last_tile):
    index = lax.axis_index("rx")
    rows = values.shape[0]
    low = jnp.where(index == 0, 0.0, 1.0)
    high = jnp.where(index == lax.axis_size("rx") - 1, 0.0, 1.0)
    pieces = [values]
    if first_tile:
        pieces = [values[:1] * low, values[1:]]
    if last_tile:
        pieces = [*pieces[:-1], pieces[-1][:-1], pieces[-1][-1:] * high]
    return jnp.concatenate(pieces, axis=0) if rows else values


def base_kernel(first, v, mass, base, inner):
    def step(s, carry):
        fields = [fields_of(v, s + 4 * k) for k in range(2)]
        for k in range(2):
            result = apply_tiles(fields[k], mass[: fields[k][0].shape[0]])
            for c in range(3):
                base[s + 4 * k, c] = result[c][first : first + base.shape[2]]
        send(inner, is_even(), s, *fields)
        return carry

    lax.fori_loop(0, 4, step, 0)


def completed(base, inner, outer, s, k, first):
    below, above = zip(*(receive(inner, outer, s, c) for c in range(2)), strict=True)
    beyond = [unpack(a, k, False) for a in above]
    before = [unpack(a, k, True) for a in below]
    changes = [
        beyond[0] + beyond[1] - y_prev(beyond[0]) - z_both(beyond[1])[1],
        -beyond[0] - before[0],
        -beyond[1] - before[1],
    ]
    return [inside(base[s + 4 * k, c] + changes[c][first:], first == 0, True) for c in range(3)]


def second_kernel(outer, base, inner, v1, next_outer):
    def step(s, carry):
        fields = [completed(base, inner, outer, s, k, 0) for k in range(2)]
        for k in range(2):
            for c in range(3):
                v1[s + 4 * k, c] = fields[k][c]
        send(next_outer, jnp.logical_not(is_even()), s, *fields)
        return carry

    lax.fori_loop(0, 4, step, 0)


def third_kernel(outer, base, inner, v2, down):
    def step(s, carry):
        fields = [completed(base, inner, outer, s, k, 1) for k in range(2)]
        for k in range(2):
            for c in range(3):
                v2[s + 4 * k, c] = fields[k][c]
        for c in range(2):
            down[s, c] = pack_down(fields[0][c + 1][:8], fields[1][c + 1][:8])
        return carry

    lax.fori_loop(0, 4, step, 0)


def columns(ref, c, first):
    at = lambda k: ref[:, 10 * c + k] if ref.shape[1] == SENT else ref[:, c, k]
    return jnp.concatenate([at(first + k).reshape(64, LANES) for k in range(2)], axis=1)


def bend(parts):
    return lax.dot_general(parts[:128], parts, NT, preferred_element_type=F32)


def fold(bends):
    return bends[:64, :64] + 2.0 * (bends[:64, 64:128] + bends[:64, 128:]) + bends[64:, 64:128]


def moments_kernel(v0, v1, v2, mass, out, curl, curl0, scaled):
    y, x, parity = lane_ids()
    first_x = jnp.where((x == 0) & (lax.axis_index("space") == 0), 1.0, 0.0)
    first_y = jnp.where(y == 0, 1.0, 0.0)
    tile = lax.broadcasted_iota(jnp.int32, (8, 8, LANES), 0)
    first_z = jnp.where((tile == 0) & (parity == 0) & (lax.axis_index("rx") == 0), 1.0, 0.0)
    own = mass[1:9]
    faces = [first_y + first_z, first_x + first_z, first_x + first_y]

    def step(s, carry):
        v = [v2[s, c] for c in range(3)]
        z1 = z_both(v[1])[0][:8]
        z0 = z_both(v[0])[0][:8]
        v = [a[:8] for a in v]
        curl0[s, 0] = y_next(v[2]) - v[2] - z1 + v[1]
        curl[s, 0] = z0 - v[0] - x_next(v[2], 0.0) + v[2]
        curl[s, 1] = x_next(v[1], 0.0) - v[1] - y_next(v[0]) + v[0]
        for c in range(3):
            scaled[s, c] = v[c] * (own + faces[c])
        return carry

    lax.fori_loop(0, 8, step, 0)
    bends = jnp.zeros((128, 192), F32)
    mixed = jnp.zeros((192, 192), F32)
    total = jnp.zeros((192, 576), F32)
    middles = jnp.zeros((192, 192), F32)
    for c in range(3):
        for k in range(0, 8, 2):
            stack = jnp.concatenate([columns(v0, c, k + 1), columns(v1, c, k + 1), columns(v2, c, k)], axis=0)
            parts = thirds(stack)
            total = total + lax.dot_general(
                parts[0], jnp.concatenate(parts, axis=0), NT, preferred_element_type=F32
            )
            middles = middles + lax.dot_general(parts[1], parts[1], NT, preferred_element_type=F32)
            wide = jnp.concatenate(thirds(columns(scaled, c, k)), axis=0)
            field = jnp.concatenate([a[128:] for a in parts], axis=0)
            mixed = mixed + lax.dot_general(wide, field, NT, preferred_element_type=F32)
            if c == 0:
                bends = bends + bend(jnp.concatenate(thirds(columns(curl0, c, k)), axis=0))
    main, cross = total[:, :192] + middles, total[:, 192:384] + total[:, 384:]
    last = fold(bends)
    for i, j in ((0, 0), (0, 1), (1, 0), (1, 1), (0, 2), (2, 0)):
        last = last + mixed[64 * i : 64 * i + 64, 64 * j : 64 * j + 64]

    def block(i, j):
        at = lambda m, p, q: m[64 * p : 64 * p + 64, 64 * q : 64 * q + 64]
        return at(main, i, j) + at(cross, i, j) + at(cross, j, i)

    out[0:64, :] = jnp.concatenate([block(0, 0), block(0, 1)], axis=1)
    out[64:128, :] = jnp.concatenate([block(1, 1), block(1, 2)], axis=1)
    out[128:192, :] = jnp.concatenate([block(2, 2), last], axis=1)


def energy_kernel(curl, above, moments, out):
    bends = jnp.zeros((128, 192), F32)
    for c in range(2):
        for k in range(0, 8, 2):
            rows = []
            for j in range(2):
                beyond = jnp.concatenate([unpack(above[:, 1 - c, k + j], half, False) for half in range(2)], axis=0)
                bent = curl[:, c, k + j] - beyond if c == 0 else curl[:, c, k + j] + beyond
                rows.append(bent.reshape(64, LANES))
            bends = bends + bend(jnp.concatenate(thirds(jnp.concatenate(rows, axis=1)), axis=0))
    out[0:128, :] = moments[0:128, :]
    out[128:192, :] = moments[128:192, :] + jnp.concatenate([jnp.zeros((64, 64), F32), fold(bends)], axis=1)


def spread(a, lane):
    return jnp.broadcast_to(a[:, lane : lane + 1], (8, LANES))


def line(a, k):
    return jnp.broadcast_to(a[k : k + 1], (8, LANES))


def invert(matrix):
    unit = lax.broadcasted_iota(jnp.int32, (64, 64), 0) == lax.broadcasted_iota(jnp.int32, (64, 64), 1)
    both = jnp.concatenate([matrix, jnp.where(unit, 1.0, 0.0)], axis=1)
    tiles = [both[8 * i : 8 * i + 8] for i in range(8)]
    origin = list(tiles)
    sub = lax.broadcasted_iota(jnp.int32, (8, LANES), 0)
    lane = lax.broadcasted_iota(jnp.int32, (8, LANES), 1)
    zero = jnp.zeros((8, LANES), F32)
    for p in range(8):
        rows, first = tiles[p], 8 * p
        cols = [spread(rows, first + k) for k in range(8)]
        for k in range(8):
            floor = line(spread(origin[p], first + k), k) * 2e-7
            pivot = line(cols[k], k)
            inverse = jnp.where(pivot > floor, 1.0 / pivot, 0.0)
            own, hit = cols[k], sub == k
            for j in range(k + 1, 8):
                scaled = line(cols[j], k) * inverse
                cols[j] = jnp.where(hit, scaled, cols[j] - own * scaled)
            scaled = line(rows, k) * inverse
            rows = jnp.where(hit, scaled, rows - own * scaled)
        tiles[p] = rows
        inside_panel = (lane >= first) & (lane < first + 8)
        apart = [zero if i in (p, p + 1) else jnp.where(inside_panel, tiles[i], 0.0) for i in range(8)]
        placed = [rows if i == p else zero for i in range(8)]
        change = multiply(jnp.concatenate(apart, axis=0)[:, :64], jnp.concatenate(placed, axis=0))
        for i in range(8):
            if i == p + 1:
                f = [spread(tiles[i], first + k) * line(rows, k) for k in range(8)]
                tiles[i] = tiles[i] - (((f[0] + f[1]) + (f[2] + f[3])) + ((f[4] + f[5]) + (f[6] + f[7])))
            elif i != p:
                tiles[i] = tiles[i] - change[8 * i : 8 * i + 8]
    return jnp.concatenate(tiles, axis=0)[:, 64:]


def solve_blocks(n, h):
    first = multiply(invert(h[0]), jnp.concatenate([h[1], h[2], n[0]], axis=1))
    change = multiply(jnp.concatenate([h[1], h[2]], axis=0), first)
    second = jnp.concatenate([h[2], h[3], n[1]], axis=1) - change[:64]
    third = jnp.concatenate([h[3], h[4], n[2]], axis=1) - change[64:]
    below = third[:, :64]
    second = multiply(invert(second[:, :64]), second[:, 64:])
    third = third[:, 64:] - multiply(below, second)
    y2 = multiply(invert(third[:, :64]), third[:, 64:])
    y1 = second[:, 64:] - multiply(second[:, :64], y2)
    y0 = first[:, 128:] - multiply(first[:, :64], y1) - multiply(first[:, 64:128], y2)
    return jnp.concatenate([y0, y1, y2], axis=0)


def finish_kernel(moments, v0, v1, v2, out):
    n = []
    for b in range(3):
        block = moments[64 * b : 64 * b + 64, :]
        other = jnp.transpose(jnp.concatenate([block, block], axis=0))
        n.append(0.5 * (block[:, :64] + other[:64, :64]))
        n.append(0.5 * (block[:, 64:] + other[64:, :64]))
    h = [n[m + 1] + SHIFT * n[m] for m in range(5)]
    solved = solve_blocks(n, h)
    weights = jnp.transpose(jnp.concatenate([solved, solved], axis=1))[64:]
    high, low = halves(weights)
    both = jnp.concatenate([high, low], axis=0)
    for c in range(3):
        for k in range(0, 8, 2):
            stack = jnp.concatenate([columns(v0, c, k + 1), columns(v1, c, k + 1), columns(v2, c, k)], axis=0)
            fine, rest = halves(stack)
            one = lax.dot_general(both, fine, NN, preferred_element_type=F32)
            two = lax.dot_general(high, rest, NN, preferred_element_type=F32)
            mixed = one[:64] + one[64:] + two
            for j in range(2):
                out[:, c, k + j] = mixed[:, LANES * j : LANES * j + LANES].reshape(8, 8, LANES)


def call(kernel, outs, scratch=(), n_in=1, flops=0, where=pltpu.VMEM, limit=48, far=False):
    single = not isinstance(outs, list)
    shapes = [outs] if single else outs
    vmem = pl.BlockSpec(memory_space=pltpu.VMEM)
    scratch = [pltpu.VMEM(a, F32) if isinstance(a, tuple) else a for a in scratch]
    done = pl.pallas_call(
        kernel,
        out_shape=[jax.ShapeDtypeStruct(s, F32) for s in shapes],
        in_specs=[pl.BlockSpec(memory_space=where)] * n_in,
        out_specs=[pl.BlockSpec(memory_space=pl.ANY) if far else vmem, *[vmem] * (len(shapes) - 1)],
        scratch_shapes=scratch,
        compiler_params=pltpu.CompilerParams(vmem_limit_bytes=limit * 1024 * 1024),
        cost_estimate=pl.CostEstimate(flops=flops, bytes_accessed=4 * 1024 * 1024, transcendentals=0),
    )
    return (lambda *a: done(*a)[0]) if single else done


def exchange(x, axis):
    return lax.all_to_all(x, axis, split_axis=0, concat_axis=0, tiled=True)


def reduce_bricks(parts):
    space, rx = (lax.axis_size("space"), lax.axis_size("rx"))
    rows = parts.shape[0]
    pieces = exchange(parts.reshape(space, rows // space, LANES), "space")
    own = jnp.sum(pieces, axis=0)
    pieces = exchange(jnp.broadcast_to(own[None], (rx, *own.shape)), "rx")
    own = jnp.sum(pieces, axis=0)
    pieces = exchange(jnp.broadcast_to(own[None], (space, *own.shape)), "space")
    return pieces.reshape(rows, LANES)


def body(lambda_next, class_ids, class_rate, coil_x, coil_y, coil_z, coil_amp):
    size = lax.axis_size("space")
    chips = [(i, i ^ 1) for i in range(size)]
    fall = [(i + 1, i) for i in range(size - 1)]
    beside = [pair for i in range(1, size - 1, 2) for pair in ((i, i + 1), (i + 1, i))]
    arrays = (lambda_next, class_ids, class_rate, coil_x, coil_y, coil_z, coil_amp)
    spaces = [pltpu.VMEM] + [pltpu.SMEM] * 5
    outgoing, mass = call(
        enter_kernel,
        [(8, 8 * SENT, LANES), (GHOST, 8, LANES)],
        [(3, 8, 2, PLANE, LANES)]
        + [space(a.shape, a.dtype) for space, a in zip(spaces, arrays[1:], strict=True)]
        + [(LANES, LANES), (3, 67 * 8, LANES), (64, LANES), (67 * 8, LANES)]
        + [pltpu.SemaphoreType.DMA((9,)), pltpu.SemaphoreType.DMA((32,))],
        n_in=7,
        where=pl.ANY,
        limit=60,
        far=True,
    )(*arrays)
    v0 = exchange(outgoing, "rx").reshape(8, SENT, 8, LANES)
    message = (4, 2, 10, 8, LANES)
    outer = lax.ppermute(call(functools.partial(message_kernel, True), message)(v0), "space", beside)
    base, inner = call(functools.partial(base_kernel, 0), [(8, 3, 10, 8, LANES), message], n_in=2, flops=10**8)(v0, mass)
    inner = lax.ppermute(inner, "space", chips)
    v1, outer = call(second_kernel, [(8, 3, 10, 8, LANES), message], n_in=3)(outer, base, inner)
    outer = lax.ppermute(outer, "space", beside)
    base, inner = call(functools.partial(base_kernel, 1), [(8, 3, 9, 8, LANES), message], n_in=2, flops=10**8)(v1, mass)
    inner = lax.ppermute(inner, "space", chips)
    v2, down = call(third_kernel, [(8, 3, 9, 8, LANES), (4, 2, 8, 8, LANES)], n_in=3)(outer, base, inner)
    above = lax.ppermute(down, "space", fall)
    moments, curl = call(
        moments_kernel, [(192, LANES), (8, 2, 8, 8, LANES)], [(8, 1, 8, 8, LANES), (8, 3, 8, 8, LANES)], n_in=4, flops=10**8
    )(v0, v1, v2, mass)
    moments = call(energy_kernel, (192, LANES), n_in=3)(curl, above, moments)
    moments = reduce_bricks(moments)
    mixed = call(finish_kernel, (8, 3, 8, 8, LANES), n_in=4)(moments, v0, v1, v2)
    mixed = exchange(mixed, "rx")
    scratch = [(512, LANES), (LANES, LANES), (3, 8, 2, PLANE, LANES), pltpu.SemaphoreType.DMA((3,))]
    return call(leave_kernel, (8, 3, 2, PLANE, LANES), scratch, far=True)(mixed)


def solution(mesh):
    in_specs = (
        P("rx", None, "space", None, None),
        P("space", None, None),
        P(),
        P("rx"),
        P("rx"),
        P("rx"),
        P("rx"),
    )
    out_specs = P("rx", None, "space", None, None)
    return jax.shard_map(body, mesh=mesh, in_specs=in_specs, out_specs=out_specs, check_vma=False)
```

```python
import functools

import jax
import jax.numpy as jnp
from jax import lax
from jax.experimental import pallas as pl
from jax.experimental.pallas import tpu as pltpu
from jax.sharding import PartitionSpec as P

SHIFT = 6.0
LANES = 128
HALF = 64
PLANE = 32
GHOST = 11
SENT = 31
F32 = jnp.float32
BF16 = jnp.bfloat16
NT = (((1,), (1,)), ((), ()))
NN = (((1,), (0,)), ((), ()))


def lane_ids():
    lane = lax.broadcasted_iota(jnp.int32, (8, LANES), 1)
    return lane & 31, (lane >> 5) & 1, lane >> 6


def turn(a, shift):
    return pltpu.roll(a, shift, axis=a.ndim - 1)


def y_next(a):
    return jnp.where(lane_ids()[0] == 31, 0.0, turn(a, LANES - 1))


def y_prev(a):
    return jnp.where(lane_ids()[0] == 0, 0.0, turn(a, 1))


def z_both(a):
    half = turn(a, HALF)
    mixed = jnp.where(lane_ids()[2] == 0, half[:-1], half[1:])
    return jnp.concatenate([mixed, half[-1:]], axis=0), jnp.concatenate([half[:1], mixed], axis=0)


def x_next(a, beyond):
    return jnp.where(lane_ids()[1] == 0, turn(a, LANES - PLANE), beyond)


def x_prev(a, beyond):
    return jnp.where(lane_ids()[1] == 1, turn(a, PLANE), beyond)


def pack_up(a, b):
    return jnp.where(lane_ids()[1] == 1, a, turn(b, LANES - PLANE))


def pack_down(a, b):
    return jnp.where(lane_ids()[1] == 0, a, turn(b, PLANE))


def unpack(m, second, up):
    if not second:
        m = turn(m, LANES - PLANE) if up else turn(m, PLANE)
    return jnp.where(lane_ids()[1] == (0 if up else 1), m, 0.0)


def slopes(v):
    return v[1] + y_next(v[0]) - v[0], v[2] + z_both(v[0])[0] - v[0]


def apply_tiles(v, shifted):
    g1, g2 = slopes(v)
    e1 = v[1] - x_next(v[1], 0.0)
    e2 = v[2] - x_next(v[2], 0.0)
    q2 = z_both(v[2])[1] - v[2]
    q1 = y_prev(v[1]) - v[1]
    v1_next, v1_prev = z_both(v[1])
    r0 = 2.0 * v[0] + v[1] + v[2] - g1 - g2 + y_prev(e1 - v[0]) + z_both(e2 - v[0])[1] - e1 - e2
    r1 = g1 - x_prev(g1, 0.0) + e1 + 2.0 * v[1] - v1_next - v1_prev - y_next(q2) + q2
    r2 = g2 - x_prev(g2, 0.0) + e2 + 2.0 * v[2] - y_next(v[2]) - y_prev(v[2]) - z_both(q1)[0] + q1
    return [shifted * v[0] + r0, shifted * v[1] + r1, shifted * v[2] + r2]


def halves(a):
    high = a.astype(BF16)
    return high, (a - high.astype(F32)).astype(BF16)


def thirds(a):
    high = a.astype(BF16)
    rest = a - high.astype(F32)
    middle = rest.astype(BF16)
    return high, middle, (rest - middle.astype(F32)).astype(BF16)


def multiply(a, b):
    ah, am, al = thirds(a)
    bh, bm, bl = thirds(b)
    left = jnp.concatenate([ah, ah, am, am, ah, al], axis=1)
    right = jnp.concatenate([bh, bm, bh, bm, bl, bh], axis=0)
    return lax.dot_general(left, right, NN, preferred_element_type=F32)


def enter_kernel(*refs):
    (source, *sources), (out, mass_out), rest = refs[:7], refs[7:9], refs[9:]
    (field, *targets), (flipped, padded, mass_pad, loads) = rest[:7], rest[7:]
    copies = [pltpu.make_async_copy(a, b, loads.at[i]) for i, (a, b) in enumerate(zip(sources, targets, strict=True))]
    copies = [pltpu.make_async_copy(source, field, loads.at[6]), *copies]
    for copy in copies:
        copy.start()
    for copy in copies:
        copy.wait()
    ids, rate, coil_x, coil_y, coil_z, amp = targets
    lane = lax.broadcasted_iota(jnp.int32, (64, LANES), 1)
    row = lax.broadcasted_iota(jnp.int32, (64, LANES), 0)
    classes = ids[...].reshape(64, LANES)
    mass = jnp.zeros((64, LANES), F32)
    for k in range(rate.shape[0]):
        mass = jnp.where(classes == k, rate[k], mass)
    left = lane < HALF
    flipped[12] = jnp.transpose(jnp.concatenate([mass, mass], axis=0))
    rows = jnp.where(left, flipped[12, pl.ds(0, 64, stride=2), :], flipped[12, pl.ds(1, 64, stride=2), :])
    mass_pad[0:8, :] = jnp.zeros((8, LANES), F32)
    mass_pad[8 * 65 :, :] = jnp.zeros((16, LANES), F32)
    for r in range(8):
        mass_pad[pl.ds(8 + r, 64, stride=8), :] = rows
    first = pl.multiple_of(lax.axis_index("rx") * 64, 64)
    mass_out[...] = mass_pad[pl.ds(first, 8 * GHOST), :].reshape(GHOST, 8, LANES) - SHIFT
    base = lax.axis_index("space") * 2

    def right(r, c):
        values = mass * field[r, c].reshape(64, LANES)
        if c == 2:
            return values
        near = coil_x[r] - base
        far = near + 1
        spot = jnp.where((near >= 0) & (near < 2), near * 32 + coil_y[r], -100)
        if c == 0:
            plus, minus = spot, spot + 1
        else:
            plus, minus = jnp.where((far >= 0) & (far < 2), far * 32 + coil_y[r], -100), spot
        strength = jnp.where(row == plus, amp[r], jnp.where(row == minus, -amp[r], 0.0))
        return values + jnp.where(lane == coil_z[r], strength, 0.0)

    for c in range(3):
        padded[c, 0:8, :] = jnp.zeros((8, LANES), F32)
        padded[c, 8 * 65 :, :] = jnp.zeros((16, LANES), F32)
        for r in range(4):
            flipped[c * 4 + r] = jnp.transpose(jnp.concatenate([right(r, c), right(r + 4, c)], axis=0))
            even = flipped[c * 4 + r, pl.ds(0, 64, stride=2), :]
            odd = flipped[c * 4 + r, pl.ds(1, 64, stride=2), :]
            padded[c, pl.ds(8 + r, 64, stride=8), :] = jnp.where(left, even, turn(odd, HALF))
            padded[c, pl.ds(12 + r, 64, stride=8), :] = jnp.where(left, turn(even, HALF), odd)
        for d in range(8):
            out[d, 80 * c : 80 * c + 80] = padded[c, 64 * d : 64 * d + 80, :]
    for d in range(8):
        tiles = [padded[k, 64 * d + 80 : 64 * d + 88, :] for k in range(2)]
        out[d, 240:248] = jnp.where(left[:8], tiles[0], turn(tiles[1], HALF))


def first_fields(v0, s):
    last = v0[s, pl.ds(SENT - 1, 1)]
    ends = [last, turn(last, HALF), jnp.zeros((1, 8, LANES), F32)]
    return [jnp.concatenate([v0[s, 10 * c : 10 * c + 10], ends[c]], axis=0) for c in range(3)]


def fields_of(v, s):
    return first_fields(v, s) if v.shape[1] == SENT else [v[s, c] for c in range(3)]


def leave_kernel(tiles, out, gathered, flipped, result, sems):
    left = lax.broadcasted_iota(jnp.int32, (64, LANES), 1) < HALF
    sends = []
    for c in range(3):
        for s in range(8):
            gathered[64 * s : 64 * s + 64, :] = tiles[s, c].reshape(64, LANES)
        for r in range(4):
            one = gathered[pl.ds(r, 64, stride=8), :]
            two = gathered[pl.ds(r + 4, 64, stride=8), :]
            flipped[pl.ds(0, 64, stride=2), :] = jnp.where(left, one, turn(two, HALF))
            flipped[pl.ds(1, 64, stride=2), :] = jnp.where(left, turn(one, HALF), two)
            back = jnp.transpose(flipped[...])
            result[c, r] = back[:64].reshape(2, PLANE, LANES)
            result[c, r + 4] = back[64:].reshape(2, PLANE, LANES)
        sends.append(pltpu.make_async_copy(result.at[c], out.at[:, c], sems.at[c]))
        sends[c].start()
    for copy in sends:
        copy.wait()


def is_even():
    return lax.axis_index("space") % 2 == 0


def send(message, to_above, s, v, w):
    last = GHOST - 1

    @pl.when(to_above)
    def _():
        for c, (a, b) in enumerate(zip(slopes(v), slopes(w), strict=True)):
            message[s, c] = pack_up(a[:last], b[:last])

    @pl.when(jnp.logical_not(to_above))
    def _():
        for c in range(2):
            message[s, c] = pack_down(v[c + 1][:last], w[c + 1][:last])


def message_kernel(outer, v, message):
    def step(s, carry):
        fields = [fields_of(v, s + 4 * k) for k in range(2)]
        send(message, is_even() != outer, s, *fields)
        return carry

    lax.fori_loop(0, 4, step, 0)


def receive(inner, outer, s, c):
    even, index = is_even(), lax.axis_index("space")
    edge = (index == 0) | (index == lax.axis_size("space") - 1)
    near, far = inner[s, c], jnp.where(edge, 0.0, outer[s, c])
    return jnp.where(even, far, near), jnp.where(even, near, far)


def inside(values, first_tile, last_tile):
    index = lax.axis_index("rx")
    rows = values.shape[0]
    low = jnp.where(index == 0, 0.0, 1.0)
    high = jnp.where(index == lax.axis_size("rx") - 1, 0.0, 1.0)
    pieces = [values]
    if first_tile:
        pieces = [values[:1] * low, values[1:]]
    if last_tile:
        pieces = [*pieces[:-1], pieces[-1][:-1], pieces[-1][-1:] * high]
    return jnp.concatenate(pieces, axis=0) if rows else values


def base_kernel(first, v, mass, base, inner):
    def step(s, carry):
        fields = [fields_of(v, s + 4 * k) for k in range(2)]
        for k in range(2):
            result = apply_tiles(fields[k], mass[: fields[k][0].shape[0]])
            for c in range(3):
                base[s + 4 * k, c] = result[c][first : first + base.shape[2]]
        send(inner, is_even(), s, *fields)
        return carry

    lax.fori_loop(0, 4, step, 0)


def completed(base, inner, outer, s, k, first):
    below, above = zip(*(receive(inner, outer, s, c) for c in range(2)), strict=True)
    beyond = [unpack(a, k, False) for a in above]
    before = [unpack(a, k, True) for a in below]
    changes = [
        beyond[0] + beyond[1] - y_prev(beyond[0]) - z_both(beyond[1])[1],
        -beyond[0] - before[0],
        -beyond[1] - before[1],
    ]
    return [inside(base[s + 4 * k, c] + changes[c][first:], first == 0, True) for c in range(3)]


def second_kernel(outer, base, inner, v1, next_outer):
    def step(s, carry):
        fields = [completed(base, inner, outer, s, k, 0) for k in range(2)]
        for k in range(2):
            for c in range(3):
                v1[s + 4 * k, c] = fields[k][c]
        send(next_outer, jnp.logical_not(is_even()), s, *fields)
        return carry

    lax.fori_loop(0, 4, step, 0)


def third_kernel(outer, base, inner, v2, down):
    def step(s, carry):
        fields = [completed(base, inner, outer, s, k, 1) for k in range(2)]
        for k in range(2):
            for c in range(3):
                v2[s + 4 * k, c] = fields[k][c]
        for c in range(2):
            down[s, c] = pack_down(fields[0][c + 1][:8], fields[1][c + 1][:8])
        return carry

    lax.fori_loop(0, 4, step, 0)


def columns(ref, c, first):
    at = lambda k: ref[:, 10 * c + k] if ref.shape[1] == SENT else ref[:, c, k]
    return jnp.concatenate([at(first + k).reshape(64, LANES) for k in range(2)], axis=1)


def bend(parts):
    return lax.dot_general(parts[:128], parts, NT, preferred_element_type=F32)


def fold(bends):
    return bends[:64, :64] + 2.0 * (bends[:64, 64:128] + bends[:64, 128:]) + bends[64:, 64:128]


def moments_kernel(v0, v1, v2, mass, out, curl, curl0, scaled):
    y, x, parity = lane_ids()
    first_x = jnp.where((x == 0) & (lax.axis_index("space") == 0), 1.0, 0.0)
    first_y = jnp.where(y == 0, 1.0, 0.0)
    tile = lax.broadcasted_iota(jnp.int32, (8, 8, LANES), 0)
    first_z = jnp.where((tile == 0) & (parity == 0) & (lax.axis_index("rx") == 0), 1.0, 0.0)
    own = mass[1:9]
    faces = [first_y + first_z, first_x + first_z, first_x + first_y]

    def step(s, carry):
        v = [v2[s, c] for c in range(3)]
        z1 = z_both(v[1])[0][:8]
        z0 = z_both(v[0])[0][:8]
        v = [a[:8] for a in v]
        curl0[s, 0] = y_next(v[2]) - v[2] - z1 + v[1]
        curl[s, 0] = z0 - v[0] - x_next(v[2], 0.0) + v[2]
        curl[s, 1] = x_next(v[1], 0.0) - v[1] - y_next(v[0]) + v[0]
        for c in range(3):
            scaled[s, c] = v[c] * (own + faces[c])
        return carry

    lax.fori_loop(0, 8, step, 0)
    bends = jnp.zeros((128, 192), F32)
    mixed = jnp.zeros((192, 192), F32)
    total = jnp.zeros((192, 576), F32)
    middles = jnp.zeros((192, 192), F32)
    for c in range(3):
        for k in range(0, 8, 2):
            stack = jnp.concatenate([columns(v0, c, k + 1), columns(v1, c, k + 1), columns(v2, c, k)], axis=0)
            parts = thirds(stack)
            total = total + lax.dot_general(
                parts[0], jnp.concatenate(parts, axis=0), NT, preferred_element_type=F32
            )
            middles = middles + lax.dot_general(parts[1], parts[1], NT, preferred_element_type=F32)
            wide = jnp.concatenate(thirds(columns(scaled, c, k)), axis=0)
            field = jnp.concatenate([a[128:] for a in parts], axis=0)
            mixed = mixed + lax.dot_general(wide, field, NT, preferred_element_type=F32)
            if c == 0:
                bends = bends + bend(jnp.concatenate(thirds(columns(curl0, c, k)), axis=0))
    main, cross = total[:, :192] + middles, total[:, 192:384] + total[:, 384:]
    last = fold(bends)
    for i, j in ((0, 0), (0, 1), (1, 0), (1, 1), (0, 2), (2, 0)):
        last = last + mixed[64 * i : 64 * i + 64, 64 * j : 64 * j + 64]

    def block(i, j):
        at = lambda m, p, q: m[64 * p : 64 * p + 64, 64 * q : 64 * q + 64]
        return at(main, i, j) + at(cross, i, j) + at(cross, j, i)

    out[0:64, :] = jnp.concatenate([block(0, 0), block(0, 1)], axis=1)
    out[64:128, :] = jnp.concatenate([block(1, 1), block(1, 2)], axis=1)
    out[128:192, :] = jnp.concatenate([block(2, 2), last], axis=1)


def energy_kernel(curl, above, moments, out):
    bends = jnp.zeros((128, 192), F32)
    edge = lax.axis_index("space") == lax.axis_size("space") - 1
    for c in range(2):
        for k in range(0, 8, 2):
            rows = []
            for j in range(2):
                beyond = jnp.concatenate([unpack(above[:, 1 - c, k + j], half, False) for half in range(2)], axis=0)
                beyond = jnp.where(edge, 0.0, beyond)
                bent = curl[:, c, k + j] - beyond if c == 0 else curl[:, c, k + j] + beyond
                rows.append(bent.reshape(64, LANES))
            bends = bends + bend(jnp.concatenate(thirds(jnp.concatenate(rows, axis=1)), axis=0))
    out[0:128, :] = moments[0:128, :]
    out[128:192, :] = moments[128:192, :] + jnp.concatenate([jnp.zeros((64, 64), F32), fold(bends)], axis=1)


def spread(a, lane):
    return jnp.broadcast_to(a[:, lane : lane + 1], (8, LANES))


def line(a, k):
    return jnp.broadcast_to(a[k : k + 1], (8, LANES))


def invert(matrix):
    unit = lax.broadcasted_iota(jnp.int32, (64, 64), 0) == lax.broadcasted_iota(jnp.int32, (64, 64), 1)
    both = jnp.concatenate([matrix, jnp.where(unit, 1.0, 0.0)], axis=1)
    tiles = [both[8 * i : 8 * i + 8] for i in range(8)]
    origin = list(tiles)
    sub = lax.broadcasted_iota(jnp.int32, (8, LANES), 0)
    lane = lax.broadcasted_iota(jnp.int32, (8, LANES), 1)
    zero = jnp.zeros((8, LANES), F32)
    for p in range(8):
        rows, first = tiles[p], 8 * p
        cols = [spread(rows, first + k) for k in range(8)]
        for k in range(8):
            floor = line(spread(origin[p], first + k), k) * 2e-7
            pivot = line(cols[k], k)
            inverse = jnp.where(pivot > floor, 1.0 / pivot, 0.0)
            own, hit = cols[k], sub == k
            for j in range(k + 1, 8):
                scaled = line(cols[j], k) * inverse
                cols[j] = jnp.where(hit, scaled, cols[j] - own * scaled)
            scaled = line(rows, k) * inverse
            rows = jnp.where(hit, scaled, rows - own * scaled)
        tiles[p] = rows
        inside_panel = (lane >= first) & (lane < first + 8)
        apart = [zero if i in (p, p + 1) else jnp.where(inside_panel, tiles[i], 0.0) for i in range(8)]
        placed = [rows if i == p else zero for i in range(8)]
        change = multiply(jnp.concatenate(apart, axis=0)[:, :64], jnp.concatenate(placed, axis=0))
        for i in range(8):
            if i == p + 1:
                f = [spread(tiles[i], first + k) * line(rows, k) for k in range(8)]
                tiles[i] = tiles[i] - (((f[0] + f[1]) + (f[2] + f[3])) + ((f[4] + f[5]) + (f[6] + f[7])))
            elif i != p:
                tiles[i] = tiles[i] - change[8 * i : 8 * i + 8]
    return jnp.concatenate(tiles, axis=0)[:, 64:]


def solve_blocks(n, h):
    first = multiply(invert(h[0]), jnp.concatenate([h[1], h[2], n[0]], axis=1))
    change = multiply(jnp.concatenate([h[1], h[2]], axis=0), first)
    second = jnp.concatenate([h[2], h[3], n[1]], axis=1) - change[:64]
    third = jnp.concatenate([h[3], h[4], n[2]], axis=1) - change[64:]
    below = third[:, :64]
    second = multiply(invert(second[:, :64]), second[:, 64:])
    third = third[:, 64:] - multiply(below, second)
    y2 = multiply(invert(third[:, :64]), third[:, 64:])
    y1 = second[:, 64:] - multiply(second[:, :64], y2)
    y0 = first[:, 128:] - multiply(first[:, :64], y1) - multiply(first[:, 64:128], y2)
    return jnp.concatenate([y0, y1, y2], axis=0)


def finish_kernel(moments, v0, v1, v2, out):
    n = []
    for b in range(3):
        block = moments[64 * b : 64 * b + 64, :]
        other = jnp.transpose(jnp.concatenate([block, block], axis=0))
        n.append(0.5 * (block[:, :64] + other[:64, :64]))
        n.append(0.5 * (block[:, 64:] + other[64:, :64]))
    h = [n[m + 1] + SHIFT * n[m] for m in range(5)]
    solved = solve_blocks(n, h)
    weights = jnp.transpose(jnp.concatenate([solved, solved], axis=1))[64:]
    high, low = halves(weights)
    both = jnp.concatenate([high, low], axis=0)
    for c in range(3):
        for k in range(0, 8, 2):
            stack = jnp.concatenate([columns(v0, c, k + 1), columns(v1, c, k + 1), columns(v2, c, k)], axis=0)
            fine, rest = halves(stack)
            one = lax.dot_general(both, fine, NN, preferred_element_type=F32)
            two = lax.dot_general(high, rest, NN, preferred_element_type=F32)
            mixed = one[:64] + one[64:] + two
            for j in range(2):
                out[:, c, k + j] = mixed[:, LANES * j : LANES * j + LANES].reshape(8, 8, LANES)


def call(kernel, outs, scratch=(), n_in=1, flops=0, where=pltpu.VMEM, limit=48, far=False):
    single = not isinstance(outs, list)
    shapes = [outs] if single else outs
    vmem = pl.BlockSpec(memory_space=pltpu.VMEM)
    scratch = [pltpu.VMEM(a, F32) if isinstance(a, tuple) else a for a in scratch]
    done = pl.pallas_call(
        kernel,
        out_shape=[jax.ShapeDtypeStruct(s, F32) for s in shapes],
        in_specs=[pl.BlockSpec(memory_space=where)] * n_in,
        out_specs=[pl.BlockSpec(memory_space=pl.ANY) if far else vmem, *[vmem] * (len(shapes) - 1)],
        scratch_shapes=scratch,
        compiler_params=pltpu.CompilerParams(vmem_limit_bytes=limit * 1024 * 1024),
        cost_estimate=pl.CostEstimate(flops=flops, bytes_accessed=4 * 1024 * 1024, transcendentals=0),
    )
    return (lambda *a: done(*a)[0]) if single else done


def exchange(x, axis):
    return lax.all_to_all(x, axis, split_axis=0, concat_axis=0, tiled=True)


def reduce_bricks(parts):
    space, rx = (lax.axis_size("space"), lax.axis_size("rx"))
    rows = parts.shape[0]
    pieces = exchange(parts.reshape(space, rows // space, LANES), "space")
    own = jnp.sum(pieces, axis=0)
    pieces = exchange(jnp.broadcast_to(own[None], (rx, *own.shape)), "rx")
    own = jnp.sum(pieces, axis=0)
    pieces = exchange(jnp.broadcast_to(own[None], (space, *own.shape)), "space")
    return pieces.reshape(rows, LANES)


def body(lambda_next, class_ids, class_rate, coil_x, coil_y, coil_z, coil_amp):
    size = lax.axis_size("space")
    chips = [(i, i ^ 1) for i in range(size)]
    fall = [((i + 1) % size, i) for i in range(size)]
    beside = [pair for i in range(1, size, 2) for pair in ((i, (i + 1) % size), ((i + 1) % size, i))]
    arrays = (lambda_next, class_ids, class_rate, coil_x, coil_y, coil_z, coil_amp)
    spaces = [pltpu.VMEM] + [pltpu.SMEM] * 5
    outgoing, mass = call(
        enter_kernel,
        [(8, 8 * SENT, LANES), (GHOST, 8, LANES)],
        [(8, 3, 2, PLANE, LANES)]
        + [space(a.shape, a.dtype) for space, a in zip(spaces, arrays[1:], strict=True)]
        + [(13, LANES, LANES), (3, 67 * 8, LANES), (67 * 8, LANES)]
        + [pltpu.SemaphoreType.DMA((7,))],
        n_in=7,
        where=pl.ANY,
        limit=60,
    )(*arrays)
    v0 = exchange(outgoing, "rx").reshape(8, SENT, 8, LANES)
    message = (4, 2, 10, 8, LANES)
    outer = lax.ppermute(call(functools.partial(message_kernel, True), message)(v0), "space", beside)
    base, inner = call(functools.partial(base_kernel, 0), [(8, 3, 10, 8, LANES), message], n_in=2, flops=10**8)(v0, mass)
    inner = lax.ppermute(inner, "space", chips)
    v1, outer = call(second_kernel, [(8, 3, 10, 8, LANES), message], n_in=3)(outer, base, inner)
    outer = lax.ppermute(outer, "space", beside)
    base, inner = call(functools.partial(base_kernel, 1), [(8, 3, 9, 8, LANES), message], n_in=2, flops=10**8)(v1, mass)
    inner = lax.ppermute(inner, "space", chips)
    v2, down = call(third_kernel, [(8, 3, 9, 8, LANES), (4, 2, 8, 8, LANES)], n_in=3)(outer, base, inner)
    above = lax.ppermute(down, "space", fall)
    moments, curl = call(
        moments_kernel, [(192, LANES), (8, 2, 8, 8, LANES)], [(8, 1, 8, 8, LANES), (8, 3, 8, 8, LANES)], n_in=4, flops=10**8
    )(v0, v1, v2, mass)
    moments = call(energy_kernel, (192, LANES), n_in=3)(curl, above, moments)
    moments = reduce_bricks(moments)
    mixed = call(finish_kernel, (8, 3, 8, 8, LANES), n_in=4)(moments, v0, v1, v2)
    mixed = exchange(mixed, "rx")
    scratch = [(512, LANES), (LANES, LANES), (3, 8, 2, PLANE, LANES), pltpu.SemaphoreType.DMA((3,))]
    return call(leave_kernel, (8, 3, 2, PLANE, LANES), scratch, far=True)(mixed)


def solution(mesh):
    in_specs = (
        P("rx", None, "space", None, None),
        P("space", None, None),
        P(),
        P("rx"),
        P("rx"),
        P("rx"),
        P("rx"),
    )
    out_specs = P("rx", None, "space", None, None)
    return jax.shard_map(body, mesh=mesh, in_specs=in_specs, out_specs=out_specs, check_vma=False)
```

```python
import functools

import jax
import jax.numpy as jnp
from jax import lax
from jax.experimental import pallas as pl
from jax.experimental.pallas import tpu as pltpu
from jax.sharding import PartitionSpec as P

SHIFT = 6.0
LANES = 128
HALF = 64
PLANE = 32
GHOST = 11
SENT = 31
F32 = jnp.float32
BF16 = jnp.bfloat16
NT = (((1,), (1,)), ((), ()))
NN = (((1,), (0,)), ((), ()))


def lane_ids():
    lane = lax.broadcasted_iota(jnp.int32, (8, LANES), 1)
    return lane & 31, (lane >> 5) & 1, lane >> 6


def turn(a, shift):
    return pltpu.roll(a, shift, axis=a.ndim - 1)


def y_next(a):
    return jnp.where(lane_ids()[0] == 31, 0.0, turn(a, LANES - 1))


def y_prev(a):
    return jnp.where(lane_ids()[0] == 0, 0.0, turn(a, 1))


def z_both(a):
    half = turn(a, HALF)
    mixed = jnp.where(lane_ids()[2] == 0, half[:-1], half[1:])
    return jnp.concatenate([mixed, half[-1:]], axis=0), jnp.concatenate([half[:1], mixed], axis=0)


def x_next(a, beyond):
    return jnp.where(lane_ids()[1] == 0, turn(a, LANES - PLANE), beyond)


def x_prev(a, beyond):
    return jnp.where(lane_ids()[1] == 1, turn(a, PLANE), beyond)


def pack_up(a, b):
    return jnp.where(lane_ids()[1] == 1, a, turn(b, LANES - PLANE))


def pack_down(a, b):
    return jnp.where(lane_ids()[1] == 0, a, turn(b, PLANE))


def unpack(m, second, up):
    if not second:
        m = turn(m, LANES - PLANE) if up else turn(m, PLANE)
    return jnp.where(lane_ids()[1] == (0 if up else 1), m, 0.0)


def slopes(v):
    return v[1] + y_next(v[0]) - v[0], v[2] + z_both(v[0])[0] - v[0]


def apply_tiles(v, shifted):
    g1, g2 = slopes(v)
    e1 = v[1] - x_next(v[1], 0.0)
    e2 = v[2] - x_next(v[2], 0.0)
    q2 = z_both(v[2])[1] - v[2]
    q1 = y_prev(v[1]) - v[1]
    v1_next, v1_prev = z_both(v[1])
    r0 = 2.0 * v[0] + v[1] + v[2] - g1 - g2 + y_prev(e1 - v[0]) + z_both(e2 - v[0])[1] - e1 - e2
    r1 = g1 - x_prev(g1, 0.0) + e1 + 2.0 * v[1] - v1_next - v1_prev - y_next(q2) + q2
    r2 = g2 - x_prev(g2, 0.0) + e2 + 2.0 * v[2] - y_next(v[2]) - y_prev(v[2]) - z_both(q1)[0] + q1
    return [shifted * v[0] + r0, shifted * v[1] + r1, shifted * v[2] + r2]


def halves(a):
    high = a.astype(BF16)
    return high, (a - high.astype(F32)).astype(BF16)


def thirds(a):
    high = a.astype(BF16)
    rest = a - high.astype(F32)
    middle = rest.astype(BF16)
    return high, middle, (rest - middle.astype(F32)).astype(BF16)


def multiply(a, b):
    ah, am, al = thirds(a)
    bh, bm, bl = thirds(b)
    left = jnp.concatenate([ah, ah, am, am, ah, al], axis=1)
    right = jnp.concatenate([bh, bm, bh, bm, bl, bh], axis=0)
    return lax.dot_general(left, right, NN, preferred_element_type=F32)


def enter_kernel(*refs):
    (source, *sources), (out, mass_out), rest = refs[:7], refs[7:9], refs[9:]
    (field, *targets), (flipped, padded, mass_pad, loads) = rest[:7], rest[7:]
    copies = [pltpu.make_async_copy(a, b, loads.at[i]) for i, (a, b) in enumerate(zip(sources, targets, strict=True))]
    copies = [pltpu.make_async_copy(source, field, loads.at[6]), *copies]
    for copy in copies:
        copy.start()
    for copy in copies:
        copy.wait()
    ids, rate, coil_x, coil_y, coil_z, amp = targets
    lane = lax.broadcasted_iota(jnp.int32, (64, LANES), 1)
    row = lax.broadcasted_iota(jnp.int32, (64, LANES), 0)
    classes = ids[...].reshape(64, LANES)
    mass = jnp.zeros((64, LANES), F32)
    for k in range(rate.shape[0]):
        mass = jnp.where(classes == k, rate[k], mass)
    left = lane < HALF
    flipped[12] = jnp.transpose(jnp.concatenate([mass, mass], axis=0))
    rows = jnp.where(left, flipped[12, pl.ds(0, 64, stride=2), :], flipped[12, pl.ds(1, 64, stride=2), :])
    mass_pad[0:8, :] = jnp.zeros((8, LANES), F32)
    mass_pad[8 * 65 :, :] = jnp.zeros((16, LANES), F32)
    for r in range(8):
        mass_pad[pl.ds(8 + r, 64, stride=8), :] = rows
    first = pl.multiple_of(lax.axis_index("rx") * 64, 64)
    mass_out[...] = mass_pad[pl.ds(first, 8 * GHOST), :].reshape(GHOST, 8, LANES) - SHIFT
    base = lax.axis_index("space") * 2

    def right(r, c):
        values = mass * field[r, c].reshape(64, LANES)
        if c == 2:
            return values
        near = coil_x[r] - base
        far = near + 1
        spot = jnp.where((near >= 0) & (near < 2), near * 32 + coil_y[r], -100)
        if c == 0:
            plus, minus = spot, spot + 1
        else:
            plus, minus = jnp.where((far >= 0) & (far < 2), far * 32 + coil_y[r], -100), spot
        strength = jnp.where(row == plus, amp[r], jnp.where(row == minus, -amp[r], 0.0))
        return values + jnp.where(lane == coil_z[r], strength, 0.0)

    for c in range(3):
        padded[c, 0:8, :] = jnp.zeros((8, LANES), F32)
        padded[c, 8 * 65 :, :] = jnp.zeros((16, LANES), F32)
        for r in range(4):
            flipped[c * 4 + r] = jnp.transpose(jnp.concatenate([right(r, c), right(r + 4, c)], axis=0))
            even = flipped[c * 4 + r, pl.ds(0, 64, stride=2), :]
            odd = flipped[c * 4 + r, pl.ds(1, 64, stride=2), :]
            padded[c, pl.ds(8 + r, 64, stride=8), :] = jnp.where(left, even, turn(odd, HALF))
            padded[c, pl.ds(12 + r, 64, stride=8), :] = jnp.where(left, turn(even, HALF), odd)
        for d in range(8):
            out[d, 80 * c : 80 * c + 80] = padded[c, 64 * d : 64 * d + 80, :]
    for d in range(8):
        tiles = [padded[k, 64 * d + 80 : 64 * d + 88, :] for k in range(2)]
        out[d, 240:248] = jnp.where(left[:8], tiles[0], turn(tiles[1], HALF))


def first_fields(v0, s):
    last = v0[s, pl.ds(SENT - 1, 1)]
    ends = [last, turn(last, HALF), jnp.zeros((1, 8, LANES), F32)]
    return [jnp.concatenate([v0[s, 10 * c : 10 * c + 10], ends[c]], axis=0) for c in range(3)]


def fields_of(v, s):
    return first_fields(v, s) if v.shape[1] == SENT else [v[s, c] for c in range(3)]


def leave_kernel(tiles, out, gathered, flipped, result, sems):
    left = lax.broadcasted_iota(jnp.int32, (64, LANES), 1) < HALF
    sends = []
    for c in range(3):
        for s in range(8):
            gathered[64 * s : 64 * s + 64, :] = tiles[s, c].reshape(64, LANES)
        for r in range(4):
            one = gathered[pl.ds(r, 64, stride=8), :]
            two = gathered[pl.ds(r + 4, 64, stride=8), :]
            flipped[pl.ds(0, 64, stride=2), :] = jnp.where(left, one, turn(two, HALF))
            flipped[pl.ds(1, 64, stride=2), :] = jnp.where(left, turn(one, HALF), two)
            back = jnp.transpose(flipped[...])
            result[c, r] = back[:64].reshape(2, PLANE, LANES)
            result[c, r + 4] = back[64:].reshape(2, PLANE, LANES)
        sends.append(pltpu.make_async_copy(result.at[c], out.at[:, c], sems.at[c]))
        sends[c].start()
    for copy in sends:
        copy.wait()


def is_even():
    return lax.axis_index("space") % 2 == 0


def send(message, to_above, s, v, w):
    last = GHOST - 1

    @pl.when(to_above)
    def _():
        for c, (a, b) in enumerate(zip(slopes(v), slopes(w), strict=True)):
            message[s, c] = pack_up(a[:last], b[:last])

    @pl.when(jnp.logical_not(to_above))
    def _():
        for c in range(2):
            message[s, c] = pack_down(v[c + 1][:last], w[c + 1][:last])


def message_kernel(outer, v, message):
    def step(s, carry):
        fields = [fields_of(v, s + 4 * k) for k in range(2)]
        send(message, is_even() != outer, s, *fields)
        return carry

    lax.fori_loop(0, 4, step, 0)


def receive(inner, outer, s, c):
    even, index = is_even(), lax.axis_index("space")
    edge = (index == 0) | (index == lax.axis_size("space") - 1)
    near, far = inner[s, c], jnp.where(edge, 0.0, outer[s, c])
    return jnp.where(even, far, near), jnp.where(even, near, far)


def inside(values, first_tile, last_tile):
    index = lax.axis_index("rx")
    rows = values.shape[0]
    low = jnp.where(index == 0, 0.0, 1.0)
    high = jnp.where(index == lax.axis_size("rx") - 1, 0.0, 1.0)
    pieces = [values]
    if first_tile:
        pieces = [values[:1] * low, values[1:]]
    if last_tile:
        pieces = [*pieces[:-1], pieces[-1][:-1], pieces[-1][-1:] * high]
    return jnp.concatenate(pieces, axis=0) if rows else values


def base_kernel(first, v, mass, base, inner):
    def step(s, carry):
        fields = [fields_of(v, s + 4 * k) for k in range(2)]
        for k in range(2):
            result = apply_tiles(fields[k], mass[: fields[k][0].shape[0]])
            for c in range(3):
                base[s + 4 * k, c] = result[c][first : first + base.shape[2]]
        send(inner, is_even(), s, *fields)
        return carry

    lax.fori_loop(0, 4, step, 0)


def completed(base, inner, outer, s, k, first):
    below, above = zip(*(receive(inner, outer, s, c) for c in range(2)), strict=True)
    beyond = [unpack(a, k, False) for a in above]
    before = [unpack(a, k, True) for a in below]
    changes = [
        beyond[0] + beyond[1] - y_prev(beyond[0]) - z_both(beyond[1])[1],
        -beyond[0] - before[0],
        -beyond[1] - before[1],
    ]
    return [inside(base[s + 4 * k, c] + changes[c][first:], first == 0, True) for c in range(3)]


def second_kernel(outer, base, inner, v1, next_outer):
    def step(s, carry):
        fields = [completed(base, inner, outer, s, k, 0) for k in range(2)]
        for k in range(2):
            for c in range(3):
                v1[s + 4 * k, c] = fields[k][c]
        send(next_outer, jnp.logical_not(is_even()), s, *fields)
        return carry

    lax.fori_loop(0, 4, step, 0)


def third_kernel(outer, base, inner, v2, down):
    def step(s, carry):
        fields = [completed(base, inner, outer, s, k, 1) for k in range(2)]
        for k in range(2):
            for c in range(3):
                v2[s + 4 * k, c] = fields[k][c]
        for c in range(2):
            down[s, c] = pack_down(fields[0][c + 1][:8], fields[1][c + 1][:8])
        return carry

    lax.fori_loop(0, 4, step, 0)


def columns(ref, c, first):
    at = lambda k: ref[:, 10 * c + k] if ref.shape[1] == SENT else ref[:, c, k]
    return jnp.concatenate([at(first + k).reshape(64, LANES) for k in range(2)], axis=1)


def bend(parts):
    return lax.dot_general(parts[:128], parts, NT, preferred_element_type=F32)


def fold(bends):
    return bends[:64, :64] + 2.0 * (bends[:64, 64:128] + bends[:64, 128:]) + bends[64:, 64:128]


def moments_kernel(v0, v1, v2, mass, down, out, curl, inner, curl0, scaled):
    inner[...] = down[...]
    y, x, parity = lane_ids()
    first_x = jnp.where((x == 0) & (lax.axis_index("space") == 0), 1.0, 0.0)
    first_y = jnp.where(y == 0, 1.0, 0.0)
    tile = lax.broadcasted_iota(jnp.int32, (8, 8, LANES), 0)
    first_z = jnp.where((tile == 0) & (parity == 0) & (lax.axis_index("rx") == 0), 1.0, 0.0)
    own = mass[1:9]
    faces = [first_y + first_z, first_x + first_z, first_x + first_y]

    def step(s, carry):
        v = [v2[s, c] for c in range(3)]
        z1 = z_both(v[1])[0][:8]
        z0 = z_both(v[0])[0][:8]
        v = [a[:8] for a in v]
        curl0[s, 0] = y_next(v[2]) - v[2] - z1 + v[1]
        curl[s, 0] = z0 - v[0] - x_next(v[2], 0.0) + v[2]
        curl[s, 1] = x_next(v[1], 0.0) - v[1] - y_next(v[0]) + v[0]
        for c in range(3):
            scaled[s, c] = v[c] * (own + faces[c])
        return carry

    lax.fori_loop(0, 8, step, 0)
    bends = jnp.zeros((128, 192), F32)
    mixed = jnp.zeros((192, 192), F32)
    total = jnp.zeros((192, 576), F32)
    middles = jnp.zeros((192, 192), F32)
    for c in range(3):
        for k in range(0, 8, 2):
            stack = jnp.concatenate([columns(v0, c, k + 1), columns(v1, c, k + 1), columns(v2, c, k)], axis=0)
            parts = thirds(stack)
            total = total + lax.dot_general(
                parts[0], jnp.concatenate(parts, axis=0), NT, preferred_element_type=F32
            )
            middles = middles + lax.dot_general(parts[1], parts[1], NT, preferred_element_type=F32)
            wide = jnp.concatenate(thirds(columns(scaled, c, k)), axis=0)
            field = jnp.concatenate([a[128:] for a in parts], axis=0)
            mixed = mixed + lax.dot_general(wide, field, NT, preferred_element_type=F32)
            if c == 0:
                bends = bends + bend(jnp.concatenate(thirds(columns(curl0, c, k)), axis=0))
    main, cross = total[:, :192] + middles, total[:, 192:384] + total[:, 384:]
    last = fold(bends)
    for i, j in ((0, 0), (0, 1), (1, 0), (1, 1), (0, 2), (2, 0)):
        last = last + mixed[64 * i : 64 * i + 64, 64 * j : 64 * j + 64]

    def block(i, j):
        at = lambda m, p, q: m[64 * p : 64 * p + 64, 64 * q : 64 * q + 64]
        return at(main, i, j) + at(cross, i, j) + at(cross, j, i)

    out[0:64, :] = jnp.concatenate([block(0, 0), block(0, 1)], axis=1)
    out[64:128, :] = jnp.concatenate([block(1, 1), block(1, 2)], axis=1)
    out[128:192, :] = jnp.concatenate([block(2, 2), last], axis=1)


def energy_kernel(outer, curl, inner, moments, out):
    bends = jnp.zeros((128, 192), F32)
    even, edge = is_even(), lax.axis_index("space") == lax.axis_size("space") - 1
    for c in range(2):
        for k in range(0, 8, 2):
            rows = []
            for j in range(2):
                above = jnp.where(even, inner[:, 1 - c, k + j], jnp.where(edge, 0.0, outer[:, 1 - c, k + j]))
                beyond = jnp.concatenate([unpack(above, half, False) for half in range(2)], axis=0)
                bent = curl[:, c, k + j] - beyond if c == 0 else curl[:, c, k + j] + beyond
                rows.append(bent.reshape(64, LANES))
            bends = bends + bend(jnp.concatenate(thirds(jnp.concatenate(rows, axis=1)), axis=0))
    out[0:128, :] = moments[0:128, :]
    out[128:192, :] = moments[128:192, :] + jnp.concatenate([jnp.zeros((64, 64), F32), fold(bends)], axis=1)


def spread(a, lane):
    return jnp.broadcast_to(a[:, lane : lane + 1], (8, LANES))


def line(a, k):
    return jnp.broadcast_to(a[k : k + 1], (8, LANES))


def invert(matrix):
    unit = lax.broadcasted_iota(jnp.int32, (64, 64), 0) == lax.broadcasted_iota(jnp.int32, (64, 64), 1)
    both = jnp.concatenate([matrix, jnp.where(unit, 1.0, 0.0)], axis=1)
    tiles = [both[8 * i : 8 * i + 8] for i in range(8)]
    origin = list(tiles)
    sub = lax.broadcasted_iota(jnp.int32, (8, LANES), 0)
    lane = lax.broadcasted_iota(jnp.int32, (8, LANES), 1)
    zero = jnp.zeros((8, LANES), F32)
    for p in range(8):
        rows, first = tiles[p], 8 * p
        cols = [spread(rows, first + k) for k in range(8)]
        for k in range(8):
            floor = line(spread(origin[p], first + k), k) * 2e-7
            pivot = line(cols[k], k)
            inverse = jnp.where(pivot > floor, 1.0 / pivot, 0.0)
            own, hit = cols[k], sub == k
            for j in range(k + 1, 8):
                scaled = line(cols[j], k) * inverse
                cols[j] = jnp.where(hit, scaled, cols[j] - own * scaled)
            scaled = line(rows, k) * inverse
            rows = jnp.where(hit, scaled, rows - own * scaled)
        tiles[p] = rows
        inside_panel = (lane >= first) & (lane < first + 8)
        apart = [zero if i in (p, p + 1) else jnp.where(inside_panel, tiles[i], 0.0) for i in range(8)]
        placed = [rows if i == p else zero for i in range(8)]
        change = multiply(jnp.concatenate(apart, axis=0)[:, :64], jnp.concatenate(placed, axis=0))
        for i in range(8):
            if i == p + 1:
                f = [spread(tiles[i], first + k) * line(rows, k) for k in range(8)]
                tiles[i] = tiles[i] - (((f[0] + f[1]) + (f[2] + f[3])) + ((f[4] + f[5]) + (f[6] + f[7])))
            elif i != p:
                tiles[i] = tiles[i] - change[8 * i : 8 * i + 8]
    return jnp.concatenate(tiles, axis=0)[:, 64:]


def solve_blocks(n, h):
    first = multiply(invert(h[0]), jnp.concatenate([h[1], h[2], n[0]], axis=1))
    change = multiply(jnp.concatenate([h[1], h[2]], axis=0), first)
    second = jnp.concatenate([h[2], h[3], n[1]], axis=1) - change[:64]
    third = jnp.concatenate([h[3], h[4], n[2]], axis=1) - change[64:]
    below = third[:, :64]
    second = multiply(invert(second[:, :64]), second[:, 64:])
    third = third[:, 64:] - multiply(below, second)
    y2 = multiply(invert(third[:, :64]), third[:, 64:])
    y1 = second[:, 64:] - multiply(second[:, :64], y2)
    y0 = first[:, 128:] - multiply(first[:, :64], y1) - multiply(first[:, 64:128], y2)
    return jnp.concatenate([y0, y1, y2], axis=0)


def finish_kernel(moments, v0, v1, v2, out):
    n = []
    for b in range(3):
        block = moments[64 * b : 64 * b + 64, :]
        other = jnp.transpose(jnp.concatenate([block, block], axis=0))
        n.append(0.5 * (block[:, :64] + other[:64, :64]))
        n.append(0.5 * (block[:, 64:] + other[64:, :64]))
    h = [n[m + 1] + SHIFT * n[m] for m in range(5)]
    solved = solve_blocks(n, h)
    weights = jnp.transpose(jnp.concatenate([solved, solved], axis=1))[64:]
    high, low = halves(weights)
    both = jnp.concatenate([high, low], axis=0)
    for c in range(3):
        for k in range(0, 8, 2):
            stack = jnp.concatenate([columns(v0, c, k + 1), columns(v1, c, k + 1), columns(v2, c, k)], axis=0)
            fine, rest = halves(stack)
            one = lax.dot_general(both, fine, NN, preferred_element_type=F32)
            two = lax.dot_general(high, rest, NN, preferred_element_type=F32)
            mixed = one[:64] + one[64:] + two
            for j in range(2):
                out[:, c, k + j] = mixed[:, LANES * j : LANES * j + LANES].reshape(8, 8, LANES)


def call(kernel, outs, scratch=(), n_in=1, flops=0, where=pltpu.VMEM, limit=48, far=False):
    single = not isinstance(outs, list)
    shapes = [outs] if single else outs
    vmem = pl.BlockSpec(memory_space=pltpu.VMEM)
    scratch = [pltpu.VMEM(a, F32) if isinstance(a, tuple) else a for a in scratch]
    done = pl.pallas_call(
        kernel,
        out_shape=[jax.ShapeDtypeStruct(s, F32) for s in shapes],
        in_specs=[pl.BlockSpec(memory_space=where)] * n_in,
        out_specs=[pl.BlockSpec(memory_space=pl.ANY) if far else vmem, *[vmem] * (len(shapes) - 1)],
        scratch_shapes=scratch,
        compiler_params=pltpu.CompilerParams(vmem_limit_bytes=limit * 1024 * 1024),
        cost_estimate=pl.CostEstimate(flops=flops, bytes_accessed=4 * 1024 * 1024, transcendentals=0),
    )
    return (lambda *a: done(*a)[0]) if single else done


def exchange(x, axis):
    return lax.all_to_all(x, axis, split_axis=0, concat_axis=0, tiled=True)


def reduce_bricks(parts):
    space, rx = (lax.axis_size("space"), lax.axis_size("rx"))
    rows = parts.shape[0]
    pieces = exchange(parts.reshape(space, rows // space, LANES), "space")
    own = jnp.sum(pieces, axis=0)
    pieces = exchange(jnp.broadcast_to(own[None], (rx, *own.shape)), "rx")
    own = jnp.sum(pieces, axis=0)
    pieces = exchange(jnp.broadcast_to(own[None], (space, *own.shape)), "space")
    return pieces.reshape(rows, LANES)


def body(lambda_next, class_ids, class_rate, coil_x, coil_y, coil_z, coil_amp):
    size = lax.axis_size("space")
    chips = [(i, i ^ 1) for i in range(size)]
    depth = lax.axis_size("rx")
    beside = []
    for i in range(size):
        for z in range(depth):
            end = i in (0, size - 1)
            other = (i, z ^ 1) if end else (i + 1 if i % 2 else i - 1, z)
            beside.append((i * depth + z, other[0] * depth + other[1]))
    arrays = (lambda_next, class_ids, class_rate, coil_x, coil_y, coil_z, coil_amp)
    spaces = [pltpu.VMEM] + [pltpu.SMEM] * 5
    outgoing, mass = call(
        enter_kernel,
        [(8, 8 * SENT, LANES), (GHOST, 8, LANES)],
        [(8, 3, 2, PLANE, LANES)]
        + [space(a.shape, a.dtype) for space, a in zip(spaces, arrays[1:], strict=True)]
        + [(13, LANES, LANES), (3, 67 * 8, LANES), (67 * 8, LANES)]
        + [pltpu.SemaphoreType.DMA((7,))],
        n_in=7,
        where=pl.ANY,
        limit=60,
    )(*arrays)
    v0 = exchange(outgoing, "rx").reshape(8, SENT, 8, LANES)
    message = (4, 2, 10, 8, LANES)
    outer = lax.ppermute(call(functools.partial(message_kernel, True), message)(v0), ("space", "rx"), beside)
    base, inner = call(functools.partial(base_kernel, 0), [(8, 3, 10, 8, LANES), message], n_in=2, flops=10**8)(v0, mass)
    inner = lax.ppermute(inner, "space", chips)
    v1, outer = call(second_kernel, [(8, 3, 10, 8, LANES), message], n_in=3)(outer, base, inner)
    outer = lax.ppermute(outer, ("space", "rx"), beside)
    base, inner = call(functools.partial(base_kernel, 1), [(8, 3, 9, 8, LANES), message], n_in=2, flops=10**8)(v1, mass)
    inner = lax.ppermute(inner, "space", chips)
    v2, down = call(third_kernel, [(8, 3, 9, 8, LANES), (4, 2, 8, 8, LANES)], n_in=3)(outer, base, inner)
    outer = lax.ppermute(down, ("space", "rx"), beside)
    moments, curl, inner = call(
        moments_kernel,
        [(192, LANES), (8, 2, 8, 8, LANES), (4, 2, 8, 8, LANES)],
        [(8, 1, 8, 8, LANES), (8, 3, 8, 8, LANES)],
        n_in=5,
        flops=10**8,
    )(v0, v1, v2, mass, down)
    inner = lax.ppermute(inner, "space", chips)
    moments = call(energy_kernel, (192, LANES), n_in=4)(outer, curl, inner, moments)
    moments = reduce_bricks(moments)
    mixed = call(finish_kernel, (8, 3, 8, 8, LANES), n_in=4)(moments, v0, v1, v2)
    mixed = exchange(mixed, "rx")
    scratch = [(512, LANES), (LANES, LANES), (3, 8, 2, PLANE, LANES), pltpu.SemaphoreType.DMA((3,))]
    return call(leave_kernel, (8, 3, 2, PLANE, LANES), scratch, far=True)(mixed)


def solution(mesh):
    in_specs = (
        P("rx", None, "space", None, None),
        P("space", None, None),
        P(),
        P("rx"),
        P("rx"),
        P("rx"),
        P("rx"),
    )
    out_specs = P("rx", None, "space", None, None)
    return jax.shard_map(body, mesh=mesh, in_specs=in_specs, out_specs=out_specs, check_vma=False)
```

```python
import functools

import jax
import jax.numpy as jnp
from jax import lax
from jax.experimental import pallas as pl
from jax.experimental.pallas import tpu as pltpu
from jax.sharding import PartitionSpec as P

SHIFT = 6.0
LANES = 128
HALF = 64
PLANE = 32
GHOST = 11
SENT = 31
F32 = jnp.float32
BF16 = jnp.bfloat16
NT = (((1,), (1,)), ((), ()))
NN = (((1,), (0,)), ((), ()))


def lane_ids():
    lane = lax.broadcasted_iota(jnp.int32, (8, LANES), 1)
    return lane & 31, (lane >> 5) & 1, lane >> 6


def turn(a, shift):
    return pltpu.roll(a, shift, axis=a.ndim - 1)


def y_next(a):
    return jnp.where(lane_ids()[0] == 31, 0.0, turn(a, LANES - 1))


def y_prev(a):
    return jnp.where(lane_ids()[0] == 0, 0.0, turn(a, 1))


def z_both(a):
    half = turn(a, HALF)
    mixed = jnp.where(lane_ids()[2] == 0, half[:-1], half[1:])
    return jnp.concatenate([mixed, half[-1:]], axis=0), jnp.concatenate([half[:1], mixed], axis=0)


def x_next(a, beyond):
    return jnp.where(lane_ids()[1] == 0, turn(a, LANES - PLANE), beyond)


def x_prev(a, beyond):
    return jnp.where(lane_ids()[1] == 1, turn(a, PLANE), beyond)


def pack_up(a, b):
    return jnp.where(lane_ids()[1] == 1, a, turn(b, LANES - PLANE))


def pack_down(a, b):
    return jnp.where(lane_ids()[1] == 0, a, turn(b, PLANE))


def unpack(m, second, up):
    if not second:
        m = turn(m, LANES - PLANE) if up else turn(m, PLANE)
    return jnp.where(lane_ids()[1] == (0 if up else 1), m, 0.0)


def slopes(v):
    return v[1] + y_next(v[0]) - v[0], v[2] + z_both(v[0])[0] - v[0]


def apply_tiles(v, shifted):
    g1, g2 = slopes(v)
    e1 = v[1] - x_next(v[1], 0.0)
    e2 = v[2] - x_next(v[2], 0.0)
    q2 = z_both(v[2])[1] - v[2]
    q1 = y_prev(v[1]) - v[1]
    v1_next, v1_prev = z_both(v[1])
    r0 = 2.0 * v[0] + v[1] + v[2] - g1 - g2 + y_prev(e1 - v[0]) + z_both(e2 - v[0])[1] - e1 - e2
    r1 = g1 - x_prev(g1, 0.0) + e1 + 2.0 * v[1] - v1_next - v1_prev - y_next(q2) + q2
    r2 = g2 - x_prev(g2, 0.0) + e2 + 2.0 * v[2] - y_next(v[2]) - y_prev(v[2]) - z_both(q1)[0] + q1
    return [shifted * v[0] + r0, shifted * v[1] + r1, shifted * v[2] + r2]


def halves(a):
    high = a.astype(BF16)
    return high, (a - high.astype(F32)).astype(BF16)


def thirds(a):
    high = a.astype(BF16)
    rest = a - high.astype(F32)
    middle = rest.astype(BF16)
    return high, middle, (rest - middle.astype(F32)).astype(BF16)


def multiply(a, b):
    ah, am, al = thirds(a)
    bh, bm, bl = thirds(b)
    left = jnp.concatenate([ah, ah, am, am, ah, al], axis=1)
    right = jnp.concatenate([bh, bm, bh, bm, bl, bh], axis=0)
    return lax.dot_general(left, right, NN, preferred_element_type=F32)


def enter_kernel(*refs):
    (source, *sources), (out, mass_out), rest = refs[:7], refs[7:9], refs[9:]
    (field, *targets), (flipped, padded, mass_pad, loads) = rest[:7], rest[7:]
    copies = [pltpu.make_async_copy(a, b, loads.at[i]) for i, (a, b) in enumerate(zip(sources, targets, strict=True))]
    copies = [pltpu.make_async_copy(source, field, loads.at[6]), *copies]
    for copy in copies:
        copy.start()
    for copy in copies[1:]:
        copy.wait()
    ids, rate, coil_x, coil_y, coil_z, amp = targets
    lane = lax.broadcasted_iota(jnp.int32, (64, LANES), 1)
    row = lax.broadcasted_iota(jnp.int32, (64, LANES), 0)
    classes = ids[...].reshape(64, LANES)
    mass = jnp.zeros((64, LANES), F32)
    for k in range(rate.shape[0]):
        mass = jnp.where(classes == k, rate[k], mass)
    left = lane < HALF
    flipped[12] = jnp.transpose(jnp.concatenate([mass, mass], axis=0))
    rows = jnp.where(left, flipped[12, pl.ds(0, 64, stride=2), :], flipped[12, pl.ds(1, 64, stride=2), :])
    mass_pad[0:8, :] = jnp.zeros((8, LANES), F32)
    mass_pad[8 * 65 :, :] = jnp.zeros((16, LANES), F32)
    for r in range(8):
        mass_pad[pl.ds(8 + r, 64, stride=8), :] = rows
    first = pl.multiple_of(lax.axis_index("rx") * 64, 64)
    mass_out[...] = mass_pad[pl.ds(first, 8 * GHOST), :].reshape(GHOST, 8, LANES) - SHIFT
    base = lax.axis_index("space") * 2
    copies[0].wait()

    def right(r, c):
        values = mass * field[r, c].reshape(64, LANES)
        if c == 2:
            return values
        near = coil_x[r] - base
        far = near + 1
        spot = jnp.where((near >= 0) & (near < 2), near * 32 + coil_y[r], -100)
        if c == 0:
            plus, minus = spot, spot + 1
        else:
            plus, minus = jnp.where((far >= 0) & (far < 2), far * 32 + coil_y[r], -100), spot
        strength = jnp.where(row == plus, amp[r], jnp.where(row == minus, -amp[r], 0.0))
        return values + jnp.where(lane == coil_z[r], strength, 0.0)

    for c in range(3):
        padded[c, 0:8, :] = jnp.zeros((8, LANES), F32)
        padded[c, 8 * 65 :, :] = jnp.zeros((16, LANES), F32)
        for r in range(4):
            flipped[c * 4 + r] = jnp.transpose(jnp.concatenate([right(r, c), right(r + 4, c)], axis=0))
            even = flipped[c * 4 + r, pl.ds(0, 64, stride=2), :]
            odd = flipped[c * 4 + r, pl.ds(1, 64, stride=2), :]
            padded[c, pl.ds(8 + r, 64, stride=8), :] = jnp.where(left, even, turn(odd, HALF))
            padded[c, pl.ds(12 + r, 64, stride=8), :] = jnp.where(left, turn(even, HALF), odd)
        for d in range(8):
            out[d, 80 * c : 80 * c + 80] = padded[c, 64 * d : 64 * d + 80, :]
    for d in range(8):
        tiles = [padded[k, 64 * d + 80 : 64 * d + 88, :] for k in range(2)]
        out[d, 240:248] = jnp.where(left[:8], tiles[0], turn(tiles[1], HALF))


def first_fields(v0, s):
    last = v0[s, pl.ds(SENT - 1, 1)]
    ends = [last, turn(last, HALF), jnp.zeros((1, 8, LANES), F32)]
    return [jnp.concatenate([v0[s, 10 * c : 10 * c + 10], ends[c]], axis=0) for c in range(3)]


def fields_of(v, s):
    return first_fields(v, s) if v.shape[1] == SENT else [v[s, c] for c in range(3)]


def leave_kernel(tiles, out, gathered, flipped, result, sems):
    left = lax.broadcasted_iota(jnp.int32, (64, LANES), 1) < HALF
    sends = []
    for c in range(3):
        for s in range(8):
            gathered[64 * s : 64 * s + 64, :] = tiles[s, c].reshape(64, LANES)
        for r in range(4):
            one = gathered[pl.ds(r, 64, stride=8), :]
            two = gathered[pl.ds(r + 4, 64, stride=8), :]
            flipped[pl.ds(0, 64, stride=2), :] = jnp.where(left, one, turn(two, HALF))
            flipped[pl.ds(1, 64, stride=2), :] = jnp.where(left, turn(one, HALF), two)
            back = jnp.transpose(flipped[...])
            result[c, r] = back[:64].reshape(2, PLANE, LANES)
            result[c, r + 4] = back[64:].reshape(2, PLANE, LANES)
        sends.append(pltpu.make_async_copy(result.at[c], out.at[:, c], sems.at[c]))
        sends[c].start()
    for copy in sends:
        copy.wait()


def is_even():
    return lax.axis_index("space") % 2 == 0


def send(message, to_above, s, v, w):
    last = GHOST - 1

    @pl.when(to_above)
    def _():
        for c, (a, b) in enumerate(zip(slopes(v), slopes(w), strict=True)):
            message[s, c] = pack_up(a[:last], b[:last])

    @pl.when(jnp.logical_not(to_above))
    def _():
        for c in range(2):
            message[s, c] = pack_down(v[c + 1][:last], w[c + 1][:last])


def message_kernel(outer, v, message):
    def step(s, carry):
        fields = [fields_of(v, s + 4 * k) for k in range(2)]
        send(message, is_even() != outer, s, *fields)
        return carry

    lax.fori_loop(0, 4, step, 0)


def receive(inner, outer, s, c):
    even, index = is_even(), lax.axis_index("space")
    edge = (index == 0) | (index == lax.axis_size("space") - 1)
    near, far = inner[s, c], jnp.where(edge, 0.0, outer[s, c])
    return jnp.where(even, far, near), jnp.where(even, near, far)


def inside(values, first_tile, last_tile):
    index = lax.axis_index("rx")
    rows = values.shape[0]
    low = jnp.where(index == 0, 0.0, 1.0)
    high = jnp.where(index == lax.axis_size("rx") - 1, 0.0, 1.0)
    pieces = [values]
    if first_tile:
        pieces = [values[:1] * low, values[1:]]
    if last_tile:
        pieces = [*pieces[:-1], pieces[-1][:-1], pieces[-1][-1:] * high]
    return jnp.concatenate(pieces, axis=0) if rows else values


def base_kernel(first, v, mass, base, inner):
    def step(s, carry):
        fields = [fields_of(v, s + 4 * k) for k in range(2)]
        for k in range(2):
            result = apply_tiles(fields[k], mass[: fields[k][0].shape[0]])
            for c in range(3):
                base[s + 4 * k, c] = result[c][first : first + base.shape[2]]
        send(inner, is_even(), s, *fields)
        return carry

    lax.fori_loop(0, 4, step, 0)


def completed(base, inner, outer, s, k, first):
    below, above = zip(*(receive(inner, outer, s, c) for c in range(2)), strict=True)
    beyond = [unpack(a, k, False) for a in above]
    before = [unpack(a, k, True) for a in below]
    changes = [
        beyond[0] + beyond[1] - y_prev(beyond[0]) - z_both(beyond[1])[1],
        -beyond[0] - before[0],
        -beyond[1] - before[1],
    ]
    return [inside(base[s + 4 * k, c] + changes[c][first:], first == 0, True) for c in range(3)]


def second_kernel(outer, base, inner, v1, next_outer):
    def step(s, carry):
        fields = [completed(base, inner, outer, s, k, 0) for k in range(2)]
        for k in range(2):
            for c in range(3):
                v1[s + 4 * k, c] = fields[k][c]
        send(next_outer, jnp.logical_not(is_even()), s, *fields)
        return carry

    lax.fori_loop(0, 4, step, 0)


def third_kernel(outer, base, inner, v2, down):
    def step(s, carry):
        fields = [completed(base, inner, outer, s, k, 1) for k in range(2)]
        for k in range(2):
            for c in range(3):
                v2[s + 4 * k, c] = fields[k][c]
        for c in range(2):
            down[s, c] = pack_down(fields[0][c + 1][:8], fields[1][c + 1][:8])
        return carry

    lax.fori_loop(0, 4, step, 0)


def columns(ref, c, first):
    at = lambda k: ref[:, 10 * c + k] if ref.shape[1] == SENT else ref[:, c, k]
    return jnp.concatenate([at(first + k).reshape(64, LANES) for k in range(2)], axis=1)


SIX = ((0, 0), (0, 1), (1, 0), (1, 1), (0, 2), (2, 0))


def six(products):
    return sum(products[64 * i : 64 * i + 64, 64 * j : 64 * j + 64] for i, j in SIX)


def squares(tiles):
    parts = jnp.concatenate(thirds(tiles), axis=0)
    return lax.dot_general(parts, parts, NT, preferred_element_type=F32)


def square_ids():
    shape = (64, 64)
    return lax.broadcasted_iota(jnp.int32, shape, 0), lax.broadcasted_iota(jnp.int32, shape, 1)


def diagonal(a):
    row, column = square_ids()
    return jnp.sum(jnp.where(row == column, a, 0.0), axis=0, keepdims=True)


def moments_kernel(v0, v1, v2, mass, down, out, curl, inner, curl0, scaled):
    inner[...] = down[...]
    y, x, parity = lane_ids()
    first_x = jnp.where((x == 0) & (lax.axis_index("space") == 0), 1.0, 0.0)
    first_y = jnp.where(y == 0, 1.0, 0.0)
    tile = lax.broadcasted_iota(jnp.int32, (8, 8, LANES), 0)
    first_z = jnp.where((tile == 0) & (parity == 0) & (lax.axis_index("rx") == 0), 1.0, 0.0)
    own = mass[1:9]
    faces = [first_y + first_z, first_x + first_z, first_x + first_y]

    def step(s, carry):
        v = [v2[s, c] for c in range(3)]
        z1 = z_both(v[1])[0][:8]
        z0 = z_both(v[0])[0][:8]
        v = [a[:8] for a in v]
        curl0[s, 0] = y_next(v[2]) - v[2] - z1 + v[1]
        curl[s, 0] = z0 - v[0] - x_next(v[2], 0.0) + v[2]
        curl[s, 1] = x_next(v[1], 0.0) - v[1] - y_next(v[0]) + v[0]
        for c in range(3):
            scaled[s, c] = v[c] * (own + faces[c])
        return carry

    lax.fori_loop(0, 8, step, 0)
    bends = jnp.zeros((192, 192), F32)
    mixed = jnp.zeros((192, 192), F32)
    total = jnp.zeros((192, 576), F32)
    middles = jnp.zeros((192, 192), F32)
    for c in range(3):
        for k in range(0, 8, 2):
            stack = jnp.concatenate([columns(v0, c, k + 1), columns(v1, c, k + 1), columns(v2, c, k)], axis=0)
            parts = thirds(stack)
            total = total + lax.dot_general(
                parts[0], jnp.concatenate(parts, axis=0), NT, preferred_element_type=F32
            )
            middles = middles + lax.dot_general(parts[1], parts[1], NT, preferred_element_type=F32)
            wide = jnp.concatenate(thirds(columns(scaled, c, k)), axis=0)
            field = jnp.concatenate([a[128:] for a in parts], axis=0)
            mixed = mixed + lax.dot_general(wide, field, NT, preferred_element_type=F32)
            if c == 0:
                bends = bends + squares(columns(curl0, c, k))
    main, cross = total[:, :192] + middles, total[:, 192:384] + total[:, 384:]
    cross = cross + jnp.transpose(jnp.concatenate([cross, jnp.zeros((192, 64), F32)], axis=1))[:192, :]
    total = main + cross

    def block(i, j):
        return total[64 * i : 64 * i + 64, 64 * j : 64 * j + 64]

    n = [block(0, 0), block(0, 1), block(1, 1), block(1, 2), block(2, 2), six(bends) + six(mixed)]
    row, column = square_ids()
    packed = [jnp.where(row <= column, n[2 * i], n[2 * i + 1]) for i in range(3)]
    diagonals = jnp.concatenate([diagonal(n[1]), diagonal(n[3]), diagonal(n[5]), jnp.zeros((61, 64), F32)], axis=0)
    out[0:64, :] = jnp.concatenate(packed[:2], axis=1)
    out[64:128, :] = jnp.concatenate([packed[2], diagonals], axis=1)


def energy_kernel(outer, curl, inner, moments, out):
    bends = jnp.zeros((192, 192), F32)
    even, edge = is_even(), lax.axis_index("space") == lax.axis_size("space") - 1
    for c in range(2):
        for k in range(0, 8, 2):
            rows = []
            for j in range(2):
                above = jnp.where(even, inner[:, 1 - c, k + j], jnp.where(edge, 0.0, outer[:, 1 - c, k + j]))
                beyond = jnp.concatenate([unpack(above, half, False) for half in range(2)], axis=0)
                bent = curl[:, c, k + j] - beyond if c == 0 else curl[:, c, k + j] + beyond
                rows.append(bent.reshape(64, LANES))
            bends = bends + squares(jnp.concatenate(rows, axis=1))
    last = six(bends)
    row, column = square_ids()
    lower = jnp.where(row > column, last, 0.0)
    third = jnp.where(row == 2, diagonal(last), 0.0)
    out[0:64, :] = moments[0:64, :]
    out[64:128, :] = moments[64:128, :] + jnp.concatenate([lower, third], axis=1)


def spread(a, lane):
    return jnp.broadcast_to(a[:, lane : lane + 1], (8, LANES))


def line(a, k):
    return jnp.broadcast_to(a[k : k + 1], (8, LANES))


def invert(matrix, nothing):
    unit = lax.broadcasted_iota(jnp.int32, (64, 64), 0) == lax.broadcasted_iota(jnp.int32, (64, 64), 1)
    both = jnp.concatenate([matrix, jnp.where(unit, 1.0, 0.0)], axis=1)
    tiles = [both[8 * i : 8 * i + 8] for i in range(8)]
    sub = lax.broadcasted_iota(jnp.int32, (8, LANES), 0)
    lane = lax.broadcasted_iota(jnp.int32, (8, LANES), 1)
    zero = jnp.zeros((8, LANES), F32)
    own = [jnp.sum(jnp.where(lane == sub + 8 * p, tiles[p], 0.0), axis=1, keepdims=True) for p in range(8)]
    floors = [jnp.broadcast_to(a * 2e-7, (8, LANES)) + nothing for a in own]
    for p in range(8):
        rows, first = tiles[p], 8 * p
        cols = [spread(rows, first + k) + nothing for k in range(8)]
        for k in range(8):
            pivot = line(cols[k], k)
            inverse = jnp.where(pivot > line(floors[p], k), 1.0 / pivot, 0.0)
            own, hit = cols[k], sub == k
            for j in range(k + 1, 8):
                scaled = line(cols[j], k) * inverse
                cols[j] = jnp.where(hit, scaled, cols[j] - own * scaled)
            scaled = line(rows, k) * inverse
            rows = jnp.where(hit, scaled, rows - own * scaled)
        tiles[p] = rows
        inside_panel = (lane >= first) & (lane < first + 8)
        apart = [zero if i in (p, p + 1) else jnp.where(inside_panel, tiles[i], 0.0) for i in range(8)]
        placed = [rows if i == p else zero for i in range(8)]
        change = multiply(jnp.concatenate(apart, axis=0)[:, :64], jnp.concatenate(placed, axis=0))
        for i in range(8):
            if i == p + 1:
                f = [spread(tiles[i], first + k) * line(rows, k) for k in range(8)]
                tiles[i] = tiles[i] - (((f[0] + f[1]) + (f[2] + f[3])) + ((f[4] + f[5]) + (f[6] + f[7])))
            elif i != p:
                tiles[i] = tiles[i] - change[8 * i : 8 * i + 8]
    return jnp.concatenate(tiles, axis=0)[:, 64:]


def solve_blocks(n, h, nothing):
    first = multiply(invert(h[0], nothing), jnp.concatenate([h[1], h[2], n[0]], axis=1))
    change = multiply(jnp.concatenate([h[1], h[2]], axis=0), first)
    second = jnp.concatenate([h[2], h[3], n[1]], axis=1) - change[:64]
    third = jnp.concatenate([h[3], h[4], n[2]], axis=1) - change[64:]
    below = third[:, :64]
    second = multiply(invert(second[:, :64], nothing), second[:, 64:])
    third = third[:, 64:] - multiply(below, second)
    y2 = multiply(invert(third[:, :64], nothing), third[:, 64:])
    y1 = second[:, 64:] - multiply(second[:, :64], y2)
    y0 = first[:, 128:] - multiply(first[:, :64], y1) - multiply(first[:, 64:128], y2)
    return jnp.concatenate([y0, y1, y2], axis=0)


def finish_kernel(moments, v0, v1, v2, out, zeros):
    zeros[...] = jnp.zeros((8, LANES), F32)
    row, column = square_ids()
    one, two = moments[0:64, :], moments[64:128, :]
    turned = [jnp.transpose(jnp.concatenate([a, a], axis=0))[:, :64] for a in (one, two)]
    pairs = [(one[:, :64], turned[0][:64]), (one[:, 64:], turned[0][64:]), (two[:, :64], turned[1][:64])]
    n = []
    for i, (block, other) in enumerate(pairs):
        n.append(jnp.where(row <= column, block, other))
        n.append(jnp.where(row > column, block, jnp.where(row < column, other, two[i : i + 1, 64:])))
    h = [n[m + 1] + SHIFT * n[m] for m in range(5)]
    solved = solve_blocks(n, h, zeros[...])
    weights = jnp.transpose(jnp.concatenate([solved, solved], axis=1))[64:]
    high, low = halves(weights)
    both = jnp.concatenate([high, low], axis=0)
    for c in range(3):
        for k in range(0, 8, 2):
            stack = jnp.concatenate([columns(v0, c, k + 1), columns(v1, c, k + 1), columns(v2, c, k)], axis=0)
            fine, rest = halves(stack)
            one = lax.dot_general(both, fine, NN, preferred_element_type=F32)
            two = lax.dot_general(high, rest, NN, preferred_element_type=F32)
            mixed = one[:64] + one[64:] + two
            for j in range(2):
                out[:, c, k + j] = mixed[:, LANES * j : LANES * j + LANES].reshape(8, 8, LANES)


def call(kernel, outs, scratch=(), n_in=1, flops=0, where=pltpu.VMEM, limit=48, far=False):
    single = not isinstance(outs, list)
    shapes = [outs] if single else outs
    vmem = pl.BlockSpec(memory_space=pltpu.VMEM)
    scratch = [pltpu.VMEM(a, F32) if isinstance(a, tuple) else a for a in scratch]
    done = pl.pallas_call(
        kernel,
        out_shape=[jax.ShapeDtypeStruct(s, F32) for s in shapes],
        in_specs=[pl.BlockSpec(memory_space=where)] * n_in,
        out_specs=[pl.BlockSpec(memory_space=pl.ANY) if far else vmem, *[vmem] * (len(shapes) - 1)],
        scratch_shapes=scratch,
        compiler_params=pltpu.CompilerParams(vmem_limit_bytes=limit * 1024 * 1024),
        cost_estimate=pl.CostEstimate(flops=flops, bytes_accessed=4 * 1024 * 1024, transcendentals=0),
    )
    return (lambda *a: done(*a)[0]) if single else done


def exchange(x, axis):
    return lax.all_to_all(x, axis, split_axis=0, concat_axis=0, tiled=True)


def reduce_bricks(parts):
    space, rx = (lax.axis_size("space"), lax.axis_size("rx"))
    rows = parts.shape[0]
    pieces = exchange(parts.reshape(space, rows // space, LANES), "space")
    own = jnp.sum(pieces, axis=0)
    pieces = exchange(jnp.broadcast_to(own[None], (rx, *own.shape)), "rx")
    own = jnp.sum(pieces, axis=0)
    pieces = exchange(jnp.broadcast_to(own[None], (space, *own.shape)), "space")
    return pieces.reshape(rows, LANES)


def body(lambda_next, class_ids, class_rate, coil_x, coil_y, coil_z, coil_amp):
    size = lax.axis_size("space")
    chips = [(i, i ^ 1) for i in range(size)]
    depth = lax.axis_size("rx")
    beside = []
    for i in range(size):
        for z in range(depth):
            end = i in (0, size - 1)
            other = (i, z ^ 1) if end else (i + 1 if i % 2 else i - 1, z)
            beside.append((i * depth + z, other[0] * depth + other[1]))
    arrays = (lambda_next, class_ids, class_rate, coil_x, coil_y, coil_z, coil_amp)
    spaces = [pltpu.VMEM] + [pltpu.SMEM] * 5
    outgoing, mass = call(
        enter_kernel,
        [(8, 8 * SENT, LANES), (GHOST, 8, LANES)],
        [(8, 3, 2, PLANE, LANES)]
        + [space(a.shape, a.dtype) for space, a in zip(spaces, arrays[1:], strict=True)]
        + [(13, LANES, LANES), (3, 67 * 8, LANES), (67 * 8, LANES)]
        + [pltpu.SemaphoreType.DMA((7,))],
        n_in=7,
        where=pl.ANY,
        limit=60,
    )(*arrays)
    v0 = exchange(outgoing, "rx").reshape(8, SENT, 8, LANES)
    message = (4, 2, 10, 8, LANES)
    outer = lax.ppermute(call(functools.partial(message_kernel, True), message)(v0), ("space", "rx"), beside)
    base, inner = call(functools.partial(base_kernel, 0), [(8, 3, 10, 8, LANES), message], n_in=2, flops=10**8)(v0, mass)
    inner = lax.ppermute(inner, "space", chips)
    v1, outer = call(second_kernel, [(8, 3, 10, 8, LANES), message], n_in=3)(outer, base, inner)
    outer = lax.ppermute(outer, ("space", "rx"), beside)
    base, inner = call(functools.partial(base_kernel, 1), [(8, 3, 9, 8, LANES), message], n_in=2, flops=10**8)(v1, mass)
    inner = lax.ppermute(inner, "space", chips)
    v2, down = call(third_kernel, [(8, 3, 9, 8, LANES), (4, 2, 8, 8, LANES)], n_in=3)(outer, base, inner)
    outer = lax.ppermute(down, ("space", "rx"), beside)
    moments, curl, inner = call(
        moments_kernel,
        [(128, LANES), (8, 2, 8, 8, LANES), (4, 2, 8, 8, LANES)],
        [(8, 1, 8, 8, LANES), (8, 3, 8, 8, LANES)],
        n_in=5,
        flops=10**8,
    )(v0, v1, v2, mass, down)
    inner = lax.ppermute(inner, "space", chips)
    moments = call(energy_kernel, (128, LANES), n_in=4)(outer, curl, inner, moments)
    moments = reduce_bricks(moments)
    mixed = call(finish_kernel, (8, 3, 8, 8, LANES), [(8, LANES)], n_in=4)(moments, v0, v1, v2)
    mixed = exchange(mixed, "rx")
    scratch = [(512, LANES), (LANES, LANES), (3, 8, 2, PLANE, LANES), pltpu.SemaphoreType.DMA((3,))]
    return call(leave_kernel, (8, 3, 2, PLANE, LANES), scratch, far=True)(mixed)


def solution(mesh):
    in_specs = (
        P("rx", None, "space", None, None),
        P("space", None, None),
        P(),
        P("rx"),
        P("rx"),
        P("rx"),
        P("rx"),
    )
    out_specs = P("rx", None, "space", None, None)
    return jax.shard_map(body, mesh=mesh, in_specs=in_specs, out_specs=out_specs, check_vma=False)
```

```python
import functools

import jax
import jax.numpy as jnp
from jax import lax
from jax.experimental import pallas as pl
from jax.experimental.pallas import tpu as pltpu
from jax.sharding import PartitionSpec as P

SHIFT = 6.0
LANES = 128
HALF = 64
PLANE = 32
GHOST = 11
SENT = 31
F32 = jnp.float32
BF16 = jnp.bfloat16
NT = (((1,), (1,)), ((), ()))
NN = (((1,), (0,)), ((), ()))


def lane_ids():
    lane = lax.broadcasted_iota(jnp.int32, (8, LANES), 1)
    return lane & 31, (lane >> 5) & 1, lane >> 6


def turn(a, shift):
    return pltpu.roll(a, shift, axis=a.ndim - 1)


def y_next(a):
    return jnp.where(lane_ids()[0] == 31, 0.0, turn(a, LANES - 1))


def y_prev(a):
    return jnp.where(lane_ids()[0] == 0, 0.0, turn(a, 1))


def z_both(a):
    half = turn(a, HALF)
    mixed = jnp.where(lane_ids()[2] == 0, half[:-1], half[1:])
    return jnp.concatenate([mixed, half[-1:]], axis=0), jnp.concatenate([half[:1], mixed], axis=0)


def x_next(a, beyond):
    return jnp.where(lane_ids()[1] == 0, turn(a, LANES - PLANE), beyond)


def x_prev(a, beyond):
    return jnp.where(lane_ids()[1] == 1, turn(a, PLANE), beyond)


def pack_up(a, b):
    return jnp.where(lane_ids()[1] == 1, a, turn(b, LANES - PLANE))


def pack_down(a, b):
    return jnp.where(lane_ids()[1] == 0, a, turn(b, PLANE))


def unpack(m, second, up):
    if not second:
        m = turn(m, LANES - PLANE) if up else turn(m, PLANE)
    return jnp.where(lane_ids()[1] == (0 if up else 1), m, 0.0)


def slopes(v):
    return v[1] + y_next(v[0]) - v[0], v[2] + z_both(v[0])[0] - v[0]


def apply_tiles(v, shifted):
    g1, g2 = slopes(v)
    e1 = v[1] - x_next(v[1], 0.0)
    e2 = v[2] - x_next(v[2], 0.0)
    q2 = z_both(v[2])[1] - v[2]
    q1 = y_prev(v[1]) - v[1]
    v1_next, v1_prev = z_both(v[1])
    r0 = 2.0 * v[0] + v[1] + v[2] - g1 - g2 + y_prev(e1 - v[0]) + z_both(e2 - v[0])[1] - e1 - e2
    r1 = g1 - x_prev(g1, 0.0) + e1 + 2.0 * v[1] - v1_next - v1_prev - y_next(q2) + q2
    r2 = g2 - x_prev(g2, 0.0) + e2 + 2.0 * v[2] - y_next(v[2]) - y_prev(v[2]) - z_both(q1)[0] + q1
    return [shifted * v[0] + r0, shifted * v[1] + r1, shifted * v[2] + r2]


def halves(a):
    high = a.astype(BF16)
    return high, (a - high.astype(F32)).astype(BF16)


def thirds(a):
    high = a.astype(BF16)
    rest = a - high.astype(F32)
    middle = rest.astype(BF16)
    return high, middle, (rest - middle.astype(F32)).astype(BF16)


def multiply(a, b):
    ah, am, al = thirds(a)
    bh, bm, bl = thirds(b)
    left = jnp.concatenate([ah, ah, am, am, ah, al], axis=1)
    right = jnp.concatenate([bh, bm, bh, bm, bl, bh], axis=0)
    return lax.dot_general(left, right, NN, preferred_element_type=F32)


def enter_kernel(*refs):
    (source, *sources), (out, mass_out), rest = refs[:7], refs[7:9], refs[9:]
    (field, *targets), (flipped, padded, mass_pad, loads) = rest[:7], rest[7:]
    copies = [pltpu.make_async_copy(a, b, loads.at[i]) for i, (a, b) in enumerate(zip(sources, targets, strict=True))]
    copies = [pltpu.make_async_copy(source, field, loads.at[6]), *copies]
    for copy in copies:
        copy.start()
    for copy in copies[1:]:
        copy.wait()
    ids, rate, coil_x, coil_y, coil_z, amp = targets
    lane = lax.broadcasted_iota(jnp.int32, (64, LANES), 1)
    row = lax.broadcasted_iota(jnp.int32, (64, LANES), 0)
    classes = ids[...].reshape(64, LANES)
    mass = jnp.zeros((64, LANES), F32)
    for k in range(rate.shape[0]):
        mass = jnp.where(classes == k, rate[k], mass)
    left = lane < HALF
    flipped[12] = jnp.transpose(jnp.concatenate([mass, mass], axis=0))
    rows = jnp.where(left, flipped[12, pl.ds(0, 64, stride=2), :], flipped[12, pl.ds(1, 64, stride=2), :])
    mass_pad[0:8, :] = jnp.zeros((8, LANES), F32)
    mass_pad[8 * 65 :, :] = jnp.zeros((16, LANES), F32)
    for r in range(8):
        mass_pad[pl.ds(8 + r, 64, stride=8), :] = rows
    first = pl.multiple_of(lax.axis_index("rx") * 64, 64)
    mass_out[...] = mass_pad[pl.ds(first, 8 * GHOST), :].reshape(GHOST, 8, LANES) - SHIFT
    base = lax.axis_index("space") * 2
    copies[0].wait()

    def right(r, c):
        values = mass * field[r, c].reshape(64, LANES)
        if c == 2:
            return values
        near = coil_x[r] - base
        far = near + 1
        spot = jnp.where((near >= 0) & (near < 2), near * 32 + coil_y[r], -100)
        if c == 0:
            plus, minus = spot, spot + 1
        else:
            plus, minus = jnp.where((far >= 0) & (far < 2), far * 32 + coil_y[r], -100), spot
        strength = jnp.where(row == plus, amp[r], jnp.where(row == minus, -amp[r], 0.0))
        return values + jnp.where(lane == coil_z[r], strength, 0.0)

    for c in range(3):
        padded[c, 0:8, :] = jnp.zeros((8, LANES), F32)
        padded[c, 8 * 65 :, :] = jnp.zeros((16, LANES), F32)
        for r in range(4):
            flipped[c * 4 + r] = jnp.transpose(jnp.concatenate([right(r, c), right(r + 4, c)], axis=0))
            even = flipped[c * 4 + r, pl.ds(0, 64, stride=2), :]
            odd = flipped[c * 4 + r, pl.ds(1, 64, stride=2), :]
            padded[c, pl.ds(8 + r, 64, stride=8), :] = jnp.where(left, even, turn(odd, HALF))
            padded[c, pl.ds(12 + r, 64, stride=8), :] = jnp.where(left, turn(even, HALF), odd)
        for d in range(8):
            out[d, 80 * c : 80 * c + 80] = padded[c, 64 * d : 64 * d + 80, :]
    for d in range(8):
        tiles = [padded[k, 64 * d + 80 : 64 * d + 88, :] for k in range(2)]
        out[d, 240:248] = jnp.where(left[:8], tiles[0], turn(tiles[1], HALF))


def first_fields(v0, s):
    last = v0[s, pl.ds(SENT - 1, 1)]
    ends = [last, turn(last, HALF), jnp.zeros((1, 8, LANES), F32)]
    return [jnp.concatenate([v0[s, 10 * c : 10 * c + 10], ends[c]], axis=0) for c in range(3)]


def fields_of(v, s):
    return first_fields(v, s) if v.shape[1] == SENT else [v[s, c] for c in range(3)]


def leave_kernel(tiles, out, gathered, flipped, result, sems):
    left = lax.broadcasted_iota(jnp.int32, (64, LANES), 1) < HALF
    sends = []
    for c in range(3):
        for s in range(8):
            gathered[64 * s : 64 * s + 64, :] = tiles[s, c].reshape(64, LANES)
        for r in range(4):
            one = gathered[pl.ds(r, 64, stride=8), :]
            two = gathered[pl.ds(r + 4, 64, stride=8), :]
            flipped[pl.ds(0, 64, stride=2), :] = jnp.where(left, one, turn(two, HALF))
            flipped[pl.ds(1, 64, stride=2), :] = jnp.where(left, turn(one, HALF), two)
            back = jnp.transpose(flipped[...])
            result[c, r] = back[:64].reshape(2, PLANE, LANES)
            result[c, r + 4] = back[64:].reshape(2, PLANE, LANES)
        sends.append(pltpu.make_async_copy(result.at[c], out.at[:, c], sems.at[c]))
        sends[c].start()
    for copy in sends:
        copy.wait()


def is_even():
    return lax.axis_index("space") % 2 == 0


def send(message, to_above, s, v, w):
    last = GHOST - 1

    @pl.when(to_above)
    def _():
        for c, (a, b) in enumerate(zip(slopes(v), slopes(w), strict=True)):
            message[s, c] = pack_up(a[:last], b[:last])

    @pl.when(jnp.logical_not(to_above))
    def _():
        for c in range(2):
            message[s, c] = pack_down(v[c + 1][:last], w[c + 1][:last])


def message_kernel(outer, v, message):
    def step(s, carry):
        fields = [fields_of(v, s + 4 * k) for k in range(2)]
        send(message, is_even() != outer, s, *fields)
        return carry

    lax.fori_loop(0, 4, step, 0)


def receive(inner, outer, s, c):
    even, index = is_even(), lax.axis_index("space")
    edge = (index == 0) | (index == lax.axis_size("space") - 1)
    near, far = inner[s, c], jnp.where(edge, 0.0, outer[s, c])
    return jnp.where(even, far, near), jnp.where(even, near, far)


def inside(values, first_tile, last_tile):
    index = lax.axis_index("rx")
    rows = values.shape[0]
    low = jnp.where(index == 0, 0.0, 1.0)
    high = jnp.where(index == lax.axis_size("rx") - 1, 0.0, 1.0)
    pieces = [values]
    if first_tile:
        pieces = [values[:1] * low, values[1:]]
    if last_tile:
        pieces = [*pieces[:-1], pieces[-1][:-1], pieces[-1][-1:] * high]
    return jnp.concatenate(pieces, axis=0) if rows else values


def base_kernel(first, v, mass, base, inner):
    def step(s, carry):
        fields = [fields_of(v, s + 4 * k) for k in range(2)]
        for k in range(2):
            result = apply_tiles(fields[k], mass[: fields[k][0].shape[0]])
            for c in range(3):
                base[s + 4 * k, c] = result[c][first : first + base.shape[2]]
        send(inner, is_even(), s, *fields)
        return carry

    lax.fori_loop(0, 4, step, 0)


def completed(base, inner, outer, s, k, first):
    below, above = zip(*(receive(inner, outer, s, c) for c in range(2)), strict=True)
    beyond = [unpack(a, k, False) for a in above]
    before = [unpack(a, k, True) for a in below]
    changes = [
        beyond[0] + beyond[1] - y_prev(beyond[0]) - z_both(beyond[1])[1],
        -beyond[0] - before[0],
        -beyond[1] - before[1],
    ]
    return [inside(base[s + 4 * k, c] + changes[c][first:], first == 0, True) for c in range(3)]


def second_kernel(outer, base, inner, v1, next_outer):
    def step(s, carry):
        fields = [completed(base, inner, outer, s, k, 0) for k in range(2)]
        for k in range(2):
            for c in range(3):
                v1[s + 4 * k, c] = fields[k][c]
        send(next_outer, jnp.logical_not(is_even()), s, *fields)
        return carry

    lax.fori_loop(0, 4, step, 0)


def third_kernel(outer, base, inner, v2, down):
    def step(s, carry):
        fields = [completed(base, inner, outer, s, k, 1) for k in range(2)]
        for k in range(2):
            for c in range(3):
                v2[s + 4 * k, c] = fields[k][c]
        for c in range(2):
            down[s, c] = pack_down(fields[0][c + 1][:8], fields[1][c + 1][:8])
        return carry

    lax.fori_loop(0, 4, step, 0)


def columns(ref, c, first):
    at = lambda k: ref[:, 10 * c + k] if ref.shape[1] == SENT else ref[:, c, k]
    return jnp.concatenate([at(first + k).reshape(64, LANES) for k in range(2)], axis=1)


SIX = ((0, 0), (0, 1), (1, 0), (1, 1), (0, 2), (2, 0))


def six(products):
    return sum(products[64 * i : 64 * i + 64, 64 * j : 64 * j + 64] for i, j in SIX)


def squares(tiles):
    parts = jnp.concatenate(thirds(tiles), axis=0)
    return lax.dot_general(parts, parts, NT, preferred_element_type=F32)


def square_ids():
    shape = (64, 64)
    return lax.broadcasted_iota(jnp.int32, shape, 0), lax.broadcasted_iota(jnp.int32, shape, 1)


def diagonal(a):
    row, column = square_ids()
    return jnp.sum(jnp.where(row == column, a, 0.0), axis=0, keepdims=True)


def moments_kernel(v0, v1, v2, mass, out, curl, curl0, scaled):
    y, x, parity = lane_ids()
    first_x = jnp.where((x == 0) & (lax.axis_index("space") == 0), 1.0, 0.0)
    first_y = jnp.where(y == 0, 1.0, 0.0)
    tile = lax.broadcasted_iota(jnp.int32, (8, 8, LANES), 0)
    first_z = jnp.where((tile == 0) & (parity == 0) & (lax.axis_index("rx") == 0), 1.0, 0.0)
    own = mass[1:9]
    faces = [first_y + first_z, first_x + first_z, first_x + first_y]

    def step(s, carry):
        v = [v2[s, c] for c in range(3)]
        z1 = z_both(v[1])[0][:8]
        z0 = z_both(v[0])[0][:8]
        v = [a[:8] for a in v]
        curl0[s, 0] = y_next(v[2]) - v[2] - z1 + v[1]
        curl[s, 0] = z0 - v[0] - x_next(v[2], 0.0) + v[2]
        curl[s, 1] = x_next(v[1], 0.0) - v[1] - y_next(v[0]) + v[0]
        for c in range(3):
            scaled[s, c] = v[c] * (own + faces[c])
        return carry

    lax.fori_loop(0, 8, step, 0)
    bends = jnp.zeros((192, 192), F32)
    mixed = jnp.zeros((192, 192), F32)
    total = jnp.zeros((192, 576), F32)
    middles = jnp.zeros((192, 192), F32)
    for c in range(3):
        for k in range(0, 8, 2):
            stack = jnp.concatenate([columns(v0, c, k + 1), columns(v1, c, k + 1), columns(v2, c, k)], axis=0)
            parts = thirds(stack)
            total = total + lax.dot_general(
                parts[0], jnp.concatenate(parts, axis=0), NT, preferred_element_type=F32
            )
            middles = middles + lax.dot_general(parts[1], parts[1], NT, preferred_element_type=F32)
            wide = jnp.concatenate(thirds(columns(scaled, c, k)), axis=0)
            field = jnp.concatenate([a[128:] for a in parts], axis=0)
            mixed = mixed + lax.dot_general(wide, field, NT, preferred_element_type=F32)
            if c == 0:
                bends = bends + squares(columns(curl0, c, k))
    main, cross = total[:, :192] + middles, total[:, 192:384] + total[:, 384:]
    cross = cross + jnp.transpose(jnp.concatenate([cross, jnp.zeros((192, 64), F32)], axis=1))[:192, :]
    total = main + cross

    def block(i, j):
        return total[64 * i : 64 * i + 64, 64 * j : 64 * j + 64]

    n = [block(0, 0), block(0, 1), block(1, 1), block(1, 2), block(2, 2), six(bends) + six(mixed)]
    row, column = square_ids()
    packed = [jnp.where(row <= column, n[2 * i], n[2 * i + 1]) for i in range(3)]
    diagonals = jnp.concatenate([diagonal(n[1]), diagonal(n[3]), diagonal(n[5]), jnp.zeros((61, 64), F32)], axis=0)
    out[0:64, :] = jnp.concatenate(packed[:2], axis=1)
    out[64:128, :] = jnp.concatenate([packed[2], diagonals], axis=1)


def energy_kernel(curl, above, moments, out):
    bends = jnp.zeros((192, 192), F32)
    edge = lax.axis_index("space") == lax.axis_size("space") - 1
    for c in range(2):
        for k in range(0, 8, 2):
            rows = []
            for j in range(2):
                message = jnp.where(edge, 0.0, above[:, 1 - c, k + j])
                beyond = jnp.concatenate([unpack(message, half, False) for half in range(2)], axis=0)
                bent = curl[:, c, k + j] - beyond if c == 0 else curl[:, c, k + j] + beyond
                rows.append(bent.reshape(64, LANES))
            bends = bends + squares(jnp.concatenate(rows, axis=1))
    last = six(bends)
    row, column = square_ids()
    lower = jnp.where(row > column, last, 0.0)
    third = jnp.where(row == 2, diagonal(last), 0.0)
    out[0:64, :] = moments[0:64, :]
    out[64:128, :] = moments[64:128, :] + jnp.concatenate([lower, third], axis=1)


def spread(a, lane):
    return jnp.broadcast_to(a[:, lane : lane + 1], (8, LANES))


def line(a, k):
    return jnp.broadcast_to(a[k : k + 1], (8, LANES))


def invert(matrix, nothing):
    unit = lax.broadcasted_iota(jnp.int32, (64, 64), 0) == lax.broadcasted_iota(jnp.int32, (64, 64), 1)
    both = jnp.concatenate([matrix, jnp.where(unit, 1.0, 0.0)], axis=1)
    tiles = [both[8 * i : 8 * i + 8] for i in range(8)]
    sub = lax.broadcasted_iota(jnp.int32, (8, LANES), 0)
    lane = lax.broadcasted_iota(jnp.int32, (8, LANES), 1)
    zero = jnp.zeros((8, LANES), F32)
    own = [jnp.sum(jnp.where(lane == sub + 8 * p, tiles[p], 0.0), axis=1, keepdims=True) for p in range(8)]
    floors = [jnp.broadcast_to(a * 2e-7, (8, LANES)) + nothing for a in own]
    for p in range(8):
        rows, first = tiles[p], 8 * p
        cols = [spread(rows, first + k) + nothing for k in range(8)]
        for k in range(8):
            pivot = line(cols[k], k)
            inverse = jnp.where(pivot > line(floors[p], k), 1.0 / pivot, 0.0)
            own, hit = cols[k], sub == k
            for j in range(k + 1, 8):
                scaled = line(cols[j], k) * inverse
                cols[j] = jnp.where(hit, scaled, cols[j] - own * scaled)
            scaled = line(rows, k) * inverse
            rows = jnp.where(hit, scaled, rows - own * scaled)
        tiles[p] = rows
        inside_panel = (lane >= first) & (lane < first + 8)
        apart = [zero if i in (p, p + 1) else jnp.where(inside_panel, tiles[i], 0.0) for i in range(8)]
        placed = [rows if i == p else zero for i in range(8)]
        change = multiply(jnp.concatenate(apart, axis=0)[:, :64], jnp.concatenate(placed, axis=0))
        for i in range(8):
            if i == p + 1:
                f = [spread(tiles[i], first + k) * line(rows, k) for k in range(8)]
                tiles[i] = tiles[i] - (((f[0] + f[1]) + (f[2] + f[3])) + ((f[4] + f[5]) + (f[6] + f[7])))
            elif i != p:
                tiles[i] = tiles[i] - change[8 * i : 8 * i + 8]
    return jnp.concatenate(tiles, axis=0)[:, 64:]


def solve_blocks(n, h, nothing):
    first = multiply(invert(h[0], nothing), jnp.concatenate([h[1], h[2], n[0]], axis=1))
    change = multiply(jnp.concatenate([h[1], h[2]], axis=0), first)
    second = jnp.concatenate([h[2], h[3], n[1]], axis=1) - change[:64]
    third = jnp.concatenate([h[3], h[4], n[2]], axis=1) - change[64:]
    below = third[:, :64]
    second = multiply(invert(second[:, :64], nothing), second[:, 64:])
    third = third[:, 64:] - multiply(below, second)
    y2 = multiply(invert(third[:, :64], nothing), third[:, 64:])
    y1 = second[:, 64:] - multiply(second[:, :64], y2)
    y0 = first[:, 128:] - multiply(first[:, :64], y1) - multiply(first[:, 64:128], y2)
    return jnp.concatenate([y0, y1, y2], axis=0)


def finish_kernel(moments, v0, v1, v2, out, zeros):
    zeros[...] = jnp.zeros((8, LANES), F32)
    row, column = square_ids()
    one, two = moments[0:64, :], moments[64:128, :]
    turned = [jnp.transpose(jnp.concatenate([a, a], axis=0))[:, :64] for a in (one, two)]
    pairs = [(one[:, :64], turned[0][:64]), (one[:, 64:], turned[0][64:]), (two[:, :64], turned[1][:64])]
    n = []
    for i, (block, other) in enumerate(pairs):
        n.append(jnp.where(row <= column, block, other))
        n.append(jnp.where(row > column, block, jnp.where(row < column, other, two[i : i + 1, 64:])))
    h = [n[m + 1] + SHIFT * n[m] for m in range(5)]
    solved = solve_blocks(n, h, zeros[...])
    weights = jnp.transpose(jnp.concatenate([solved, solved], axis=1))[64:]
    high, low = halves(weights)
    both = jnp.concatenate([high, low], axis=0)
    for c in range(3):
        for k in range(0, 8, 2):
            stack = jnp.concatenate([columns(v0, c, k + 1), columns(v1, c, k + 1), columns(v2, c, k)], axis=0)
            fine, rest = halves(stack)
            one = lax.dot_general(both, fine, NN, preferred_element_type=F32)
            two = lax.dot_general(high, rest, NN, preferred_element_type=F32)
            mixed = one[:64] + one[64:] + two
            for j in range(2):
                out[:, c, k + j] = mixed[:, LANES * j : LANES * j + LANES].reshape(8, 8, LANES)


def call(kernel, outs, scratch=(), n_in=1, flops=0, where=pltpu.VMEM, limit=48, far=False):
    single = not isinstance(outs, list)
    shapes = [outs] if single else outs
    vmem = pl.BlockSpec(memory_space=pltpu.VMEM)
    scratch = [pltpu.VMEM(a, F32) if isinstance(a, tuple) else a for a in scratch]
    done = pl.pallas_call(
        kernel,
        out_shape=[jax.ShapeDtypeStruct(s, F32) for s in shapes],
        in_specs=[pl.BlockSpec(memory_space=where)] * n_in,
        out_specs=[pl.BlockSpec(memory_space=pl.ANY) if far else vmem, *[vmem] * (len(shapes) - 1)],
        scratch_shapes=scratch,
        compiler_params=pltpu.CompilerParams(vmem_limit_bytes=limit * 1024 * 1024),
        cost_estimate=pl.CostEstimate(flops=flops, bytes_accessed=4 * 1024 * 1024, transcendentals=0),
    )
    return (lambda *a: done(*a)[0]) if single else done


def exchange(x, axis):
    return lax.all_to_all(x, axis, split_axis=0, concat_axis=0, tiled=True)


def reduce_bricks(parts):
    space, rx = (lax.axis_size("space"), lax.axis_size("rx"))
    rows = parts.shape[0]
    pieces = exchange(parts.reshape(space, rows // space, LANES), "space")
    own = jnp.sum(pieces, axis=0)
    pieces = exchange(jnp.broadcast_to(own[None], (rx, *own.shape)), "rx")
    own = jnp.sum(pieces, axis=0)
    pieces = exchange(jnp.broadcast_to(own[None], (space, *own.shape)), "space")
    return pieces.reshape(rows, LANES)


def body(lambda_next, class_ids, class_rate, coil_x, coil_y, coil_z, coil_amp):
    size = lax.axis_size("space")
    chips = [(i, i ^ 1) for i in range(size)]
    depth = lax.axis_size("rx")
    beside = []
    for i in range(size):
        for z in range(depth):
            end = i in (0, size - 1)
            other = (i, z ^ 1) if end else (i + 1 if i % 2 else i - 1, z)
            beside.append((i * depth + z, other[0] * depth + other[1]))
    arrays = (lambda_next, class_ids, class_rate, coil_x, coil_y, coil_z, coil_amp)
    spaces = [pltpu.VMEM] + [pltpu.SMEM] * 5
    outgoing, mass = call(
        enter_kernel,
        [(8, 8 * SENT, LANES), (GHOST, 8, LANES)],
        [(8, 3, 2, PLANE, LANES)]
        + [space(a.shape, a.dtype) for space, a in zip(spaces, arrays[1:], strict=True)]
        + [(13, LANES, LANES), (3, 67 * 8, LANES), (67 * 8, LANES)]
        + [pltpu.SemaphoreType.DMA((7,))],
        n_in=7,
        where=pl.ANY,
        limit=60,
    )(*arrays)
    v0 = exchange(outgoing, "rx").reshape(8, SENT, 8, LANES)
    message = (4, 2, 10, 8, LANES)
    outer = lax.ppermute(call(functools.partial(message_kernel, True), message)(v0), ("space", "rx"), beside)
    base, inner = call(functools.partial(base_kernel, 0), [(8, 3, 10, 8, LANES), message], n_in=2, flops=10**8)(v0, mass)
    inner = lax.ppermute(inner, "space", chips)
    v1, outer = call(second_kernel, [(8, 3, 10, 8, LANES), message], n_in=3)(outer, base, inner)
    outer = lax.ppermute(outer, ("space", "rx"), beside)
    base, inner = call(functools.partial(base_kernel, 1), [(8, 3, 9, 8, LANES), message], n_in=2, flops=10**8)(v1, mass)
    inner = lax.ppermute(inner, "space", chips)
    v2, down = call(third_kernel, [(8, 3, 9, 8, LANES), (4, 2, 8, 8, LANES)], n_in=3)(outer, base, inner)
    above = lax.ppermute(down, "space", [((i + 1) % size, i) for i in range(size)])
    moments, curl = call(
        moments_kernel,
        [(128, LANES), (8, 2, 8, 8, LANES)],
        [(8, 1, 8, 8, LANES), (8, 3, 8, 8, LANES)],
        n_in=4,
        flops=10**8,
    )(v0, v1, v2, mass)
    moments = call(energy_kernel, (128, LANES), n_in=3)(curl, above, moments)
    moments = reduce_bricks(moments)
    mixed = call(finish_kernel, (8, 3, 8, 8, LANES), [(8, LANES)], n_in=4)(moments, v0, v1, v2)
    mixed = exchange(mixed, "rx")
    scratch = [(512, LANES), (LANES, LANES), (3, 8, 2, PLANE, LANES), pltpu.SemaphoreType.DMA((3,))]
    return call(leave_kernel, (8, 3, 2, PLANE, LANES), scratch, far=True)(mixed)


def solution(mesh):
    in_specs = (
        P("rx", None, "space", None, None),
        P("space", None, None),
        P(),
        P("rx"),
        P("rx"),
        P("rx"),
        P("rx"),
    )
    out_specs = P("rx", None, "space", None, None)
    return jax.shard_map(body, mesh=mesh, in_specs=in_specs, out_specs=out_specs, check_vma=False)
```

```python
import functools

import jax
import jax.numpy as jnp
from jax import lax
from jax.experimental import pallas as pl
from jax.experimental.pallas import tpu as pltpu
from jax.sharding import PartitionSpec as P

SHIFT = 6.0
LANES = 128
HALF = 64
PLANE = 32
GHOST = 11
SENT = 31
F32 = jnp.float32
BF16 = jnp.bfloat16
NT = (((1,), (1,)), ((), ()))
NN = (((1,), (0,)), ((), ()))


def lane_ids():
    lane = lax.broadcasted_iota(jnp.int32, (8, LANES), 1)
    return lane & 31, (lane >> 5) & 1, lane >> 6


def turn(a, shift):
    return pltpu.roll(a, shift, axis=a.ndim - 1)


def y_next(a):
    return jnp.where(lane_ids()[0] == 31, 0.0, turn(a, LANES - 1))


def y_prev(a):
    return jnp.where(lane_ids()[0] == 0, 0.0, turn(a, 1))


def z_both(a):
    half = turn(a, HALF)
    mixed = jnp.where(lane_ids()[2] == 0, half[:-1], half[1:])
    return jnp.concatenate([mixed, half[-1:]], axis=0), jnp.concatenate([half[:1], mixed], axis=0)


def x_next(a, beyond):
    return jnp.where(lane_ids()[1] == 0, turn(a, LANES - PLANE), beyond)


def x_prev(a, beyond):
    return jnp.where(lane_ids()[1] == 1, turn(a, PLANE), beyond)


def pack_up(a, b):
    return jnp.where(lane_ids()[1] == 1, a, turn(b, LANES - PLANE))


def pack_down(a, b):
    return jnp.where(lane_ids()[1] == 0, a, turn(b, PLANE))


def unpack(m, second, up):
    if not second:
        m = turn(m, LANES - PLANE) if up else turn(m, PLANE)
    return jnp.where(lane_ids()[1] == (0 if up else 1), m, 0.0)


def slopes(v):
    return v[1] + y_next(v[0]) - v[0], v[2] + z_both(v[0])[0] - v[0]


def apply_tiles(v, shifted):
    g1, g2 = slopes(v)
    e1 = v[1] - x_next(v[1], 0.0)
    e2 = v[2] - x_next(v[2], 0.0)
    q2 = z_both(v[2])[1] - v[2]
    q1 = y_prev(v[1]) - v[1]
    v1_next, v1_prev = z_both(v[1])
    r0 = 2.0 * v[0] + v[1] + v[2] - g1 - g2 + y_prev(e1 - v[0]) + z_both(e2 - v[0])[1] - e1 - e2
    r1 = g1 - x_prev(g1, 0.0) + e1 + 2.0 * v[1] - v1_next - v1_prev - y_next(q2) + q2
    r2 = g2 - x_prev(g2, 0.0) + e2 + 2.0 * v[2] - y_next(v[2]) - y_prev(v[2]) - z_both(q1)[0] + q1
    return [shifted * v[0] + r0, shifted * v[1] + r1, shifted * v[2] + r2]


def halves(a):
    high = a.astype(BF16)
    return high, (a - high.astype(F32)).astype(BF16)


def thirds(a):
    high = a.astype(BF16)
    rest = a - high.astype(F32)
    middle = rest.astype(BF16)
    return high, middle, (rest - middle.astype(F32)).astype(BF16)


def multiply(a, b):
    ah, am, al = thirds(a)
    bh, bm, bl = thirds(b)
    left = jnp.concatenate([ah, ah, am, am, ah, al], axis=1)
    right = jnp.concatenate([bh, bm, bh, bm, bl, bh], axis=0)
    return lax.dot_general(left, right, NN, preferred_element_type=F32)


def enter_kernel(*refs):
    (source, *sources), (out, mass_out), rest = refs[:7], refs[7:9], refs[9:]
    (field, *targets), (flipped, padded, mass_pad, loads) = rest[:7], rest[7:]
    copies = [pltpu.make_async_copy(a, b, loads.at[i]) for i, (a, b) in enumerate(zip(sources, targets, strict=True))]
    copies = [pltpu.make_async_copy(source, field, loads.at[6]), *copies]
    for copy in copies:
        copy.start()
    for copy in copies[1:]:
        copy.wait()
    ids, rate, coil_x, coil_y, coil_z, amp = targets
    lane = lax.broadcasted_iota(jnp.int32, (64, LANES), 1)
    row = lax.broadcasted_iota(jnp.int32, (64, LANES), 0)
    classes = ids[...].reshape(64, LANES)
    mass = jnp.zeros((64, LANES), F32)
    for k in range(rate.shape[0]):
        mass = jnp.where(classes == k, rate[k], mass)
    left = lane < HALF
    flipped[12] = jnp.transpose(jnp.concatenate([mass, mass], axis=0))
    rows = jnp.where(left, flipped[12, pl.ds(0, 64, stride=2), :], flipped[12, pl.ds(1, 64, stride=2), :])
    mass_pad[0:8, :] = jnp.zeros((8, LANES), F32)
    mass_pad[8 * 65 :, :] = jnp.zeros((16, LANES), F32)
    for r in range(8):
        mass_pad[pl.ds(8 + r, 64, stride=8), :] = rows
    first = pl.multiple_of(lax.axis_index("rx") * 64, 64)
    mass_out[...] = mass_pad[pl.ds(first, 8 * GHOST), :].reshape(GHOST, 8, LANES) - SHIFT
    base = lax.axis_index("space") * 2
    copies[0].wait()

    def right(r, c):
        values = mass * field[r, c].reshape(64, LANES)
        if c == 2:
            return values
        near = coil_x[r] - base
        far = near + 1
        spot = jnp.where((near >= 0) & (near < 2), near * 32 + coil_y[r], -100)
        if c == 0:
            plus, minus = spot, spot + 1
        else:
            plus, minus = jnp.where((far >= 0) & (far < 2), far * 32 + coil_y[r], -100), spot
        strength = jnp.where(row == plus, amp[r], jnp.where(row == minus, -amp[r], 0.0))
        return values + jnp.where(lane == coil_z[r], strength, 0.0)

    for c in range(3):
        padded[c, 0:8, :] = jnp.zeros((8, LANES), F32)
        padded[c, 8 * 65 :, :] = jnp.zeros((16, LANES), F32)
        for r in range(4):
            flipped[c * 4 + r] = jnp.transpose(jnp.concatenate([right(r, c), right(r + 4, c)], axis=0))
            even = flipped[c * 4 + r, pl.ds(0, 64, stride=2), :]
            odd = flipped[c * 4 + r, pl.ds(1, 64, stride=2), :]
            padded[c, pl.ds(8 + r, 64, stride=8), :] = jnp.where(left, even, turn(odd, HALF))
            padded[c, pl.ds(12 + r, 64, stride=8), :] = jnp.where(left, turn(even, HALF), odd)
        for d in range(8):
            out[d, 80 * c : 80 * c + 80] = padded[c, 64 * d : 64 * d + 80, :]
    for d in range(8):
        tiles = [padded[k, 64 * d + 80 : 64 * d + 88, :] for k in range(2)]
        out[d, 240:248] = jnp.where(left[:8], tiles[0], turn(tiles[1], HALF))


def first_fields(v0, s):
    last = v0[s, pl.ds(SENT - 1, 1)]
    ends = [last, turn(last, HALF), jnp.zeros((1, 8, LANES), F32)]
    return [jnp.concatenate([v0[s, 10 * c : 10 * c + 10], ends[c]], axis=0) for c in range(3)]


def fields_of(v, s):
    return first_fields(v, s) if v.shape[1] == SENT else [v[s, c] for c in range(3)]


def leave_kernel(tiles, out, gathered, flipped, result, sems):
    left = lax.broadcasted_iota(jnp.int32, (64, LANES), 1) < HALF
    sends = []
    for c in range(3):
        for s in range(8):
            gathered[64 * s : 64 * s + 64, :] = tiles[s, c].reshape(64, LANES)
        for r in range(4):
            one = gathered[pl.ds(r, 64, stride=8), :]
            two = gathered[pl.ds(r + 4, 64, stride=8), :]
            flipped[pl.ds(0, 64, stride=2), :] = jnp.where(left, one, turn(two, HALF))
            flipped[pl.ds(1, 64, stride=2), :] = jnp.where(left, turn(one, HALF), two)
            back = jnp.transpose(flipped[...])
            result[c, r] = back[:64].reshape(2, PLANE, LANES)
            result[c, r + 4] = back[64:].reshape(2, PLANE, LANES)
        sends.append(pltpu.make_async_copy(result.at[c], out.at[:, c], sems.at[c]))
        sends[c].start()
    for copy in sends:
        copy.wait()


def is_even():
    return lax.axis_index("space") % 2 == 0


def send(message, to_above, s, v, w):
    last = GHOST - 1

    @pl.when(to_above)
    def _():
        for c, (a, b) in enumerate(zip(slopes(v), slopes(w), strict=True)):
            message[s, c] = pack_up(a[:last], b[:last])

    @pl.when(jnp.logical_not(to_above))
    def _():
        for c in range(2):
            message[s, c] = pack_down(v[c + 1][:last], w[c + 1][:last])


def message_kernel(outer, v, message):
    def step(s, carry):
        fields = [fields_of(v, s + 4 * k) for k in range(2)]
        send(message, is_even() != outer, s, *fields)
        return carry

    lax.fori_loop(0, 4, step, 0)


def receive(inner, outer, s, c):
    even, index = is_even(), lax.axis_index("space")
    edge = (index == 0) | (index == lax.axis_size("space") - 1)
    near, far = inner[s, c], jnp.where(edge, 0.0, outer[s, c])
    return jnp.where(even, far, near), jnp.where(even, near, far)


def inside(values, first_tile, last_tile):
    index = lax.axis_index("rx")
    rows = values.shape[0]
    low = jnp.where(index == 0, 0.0, 1.0)
    high = jnp.where(index == lax.axis_size("rx") - 1, 0.0, 1.0)
    pieces = [values]
    if first_tile:
        pieces = [values[:1] * low, values[1:]]
    if last_tile:
        pieces = [*pieces[:-1], pieces[-1][:-1], pieces[-1][-1:] * high]
    return jnp.concatenate(pieces, axis=0) if rows else values


def base_kernel(v, mass, base, inner):
    def step(s, carry):
        fields = [fields_of(v, s + 4 * k) for k in range(2)]
        for k in range(2):
            result = apply_tiles(fields[k], mass[...])
            for c in range(3):
                base[s + 4 * k, c] = result[c][: base.shape[2]]
        send(inner, is_even(), s, *fields)
        return carry

    lax.fori_loop(0, 4, step, 0)


def completed(base, inner, outer, s, k, first):
    below, above = zip(*(receive(inner, outer, s, c) for c in range(2)), strict=True)
    beyond = [unpack(a, k, False) for a in above]
    before = [unpack(a, k, True) for a in below]
    changes = [
        beyond[0] + beyond[1] - y_prev(beyond[0]) - z_both(beyond[1])[1],
        -beyond[0] - before[0],
        -beyond[1] - before[1],
    ]
    return [inside(base[s + 4 * k, c] + changes[c][first:], first == 0, True) for c in range(3)]


def at_first(base, inner, outer, s, c, k):
    return base[s + 4 * k, c + 1] - unpack(receive(inner, outer, s, c)[0], k, True)[10 - base.shape[2] :]


def outer_kernel(outer, base, inner, message):
    def step(s, carry):
        @pl.when(is_even())
        def _():
            for c in range(2):
                parts = [inside(at_first(base, inner, outer, s, c, k), True, True) for k in range(2)]
                message[s, c] = pack_down(*parts)

        @pl.when(jnp.logical_not(is_even()))
        def _():
            send(message, True, s, *[completed(base, inner, outer, s, k, 0) for k in range(2)])

        return carry

    lax.fori_loop(0, 4, step, 0)


def second_kernel(outer, base, inner, mass, v1, next_base, next_inner):
    def step(s, carry):
        fields = [completed(base, inner, outer, s, k, 0) for k in range(2)]
        for k in range(2):
            result = apply_tiles(fields[k], mass[:10])
            for c in range(3):
                v1[s + 4 * k, c] = fields[k][c]
                next_base[s + 4 * k, c] = result[c][1:]
        send(next_inner, is_even(), s, *fields)
        return carry

    lax.fori_loop(0, 4, step, 0)


def down_kernel(outer, base, inner, down):
    def step(s, carry):
        for c in range(2):
            down[s, c] = pack_down(*[at_first(base, inner, outer, s, c, k)[:8] for k in range(2)])
        return carry

    lax.fori_loop(0, 4, step, 0)


def columns(ref, c, first):
    at = lambda k: ref[:, 10 * c + k] if ref.shape[1] == SENT else ref[:, c, k]
    return jnp.concatenate([at(first + k).reshape(64, LANES) for k in range(2)], axis=1)


SIX = ((0, 0), (0, 1), (1, 0), (1, 1), (0, 2), (2, 0))


def six(products):
    return sum(products[64 * i : 64 * i + 64, 64 * j : 64 * j + 64] for i, j in SIX)


def squares(tiles):
    parts = jnp.concatenate(thirds(tiles), axis=0)
    return lax.dot_general(parts, parts, NT, preferred_element_type=F32)


def square_ids():
    shape = (64, 64)
    return lax.broadcasted_iota(jnp.int32, shape, 0), lax.broadcasted_iota(jnp.int32, shape, 1)


def diagonal(a):
    row, column = square_ids()
    return jnp.sum(jnp.where(row == column, a, 0.0), axis=0, keepdims=True)


def moments_kernel(outer, base, inner, v0, v1, mass, out, curl, v2, curl0, scaled):
    y, x, parity = lane_ids()
    first_x = jnp.where((x == 0) & (lax.axis_index("space") == 0), 1.0, 0.0)
    first_y = jnp.where(y == 0, 1.0, 0.0)
    tile = lax.broadcasted_iota(jnp.int32, (8, 8, LANES), 0)
    first_z = jnp.where((tile == 0) & (parity == 0) & (lax.axis_index("rx") == 0), 1.0, 0.0)
    own = mass[1:9]
    faces = [first_y + first_z, first_x + first_z, first_x + first_y]

    def step(s, carry):
        for k in range(2):
            v, at = completed(base, inner, outer, s, k, 1), s + 4 * k
            for c in range(3):
                v2[at, c] = v[c]
            z1 = z_both(v[1])[0][:8]
            z0 = z_both(v[0])[0][:8]
            v = [a[:8] for a in v]
            curl0[at, 0] = y_next(v[2]) - v[2] - z1 + v[1]
            curl[at, 0] = z0 - v[0] - x_next(v[2], 0.0) + v[2]
            curl[at, 1] = x_next(v[1], 0.0) - v[1] - y_next(v[0]) + v[0]
            for c in range(3):
                scaled[at, c] = v[c] * (own + faces[c])
        return carry

    lax.fori_loop(0, 4, step, 0)
    bends = jnp.zeros((192, 192), F32)
    mixed = jnp.zeros((192, 192), F32)
    total = jnp.zeros((192, 576), F32)
    middles = jnp.zeros((192, 192), F32)
    for c in range(3):
        for k in range(0, 8, 2):
            stack = jnp.concatenate([columns(v0, c, k + 1), columns(v1, c, k + 1), columns(v2, c, k)], axis=0)
            parts = thirds(stack)
            total = total + lax.dot_general(
                parts[0], jnp.concatenate(parts, axis=0), NT, preferred_element_type=F32
            )
            middles = middles + lax.dot_general(parts[1], parts[1], NT, preferred_element_type=F32)
            wide = jnp.concatenate(thirds(columns(scaled, c, k)), axis=0)
            field = jnp.concatenate([a[128:] for a in parts], axis=0)
            mixed = mixed + lax.dot_general(wide, field, NT, preferred_element_type=F32)
            if c == 0:
                bends = bends + squares(columns(curl0, c, k))
    main, cross = total[:, :192] + middles, total[:, 192:384] + total[:, 384:]
    cross = cross + jnp.transpose(jnp.concatenate([cross, jnp.zeros((192, 64), F32)], axis=1))[:192, :]
    total = main + cross

    def block(i, j):
        return total[64 * i : 64 * i + 64, 64 * j : 64 * j + 64]

    n = [block(0, 0), block(0, 1), block(1, 1), block(1, 2), block(2, 2), six(bends) + six(mixed)]
    row, column = square_ids()
    packed = [jnp.where(row <= column, n[2 * i], n[2 * i + 1]) for i in range(3)]
    diagonals = jnp.concatenate([diagonal(n[1]), diagonal(n[3]), diagonal(n[5]), jnp.zeros((61, 64), F32)], axis=0)
    out[0:64, :] = jnp.concatenate(packed[:2], axis=1)
    out[64:128, :] = jnp.concatenate([packed[2], diagonals], axis=1)


def energy_kernel(curl, above, moments, out):
    bends = jnp.zeros((192, 192), F32)
    edge = lax.axis_index("space") == lax.axis_size("space") - 1
    for c in range(2):
        for k in range(0, 8, 2):
            rows = []
            for j in range(2):
                message = jnp.where(edge, 0.0, above[:, 1 - c, k + j])
                beyond = jnp.concatenate([unpack(message, half, False) for half in range(2)], axis=0)
                bent = curl[:, c, k + j] - beyond if c == 0 else curl[:, c, k + j] + beyond
                rows.append(bent.reshape(64, LANES))
            bends = bends + squares(jnp.concatenate(rows, axis=1))
    last = six(bends)
    row, column = square_ids()
    lower = jnp.where(row > column, last, 0.0)
    third = jnp.where(row == 2, diagonal(last), 0.0)
    out[0:64, :] = moments[0:64, :]
    out[64:128, :] = moments[64:128, :] + jnp.concatenate([lower, third], axis=1)


def spread(a, lane):
    return jnp.broadcast_to(a[:, lane : lane + 1], (8, LANES))


def line(a, k):
    return jnp.broadcast_to(a[k : k + 1], (8, LANES))


def invert(matrix, nothing):
    unit = lax.broadcasted_iota(jnp.int32, (64, 64), 0) == lax.broadcasted_iota(jnp.int32, (64, 64), 1)
    both = jnp.concatenate([matrix, jnp.where(unit, 1.0, 0.0)], axis=1)
    tiles = [both[8 * i : 8 * i + 8] for i in range(8)]
    sub = lax.broadcasted_iota(jnp.int32, (8, LANES), 0)
    lane = lax.broadcasted_iota(jnp.int32, (8, LANES), 1)
    zero = jnp.zeros((8, LANES), F32)
    own = [jnp.sum(jnp.where(lane == sub + 8 * p, tiles[p], 0.0), axis=1, keepdims=True) for p in range(8)]
    floors = [jnp.broadcast_to(a * 2e-7, (8, LANES)) + nothing for a in own]
    for p in range(8):
        rows, first = tiles[p], 8 * p
        cols = [spread(rows, first + k) + nothing for k in range(8)]
        for k in range(8):
            pivot = line(cols[k], k)
            inverse = jnp.where(pivot > line(floors[p], k), 1.0 / pivot, 0.0)
            own, hit = cols[k], sub == k
            for j in range(k + 1, 8):
                scaled = line(cols[j], k) * inverse
                cols[j] = jnp.where(hit, scaled, cols[j] - own * scaled)
            scaled = line(rows, k) * inverse
            rows = jnp.where(hit, scaled, rows - own * scaled)
        tiles[p] = rows
        inside_panel = (lane >= first) & (lane < first + 8)
        apart = [zero if i in (p, p + 1) else jnp.where(inside_panel, tiles[i], 0.0) for i in range(8)]
        placed = [rows if i == p else zero for i in range(8)]
        change = multiply(jnp.concatenate(apart, axis=0)[:, :64], jnp.concatenate(placed, axis=0))
        for i in range(8):
            if i == p + 1:
                f = [spread(tiles[i], first + k) * line(rows, k) for k in range(8)]
                tiles[i] = tiles[i] - (((f[0] + f[1]) + (f[2] + f[3])) + ((f[4] + f[5]) + (f[6] + f[7])))
            elif i != p:
                tiles[i] = tiles[i] - change[8 * i : 8 * i + 8]
    return jnp.concatenate(tiles, axis=0)[:, 64:]


def solve_blocks(n, h, nothing):
    first = multiply(invert(h[0], nothing), jnp.concatenate([h[1], h[2], n[0]], axis=1))
    change = multiply(jnp.concatenate([h[1], h[2]], axis=0), first)
    second = jnp.concatenate([h[2], h[3], n[1]], axis=1) - change[:64]
    third = jnp.concatenate([h[3], h[4], n[2]], axis=1) - change[64:]
    below = third[:, :64]
    second = multiply(invert(second[:, :64], nothing), second[:, 64:])
    third = third[:, 64:] - multiply(below, second)
    y2 = multiply(invert(third[:, :64], nothing), third[:, 64:])
    y1 = second[:, 64:] - multiply(second[:, :64], y2)
    y0 = first[:, 128:] - multiply(first[:, :64], y1) - multiply(first[:, 64:128], y2)
    return jnp.concatenate([y0, y1, y2], axis=0)


def finish_kernel(moments, v0, v1, v2, out, zeros):
    zeros[...] = jnp.zeros((8, LANES), F32)
    row, column = square_ids()
    one, two = moments[0:64, :], moments[64:128, :]
    turned = [jnp.transpose(jnp.concatenate([a, a], axis=0))[:, :64] for a in (one, two)]
    pairs = [(one[:, :64], turned[0][:64]), (one[:, 64:], turned[0][64:]), (two[:, :64], turned[1][:64])]
    n = []
    for i, (block, other) in enumerate(pairs):
        n.append(jnp.where(row <= column, block, other))
        n.append(jnp.where(row > column, block, jnp.where(row < column, other, two[i : i + 1, 64:])))
    h = [n[m + 1] + SHIFT * n[m] for m in range(5)]
    solved = solve_blocks(n, h, zeros[...])
    weights = jnp.transpose(jnp.concatenate([solved, solved], axis=1))[64:]
    high, low = halves(weights)
    both = jnp.concatenate([high, low], axis=0)
    for c in range(3):
        for k in range(0, 8, 2):
            stack = jnp.concatenate([columns(v0, c, k + 1), columns(v1, c, k + 1), columns(v2, c, k)], axis=0)
            fine, rest = halves(stack)
            one = lax.dot_general(both, fine, NN, preferred_element_type=F32)
            two = lax.dot_general(high, rest, NN, preferred_element_type=F32)
            mixed = one[:64] + one[64:] + two
            for j in range(2):
                out[:, c, k + j] = mixed[:, LANES * j : LANES * j + LANES].reshape(8, 8, LANES)


def call(kernel, outs, scratch=(), n_in=1, flops=0, where=pltpu.VMEM, limit=48, far=False):
    single = not isinstance(outs, list)
    shapes = [outs] if single else outs
    vmem = pl.BlockSpec(memory_space=pltpu.VMEM)
    scratch = [pltpu.VMEM(a, F32) if isinstance(a, tuple) else a for a in scratch]
    done = pl.pallas_call(
        kernel,
        out_shape=[jax.ShapeDtypeStruct(s, F32) for s in shapes],
        in_specs=[pl.BlockSpec(memory_space=where)] * n_in,
        out_specs=[pl.BlockSpec(memory_space=pl.ANY) if far else vmem, *[vmem] * (len(shapes) - 1)],
        scratch_shapes=scratch,
        compiler_params=pltpu.CompilerParams(vmem_limit_bytes=limit * 1024 * 1024),
        cost_estimate=pl.CostEstimate(flops=flops, bytes_accessed=4 * 1024 * 1024, transcendentals=0),
    )
    return (lambda *a: done(*a)[0]) if single else done


def exchange(x, axis):
    return lax.all_to_all(x, axis, split_axis=0, concat_axis=0, tiled=True)


def reduce_bricks(parts):
    space, rx = (lax.axis_size("space"), lax.axis_size("rx"))
    rows = parts.shape[0]
    pieces = exchange(parts.reshape(space, rows // space, LANES), "space")
    own = jnp.sum(pieces, axis=0)
    pieces = exchange(jnp.broadcast_to(own[None], (rx, *own.shape)), "rx")
    own = jnp.sum(pieces, axis=0)
    pieces = exchange(jnp.broadcast_to(own[None], (space, *own.shape)), "space")
    return pieces.reshape(rows, LANES)


def body(lambda_next, class_ids, class_rate, coil_x, coil_y, coil_z, coil_amp):
    size = lax.axis_size("space")
    chips = [(i, i ^ 1) for i in range(size)]
    depth = lax.axis_size("rx")
    beside = []
    for i in range(size):
        for z in range(depth):
            end = i in (0, size - 1)
            other = (i, z ^ 1) if end else (i + 1 if i % 2 else i - 1, z)
            beside.append((i * depth + z, other[0] * depth + other[1]))
    arrays = (lambda_next, class_ids, class_rate, coil_x, coil_y, coil_z, coil_amp)
    spaces = [pltpu.VMEM] + [pltpu.SMEM] * 5
    outgoing, mass = call(
        enter_kernel,
        [(8, 8 * SENT, LANES), (GHOST, 8, LANES)],
        [(8, 3, 2, PLANE, LANES)]
        + [space(a.shape, a.dtype) for space, a in zip(spaces, arrays[1:], strict=True)]
        + [(13, LANES, LANES), (3, 67 * 8, LANES), (67 * 8, LANES)]
        + [pltpu.SemaphoreType.DMA((7,))],
        n_in=7,
        where=pl.ANY,
        limit=60,
    )(*arrays)
    v0 = exchange(outgoing, "rx").reshape(8, SENT, 8, LANES)
    message = (4, 2, 10, 8, LANES)
    outer = lax.ppermute(call(functools.partial(message_kernel, True), message)(v0), ("space", "rx"), beside)
    base, inner = call(base_kernel, [(8, 3, 10, 8, LANES), message], n_in=2, flops=10**8)(v0, mass)
    inner = lax.ppermute(inner, "space", chips)
    following = call(outer_kernel, message, n_in=3)(outer, base, inner)
    shapes = [(8, 3, 10, 8, LANES), (8, 3, 9, 8, LANES), message]
    v1, base, inner = call(second_kernel, shapes, n_in=4, flops=10**8)(outer, base, inner, mass)
    outer = lax.ppermute(following, ("space", "rx"), beside)
    inner = lax.ppermute(inner, "space", chips)
    down = call(down_kernel, (4, 2, 8, 8, LANES), n_in=3)(outer, base, inner)
    above = lax.ppermute(down, "space", [((i + 1) % size, i) for i in range(size)])
    moments, curl, v2 = call(
        moments_kernel,
        [(128, LANES), (8, 2, 8, 8, LANES), (8, 3, 9, 8, LANES)],
        [(8, 1, 8, 8, LANES), (8, 3, 8, 8, LANES)],
        n_in=6,
        flops=10**8,
    )(outer, base, inner, v0, v1, mass)
    moments = call(energy_kernel, (128, LANES), n_in=3)(curl, above, moments)
    moments = reduce_bricks(moments)
    mixed = call(finish_kernel, (8, 3, 8, 8, LANES), [(8, LANES)], n_in=4)(moments, v0, v1, v2)
    mixed = exchange(mixed, "rx")
    scratch = [(512, LANES), (LANES, LANES), (3, 8, 2, PLANE, LANES), pltpu.SemaphoreType.DMA((3,))]
    return call(leave_kernel, (8, 3, 2, PLANE, LANES), scratch, far=True)(mixed)


def solution(mesh):
    in_specs = (
        P("rx", None, "space", None, None),
        P("space", None, None),
        P(),
        P("rx"),
        P("rx"),
        P("rx"),
        P("rx"),
    )
    out_specs = P("rx", None, "space", None, None)
    return jax.shard_map(body, mesh=mesh, in_specs=in_specs, out_specs=out_specs, check_vma=False)
```

```python
import functools

import jax
import jax.numpy as jnp
from jax import lax
from jax.experimental import pallas as pl
from jax.experimental.pallas import tpu as pltpu
from jax.sharding import PartitionSpec as P

SHIFT = 6.0
LANES = 128
HALF = 64
PLANE = 32
GHOST = 11
SENT = 31
F32 = jnp.float32
BF16 = jnp.bfloat16
NT = (((1,), (1,)), ((), ()))
NN = (((1,), (0,)), ((), ()))


def lane_ids():
    lane = lax.broadcasted_iota(jnp.int32, (8, LANES), 1)
    return lane & 31, (lane >> 5) & 1, lane >> 6


def turn(a, shift):
    return pltpu.roll(a, shift, axis=a.ndim - 1)


def y_next(a):
    return jnp.where(lane_ids()[0] == 31, 0.0, turn(a, LANES - 1))


def y_prev(a):
    return jnp.where(lane_ids()[0] == 0, 0.0, turn(a, 1))


def z_both(a):
    half = turn(a, HALF)
    mixed = jnp.where(lane_ids()[2] == 0, half[:-1], half[1:])
    return jnp.concatenate([mixed, half[-1:]], axis=0), jnp.concatenate([half[:1], mixed], axis=0)


def x_next(a, beyond):
    return jnp.where(lane_ids()[1] == 0, turn(a, LANES - PLANE), beyond)


def x_prev(a, beyond):
    return jnp.where(lane_ids()[1] == 1, turn(a, PLANE), beyond)


def pack_up(a, b):
    return jnp.where(lane_ids()[1] == 1, a, turn(b, LANES - PLANE))


def pack_down(a, b):
    return jnp.where(lane_ids()[1] == 0, a, turn(b, PLANE))


def unpack(m, second, up):
    if not second:
        m = turn(m, LANES - PLANE) if up else turn(m, PLANE)
    return jnp.where(lane_ids()[1] == (0 if up else 1), m, 0.0)


def slopes(v):
    return v[1] + y_next(v[0]) - v[0], v[2] + z_both(v[0])[0] - v[0]


def apply_tiles(v, shifted):
    g1, g2 = slopes(v)
    e1 = v[1] - x_next(v[1], 0.0)
    e2 = v[2] - x_next(v[2], 0.0)
    q2 = z_both(v[2])[1] - v[2]
    q1 = y_prev(v[1]) - v[1]
    v1_next, v1_prev = z_both(v[1])
    r0 = 2.0 * v[0] + v[1] + v[2] - g1 - g2 + y_prev(e1 - v[0]) + z_both(e2 - v[0])[1] - e1 - e2
    r1 = g1 - x_prev(g1, 0.0) + e1 + 2.0 * v[1] - v1_next - v1_prev - y_next(q2) + q2
    r2 = g2 - x_prev(g2, 0.0) + e2 + 2.0 * v[2] - y_next(v[2]) - y_prev(v[2]) - z_both(q1)[0] + q1
    return [shifted * v[0] + r0, shifted * v[1] + r1, shifted * v[2] + r2]


def halves(a):
    high = a.astype(BF16)
    return high, (a - high.astype(F32)).astype(BF16)


def thirds(a):
    high = a.astype(BF16)
    rest = a - high.astype(F32)
    middle = rest.astype(BF16)
    return high, middle, (rest - middle.astype(F32)).astype(BF16)


def multiply(a, b):
    ah, am, al = thirds(a)
    bh, bm, bl = thirds(b)
    left = jnp.concatenate([ah, ah, am, am, ah, al], axis=1)
    right = jnp.concatenate([bh, bm, bh, bm, bl, bh], axis=0)
    return lax.dot_general(left, right, NN, preferred_element_type=F32)


def enter_kernel(*refs):
    (source, *sources), (out, mass_out), rest = refs[:7], refs[7:9], refs[9:]
    (field, *targets), (flipped, padded, mass_pad, loads) = rest[:7], rest[7:]
    copies = [pltpu.make_async_copy(a, b, loads.at[i]) for i, (a, b) in enumerate(zip(sources, targets, strict=True))]
    copies = [pltpu.make_async_copy(source, field, loads.at[6]), *copies]
    for copy in copies:
        copy.start()
    for copy in copies[1:]:
        copy.wait()
    ids, rate, coil_x, coil_y, coil_z, amp = targets
    lane = lax.broadcasted_iota(jnp.int32, (64, LANES), 1)
    row = lax.broadcasted_iota(jnp.int32, (64, LANES), 0)
    classes = ids[...].reshape(64, LANES)
    mass = jnp.zeros((64, LANES), F32)
    for k in range(rate.shape[0]):
        mass = jnp.where(classes == k, rate[k], mass)
    left = lane < HALF
    flipped[12] = jnp.transpose(jnp.concatenate([mass, mass], axis=0))
    rows = jnp.where(left, flipped[12, pl.ds(0, 64, stride=2), :], flipped[12, pl.ds(1, 64, stride=2), :])
    mass_pad[0:8, :] = jnp.zeros((8, LANES), F32)
    mass_pad[8 * 65 :, :] = jnp.zeros((16, LANES), F32)
    for r in range(8):
        mass_pad[pl.ds(8 + r, 64, stride=8), :] = rows
    first = pl.multiple_of(lax.axis_index("rx") * 64, 64)
    mass_out[...] = mass_pad[pl.ds(first, 8 * GHOST), :].reshape(GHOST, 8, LANES) - SHIFT
    base = lax.axis_index("space") * 2
    copies[0].wait()

    def right(r, c):
        values = mass * field[r, c].reshape(64, LANES)
        if c == 2:
            return values
        near = coil_x[r] - base
        far = near + 1
        spot = jnp.where((near >= 0) & (near < 2), near * 32 + coil_y[r], -100)
        if c == 0:
            plus, minus = spot, spot + 1
        else:
            plus, minus = jnp.where((far >= 0) & (far < 2), far * 32 + coil_y[r], -100), spot
        strength = jnp.where(row == plus, amp[r], jnp.where(row == minus, -amp[r], 0.0))
        return values + jnp.where(lane == coil_z[r], strength, 0.0)

    for c in range(3):
        padded[c, 0:8, :] = jnp.zeros((8, LANES), F32)
        padded[c, 8 * 65 :, :] = jnp.zeros((16, LANES), F32)
        for r in range(4):
            flipped[c * 4 + r] = jnp.transpose(jnp.concatenate([right(r, c), right(r + 4, c)], axis=0))
            even = flipped[c * 4 + r, pl.ds(0, 64, stride=2), :]
            odd = flipped[c * 4 + r, pl.ds(1, 64, stride=2), :]
            padded[c, pl.ds(8 + r, 64, stride=8), :] = jnp.where(left, even, turn(odd, HALF))
            padded[c, pl.ds(12 + r, 64, stride=8), :] = jnp.where(left, turn(even, HALF), odd)
        for d in range(8):
            out[d, 80 * c : 80 * c + 80] = padded[c, 64 * d : 64 * d + 80, :]
    for d in range(8):
        tiles = [padded[k, 64 * d + 80 : 64 * d + 88, :] for k in range(2)]
        out[d, 240:248] = jnp.where(left[:8], tiles[0], turn(tiles[1], HALF))


def first_fields(v0, s):
    last = v0[s, pl.ds(SENT - 1, 1)]
    ends = [last, turn(last, HALF), jnp.zeros((1, 8, LANES), F32)]
    return [jnp.concatenate([v0[s, 10 * c : 10 * c + 10], ends[c]], axis=0) for c in range(3)]


def fields_of(v, s):
    return first_fields(v, s) if v.shape[1] == SENT else [v[s, c] for c in range(3)]


def leave_kernel(tiles, out, gathered, flipped, result, sems):
    left = lax.broadcasted_iota(jnp.int32, (64, LANES), 1) < HALF
    sends = []
    for c in range(3):
        for s in range(8):
            gathered[64 * s : 64 * s + 64, :] = tiles[s, c].reshape(64, LANES)
        for r in range(4):
            one = gathered[pl.ds(r, 64, stride=8), :]
            two = gathered[pl.ds(r + 4, 64, stride=8), :]
            flipped[pl.ds(0, 64, stride=2), :] = jnp.where(left, one, turn(two, HALF))
            flipped[pl.ds(1, 64, stride=2), :] = jnp.where(left, turn(one, HALF), two)
            back = jnp.transpose(flipped[...])
            result[c, r] = back[:64].reshape(2, PLANE, LANES)
            result[c, r + 4] = back[64:].reshape(2, PLANE, LANES)
        sends.append(pltpu.make_async_copy(result.at[c], out.at[:, c], sems.at[c]))
        sends[c].start()
    for copy in sends:
        copy.wait()


def is_even():
    return lax.axis_index("space") % 2 == 0


def send(message, to_above, s, v, w):
    last = GHOST - 1

    @pl.when(to_above)
    def _():
        for c, (a, b) in enumerate(zip(slopes(v), slopes(w), strict=True)):
            message[s, c] = pack_up(a[:last], b[:last])

    @pl.when(jnp.logical_not(to_above))
    def _():
        for c in range(2):
            message[s, c] = pack_down(v[c + 1][:last], w[c + 1][:last])


def message_kernel(outer, v, message):
    def step(s, carry):
        fields = [fields_of(v, s + 4 * k) for k in range(2)]
        send(message, is_even() != outer, s, *fields)
        return carry

    lax.fori_loop(0, 4, step, 0)


def receive(inner, outer, s, c):
    even, index = is_even(), lax.axis_index("space")
    edge = (index == 0) | (index == lax.axis_size("space") - 1)
    near, far = inner[s, c], jnp.where(edge, 0.0, outer[s, c])
    return jnp.where(even, far, near), jnp.where(even, near, far)


def inside(values, first_tile, last_tile):
    index = lax.axis_index("rx")
    rows = values.shape[0]
    low = jnp.where(index == 0, 0.0, 1.0)
    high = jnp.where(index == lax.axis_size("rx") - 1, 0.0, 1.0)
    pieces = [values]
    if first_tile:
        pieces = [values[:1] * low, values[1:]]
    if last_tile:
        pieces = [*pieces[:-1], pieces[-1][:-1], pieces[-1][-1:] * high]
    return jnp.concatenate(pieces, axis=0) if rows else values


def base_kernel(v, mass, base, inner):
    def step(s, carry):
        fields = [fields_of(v, s + 4 * k) for k in range(2)]
        for k in range(2):
            result = apply_tiles(fields[k], mass[...])
            for c in range(3):
                base[s + 4 * k, c] = result[c][: base.shape[2]]
        send(inner, is_even(), s, *fields)
        return carry

    lax.fori_loop(0, 4, step, 0)


def completed(base, inner, outer, s, k, first):
    below, above = zip(*(receive(inner, outer, s, c) for c in range(2)), strict=True)
    beyond = [unpack(a, k, False) for a in above]
    before = [unpack(a, k, True) for a in below]
    changes = [
        beyond[0] + beyond[1] - y_prev(beyond[0]) - z_both(beyond[1])[1],
        -beyond[0] - before[0],
        -beyond[1] - before[1],
    ]
    return [inside(base[s + 4 * k, c] + changes[c][first:], first == 0, True) for c in range(3)]


def at_first(base, inner, outer, s, c, k):
    return base[s + 4 * k, c + 1] - unpack(receive(inner, outer, s, c)[0], k, True)[10 - base.shape[2] :]


def outer_kernel(outer, base, inner, message):
    def step(s, carry):
        @pl.when(is_even())
        def _():
            for c in range(2):
                parts = [inside(at_first(base, inner, outer, s, c, k), True, True) for k in range(2)]
                message[s, c] = pack_down(*parts)

        @pl.when(jnp.logical_not(is_even()))
        def _():
            send(message, True, s, *[completed(base, inner, outer, s, k, 0) for k in range(2)])

        return carry

    lax.fori_loop(0, 4, step, 0)


def second_kernel(outer, base, inner, mass, v1, next_base, next_inner):
    def step(s, carry):
        fields = [completed(base, inner, outer, s, k, 0) for k in range(2)]
        for k in range(2):
            result = apply_tiles(fields[k], mass[:10])
            for c in range(3):
                v1[s + 4 * k, c] = fields[k][c]
                next_base[s + 4 * k, c] = result[c][1:]
        send(next_inner, is_even(), s, *fields)
        return carry

    lax.fori_loop(0, 4, step, 0)


def down_kernel(outer, base, inner, down):
    def step(s, carry):
        for c in range(2):
            down[s, c] = pack_down(*[at_first(base, inner, outer, s, c, k)[:8] for k in range(2)])
        return carry

    lax.fori_loop(0, 4, step, 0)


def columns(ref, c, first):
    at = lambda k: ref[:, 10 * c + k] if ref.shape[1] == SENT else ref[:, c, k]
    return jnp.concatenate([at(first + k).reshape(64, LANES) for k in range(2)], axis=1)


SIX = ((0, 0), (0, 1), (1, 0), (1, 1), (0, 2), (2, 0))


def six(products):
    return sum(products[64 * i : 64 * i + 64, 64 * j : 64 * j + 64] for i, j in SIX)


def squares(tiles):
    parts = jnp.concatenate(thirds(tiles), axis=0)
    return lax.dot_general(parts, parts, NT, preferred_element_type=F32)


def square_ids():
    shape = (64, 64)
    return lax.broadcasted_iota(jnp.int32, shape, 0), lax.broadcasted_iota(jnp.int32, shape, 1)


def diagonal(a):
    row, column = square_ids()
    return jnp.sum(jnp.where(row == column, a, 0.0), axis=0, keepdims=True)


def moments_kernel(outer, base, inner, v0, v1, mass, out, curl, v2, curl0, scaled):
    y, x, parity = lane_ids()
    first_x = jnp.where((x == 0) & (lax.axis_index("space") == 0), 1.0, 0.0)
    first_y = jnp.where(y == 0, 1.0, 0.0)
    tile = lax.broadcasted_iota(jnp.int32, (8, 8, LANES), 0)
    first_z = jnp.where((tile == 0) & (parity == 0) & (lax.axis_index("rx") == 0), 1.0, 0.0)
    own = mass[1:9]
    faces = [first_y + first_z, first_x + first_z, first_x + first_y]

    def step(s, carry):
        for k in range(2):
            v, at = completed(base, inner, outer, s, k, 1), s + 4 * k
            for c in range(3):
                v2[at, c] = v[c]
            z1 = z_both(v[1])[0][:8]
            z0 = z_both(v[0])[0][:8]
            v = [a[:8] for a in v]
            curl0[at, 0] = y_next(v[2]) - v[2] - z1 + v[1]
            curl[at, 0] = z0 - v[0] - x_next(v[2], 0.0) + v[2]
            curl[at, 1] = x_next(v[1], 0.0) - v[1] - y_next(v[0]) + v[0]
            for c in range(3):
                scaled[at, c] = v[c] * (own + faces[c])
        return carry

    lax.fori_loop(0, 4, step, 0)
    bends = jnp.zeros((192, 192), F32)
    mixed = jnp.zeros((192, 192), F32)
    total = jnp.zeros((192, 576), F32)
    middles = jnp.zeros((192, 192), F32)
    for c in range(3):
        for k in range(0, 8, 2):
            stack = jnp.concatenate([columns(v0, c, k + 1), columns(v1, c, k + 1), columns(v2, c, k)], axis=0)
            parts = thirds(stack)
            total = total + lax.dot_general(
                parts[0], jnp.concatenate(parts, axis=0), NT, preferred_element_type=F32
            )
            middles = middles + lax.dot_general(parts[1], parts[1], NT, preferred_element_type=F32)
            wide = jnp.concatenate(thirds(columns(scaled, c, k)), axis=0)
            field = jnp.concatenate([a[128:] for a in parts], axis=0)
            mixed = mixed + lax.dot_general(wide, field, NT, preferred_element_type=F32)
            if c == 0:
                bends = bends + squares(columns(curl0, c, k))
    main, cross = total[:, :192] + middles, total[:, 192:384] + total[:, 384:]
    cross = cross + jnp.transpose(jnp.concatenate([cross, jnp.zeros((192, 64), F32)], axis=1))[:192, :]
    total = main + cross

    def block(i, j):
        return total[64 * i : 64 * i + 64, 64 * j : 64 * j + 64]

    n = [block(0, 0), block(0, 1), block(1, 1), block(1, 2), block(2, 2), six(bends) + six(mixed)]
    row, column = square_ids()
    packed = [jnp.where(row <= column, n[2 * i], n[2 * i + 1]) for i in range(3)]
    diagonals = jnp.concatenate([diagonal(n[1]), diagonal(n[3]), diagonal(n[5]), jnp.zeros((61, 64), F32)], axis=0)
    out[0:64, :] = jnp.concatenate(packed[:2], axis=1)
    out[64:128, :] = jnp.concatenate([packed[2], diagonals], axis=1)


def energy_kernel(curl, above, moments, out):
    bends = jnp.zeros((192, 192), F32)
    edge = lax.axis_index("space") == lax.axis_size("space") - 1
    for c in range(2):
        for k in range(0, 8, 2):
            rows = []
            for j in range(2):
                message = jnp.where(edge, 0.0, above[:, 1 - c, k + j])
                beyond = jnp.concatenate([unpack(message, half, False) for half in range(2)], axis=0)
                bent = curl[:, c, k + j] - beyond if c == 0 else curl[:, c, k + j] + beyond
                rows.append(bent.reshape(64, LANES))
            bends = bends + squares(jnp.concatenate(rows, axis=1))
    last = six(bends)
    row, column = square_ids()
    lower = jnp.where(row > column, last, 0.0)
    third = jnp.where(row == 2, diagonal(last), 0.0)
    out[0:64, :] = moments[0:64, :]
    out[64:128, :] = moments[64:128, :] + jnp.concatenate([lower, third], axis=1)


def spread(a, lane):
    return jnp.broadcast_to(a[:, lane : lane + 1], (8, LANES))


def line(a, k):
    return jnp.broadcast_to(a[k : k + 1], (8, LANES))


def tall_multiply(a, b):
    ah, am, al = thirds(a)
    bh, bm, bl = thirds(b)
    dot = lambda x, y: lax.dot_general(x, y, NN, preferred_element_type=F32)
    rows = a.shape[0]
    one = dot(jnp.concatenate([ah, am, al], axis=0), bh)
    two = dot(jnp.concatenate([ah, am], axis=0), bm)
    corner = dot(ah, bl)
    return ((one[:rows] + one[rows : 2 * rows]) + (one[2 * rows :] + two[:rows])) + (two[rows:] + corner)


def total(f):
    return ((f[0] + f[1]) + (f[2] + f[3])) + ((f[4] + f[5]) + (f[6] + f[7]))


def invert(matrix):
    unit = lax.broadcasted_iota(jnp.int32, (64, 64), 0) == lax.broadcasted_iota(jnp.int32, (64, 64), 1)
    both = jnp.concatenate([matrix, jnp.where(unit, 1.0, 0.0)], axis=1)
    tiles = [both[8 * i : 8 * i + 8] for i in range(8)]
    sub = lax.broadcasted_iota(jnp.int32, (8, LANES), 0)
    lane = lax.broadcasted_iota(jnp.int32, (8, LANES), 1)
    zero = jnp.zeros((8, LANES), F32)
    own = [jnp.sum(jnp.where(lane == sub + 8 * p, tiles[p], 0.0), axis=1, keepdims=True) for p in range(8)]
    floors = [jnp.broadcast_to(a * 2e-7, (8, LANES)) for a in own]
    cols = [spread(tiles[0], k) for k in range(8)]
    raw, scaled = [], []
    for p in range(8):
        rows, first, after = tiles[p], 8 * p, p + 1
        raw.append(rows)
        aside, near, far = [], list(range(after, min(after + 2, 8))), list(range(after + 2, 8))
        if near:
            factors = {i: [spread(tiles[i], first + k) for k in range(8)] for i in near}
            aside = [spread(rows, first + 8 + k) for k in range(8)]
            ahead = [spread(tiles[after], first + 8 + k) for k in range(8)]
        for k in range(8):
            pivot = line(cols[k], k)
            inverse = jnp.where(pivot > line(floors[p], k), 1.0 / pivot, 0.0)
            column, hit = cols[k], sub == k

            def eliminate(x):
                top = line(x, k) * inverse
                return jnp.where(hit, top, x - column * top)

            for j in range(k + 1, 8):
                cols[j] = eliminate(cols[j])
            rows = eliminate(rows)
            aside = [eliminate(x) for x in aside]
        scaled.append(rows)
        if not near:
            break
        lines = [line(rows, k) for k in range(8)]
        cols = [ahead[j] - total([factors[after][k] * line(aside[j], k) for k in range(8)]) for j in range(8)]
        tiles = list(tiles)
        if far:
            panel = (lane >= first) & (lane < first + 8)
            apart = jnp.concatenate([jnp.where(panel, tiles[i], 0.0) for i in far], axis=0)[:, :64]
            change = tall_multiply(apart, jnp.concatenate([rows if i == p else zero for i in range(8)], axis=0))
            for n, i in enumerate(far):
                tiles[i] = tiles[i] - change[8 * n : 8 * n + 8]
        for i in near:
            tiles[i] = tiles[i] - total([factors[i][k] * lines[k] for k in range(8)])
    left = jnp.concatenate(raw, axis=0)
    left = jnp.transpose(jnp.concatenate([left, left], axis=0))[64:, :64]
    return multiply(left, jnp.concatenate(scaled, axis=0)[:, 64:])


def solve_blocks(n, h):
    first = multiply(invert(h[0]), jnp.concatenate([h[1], h[2], n[0]], axis=1))
    change = multiply(jnp.concatenate([h[1], h[2]], axis=0), first)
    second = jnp.concatenate([h[2], h[3], n[1]], axis=1) - change[:64]
    third = jnp.concatenate([h[3], h[4], n[2]], axis=1) - change[64:]
    below = third[:, :64]
    second = multiply(invert(second[:, :64]), second[:, 64:])
    third = third[:, 64:] - multiply(below, second)
    y2 = multiply(invert(third[:, :64]), third[:, 64:])
    y1 = second[:, 64:] - multiply(second[:, :64], y2)
    y0 = first[:, 128:] - multiply(first[:, :64], y1) - multiply(first[:, 64:128], y2)
    return jnp.concatenate([y0, y1, y2], axis=0)


def finish_kernel(moments, v0, v1, v2, out):
    row, column = square_ids()
    one, two = moments[0:64, :], moments[64:128, :]
    turned = [jnp.transpose(jnp.concatenate([a, a], axis=0))[:, :64] for a in (one, two)]
    pairs = [(one[:, :64], turned[0][:64]), (one[:, 64:], turned[0][64:]), (two[:, :64], turned[1][:64])]
    n = []
    for i, (block, other) in enumerate(pairs):
        n.append(jnp.where(row <= column, block, other))
        n.append(jnp.where(row > column, block, jnp.where(row < column, other, two[i : i + 1, 64:])))
    h = [n[m + 1] + SHIFT * n[m] for m in range(5)]
    solved = solve_blocks(n, h)
    weights = jnp.transpose(jnp.concatenate([solved, solved], axis=1))[64:]
    high, low = halves(weights)
    both = jnp.concatenate([high, low], axis=0)
    for c in range(3):
        for k in range(0, 8, 2):
            stack = jnp.concatenate([columns(v0, c, k + 1), columns(v1, c, k + 1), columns(v2, c, k)], axis=0)
            fine, rest = halves(stack)
            one = lax.dot_general(both, fine, NN, preferred_element_type=F32)
            two = lax.dot_general(high, rest, NN, preferred_element_type=F32)
            mixed = one[:64] + one[64:] + two
            for j in range(2):
                out[:, c, k + j] = mixed[:, LANES * j : LANES * j + LANES].reshape(8, 8, LANES)


def call(kernel, outs, scratch=(), n_in=1, flops=0, where=pltpu.VMEM, limit=48, far=False):
    single = not isinstance(outs, list)
    shapes = [outs] if single else outs
    vmem = pl.BlockSpec(memory_space=pltpu.VMEM)
    scratch = [pltpu.VMEM(a, F32) if isinstance(a, tuple) else a for a in scratch]
    done = pl.pallas_call(
        kernel,
        out_shape=[jax.ShapeDtypeStruct(s, F32) for s in shapes],
        in_specs=[pl.BlockSpec(memory_space=where)] * n_in,
        out_specs=[pl.BlockSpec(memory_space=pl.ANY) if far else vmem, *[vmem] * (len(shapes) - 1)],
        scratch_shapes=scratch,
        compiler_params=pltpu.CompilerParams(vmem_limit_bytes=limit * 1024 * 1024),
        cost_estimate=pl.CostEstimate(flops=flops, bytes_accessed=4 * 1024 * 1024, transcendentals=0),
    )
    return (lambda *a: done(*a)[0]) if single else done


def exchange(x, axis):
    return lax.all_to_all(x, axis, split_axis=0, concat_axis=0, tiled=True)


def reduce_bricks(parts):
    space, rx = (lax.axis_size("space"), lax.axis_size("rx"))
    rows = parts.shape[0]
    pieces = exchange(parts.reshape(space, rows // space, LANES), "space")
    own = jnp.sum(pieces, axis=0)
    pieces = exchange(jnp.broadcast_to(own[None], (rx, *own.shape)), "rx")
    own = jnp.sum(pieces, axis=0)
    pieces = exchange(jnp.broadcast_to(own[None], (space, *own.shape)), "space")
    return pieces.reshape(rows, LANES)


def body(lambda_next, class_ids, class_rate, coil_x, coil_y, coil_z, coil_amp):
    size = lax.axis_size("space")
    chips = [(i, i ^ 1) for i in range(size)]
    depth = lax.axis_size("rx")
    beside = []
    for i in range(size):
        for z in range(depth):
            end = i in (0, size - 1)
            other = (i, z ^ 1) if end else (i + 1 if i % 2 else i - 1, z)
            beside.append((i * depth + z, other[0] * depth + other[1]))
    arrays = (lambda_next, class_ids, class_rate, coil_x, coil_y, coil_z, coil_amp)
    spaces = [pltpu.VMEM] + [pltpu.SMEM] * 5
    outgoing, mass = call(
        enter_kernel,
        [(8, 8 * SENT, LANES), (GHOST, 8, LANES)],
        [(8, 3, 2, PLANE, LANES)]
        + [space(a.shape, a.dtype) for space, a in zip(spaces, arrays[1:], strict=True)]
        + [(13, LANES, LANES), (3, 67 * 8, LANES), (67 * 8, LANES)]
        + [pltpu.SemaphoreType.DMA((7,))],
        n_in=7,
        where=pl.ANY,
        limit=60,
    )(*arrays)
    v0 = exchange(outgoing, "rx").reshape(8, SENT, 8, LANES)
    message = (4, 2, 10, 8, LANES)
    outer = lax.ppermute(call(functools.partial(message_kernel, True), message)(v0), ("space", "rx"), beside)
    base, inner = call(base_kernel, [(8, 3, 10, 8, LANES), message], n_in=2, flops=10**8)(v0, mass)
    inner = lax.ppermute(inner, "space", chips)
    following = call(outer_kernel, message, n_in=3)(outer, base, inner)
    shapes = [(8, 3, 10, 8, LANES), (8, 3, 9, 8, LANES), message]
    v1, base, inner = call(second_kernel, shapes, n_in=4, flops=10**8)(outer, base, inner, mass)
    outer = lax.ppermute(following, ("space", "rx"), beside)
    inner = lax.ppermute(inner, "space", chips)
    down = call(down_kernel, (4, 2, 8, 8, LANES), n_in=3)(outer, base, inner)
    above = lax.ppermute(down, "space", [((i + 1) % size, i) for i in range(size)])
    moments, curl, v2 = call(
        moments_kernel,
        [(128, LANES), (8, 2, 8, 8, LANES), (8, 3, 9, 8, LANES)],
        [(8, 1, 8, 8, LANES), (8, 3, 8, 8, LANES)],
        n_in=6,
        flops=10**8,
    )(outer, base, inner, v0, v1, mass)
    moments = call(energy_kernel, (128, LANES), n_in=3)(curl, above, moments)
    moments = reduce_bricks(moments)
    mixed = call(finish_kernel, (8, 3, 8, 8, LANES), n_in=4)(moments, v0, v1, v2)
    mixed = exchange(mixed, "rx")
    scratch = [(512, LANES), (LANES, LANES), (3, 8, 2, PLANE, LANES), pltpu.SemaphoreType.DMA((3,))]
    return call(leave_kernel, (8, 3, 2, PLANE, LANES), scratch, far=True)(mixed)


def solution(mesh):
    in_specs = (
        P("rx", None, "space", None, None),
        P("space", None, None),
        P(),
        P("rx"),
        P("rx"),
        P("rx"),
        P("rx"),
    )
    out_specs = P("rx", None, "space", None, None)
    return jax.shard_map(body, mesh=mesh, in_specs=in_specs, out_specs=out_specs, check_vma=False)
```
